32 devices in a mesh: blk: 8 (over z, y), dp: 4 (over x, core).
Axes of the slice: x: 2, y: 2, z: 4, core: 2. Of those that a mesh axis runs over, the one named last changes fastest.
Arguments:
- dec_input: bfloat16 [1024, 8, 768], P('blk', 'dp'), may hold values from -6 to 6
- enc_output: bfloat16 [8, 7168, 768], P('dp', 'blk'), may hold values from -6 to 6
- lengths: int32 [8, 16], P('dp'), may hold values from 56 to 448, as said below
- gains: bfloat16 [3, 768], replicated, may hold values from 0.25 to 1.75
- self_qkv: bfloat16 [3, 768, 768], replicated, may hold values from -0.21875 to 0.21875
- self_out: bfloat16 [768, 768], replicated, may hold values from -0.875 to 0.875
- cross_q: bfloat16 [768, 768], replicated, may hold values from -0.21875 to 0.21875
- cross_kv: bfloat16 [2, 768, 768], replicated, may hold values from -0.21875 to 0.21875
- cross_out: bfloat16 [768, 768], replicated, may hold values from -8 to 8
- ffn_in: bfloat16 [768, 3072], replicated, may hold values from -0.21875 to 0.21875
- ffn_out: bfloat16 [3072, 768], replicated, may hold values from -0.109375 to 0.109375
- cotangent: bfloat16 [1024, 8, 768], P('blk', 'dp'), may hold values from -6 to 6
Outputs:
- output: bfloat16 [1024, 8, 768], P('blk', 'dp')
- dec_grad: bfloat16 [1024, 8, 768], P('blk', 'dp')
- enc_grad: bfloat16 [8, 7168, 768], P('dp', 'blk')
- gains_grad: float32 [3, 768], replicated
- self_qkv_grad: float32 [3, 768, 768], P(None, 'blk', 'dp')
- self_out_grad: float32 [768, 768], P('blk', 'dp')
- cross_q_grad: float32 [768, 768], P('blk', 'dp')
- cross_kv_grad: float32 [2, 768, 768], P(None, 'blk', 'dp')
- cross_out_grad: float32 [768, 768], P('blk', 'dp')
- ffn_in_grad: float32 [768, 3072], P('blk', 'dp')
- ffn_out_grad: float32 [3072, 768], P('blk', 'dp')
The draws below stay inside these ranges and needn't reach their ends.
Inputs may be any that keep to these rules, and one draw needn't show every extreme that they name: `lengths`: in every aligned group of 2 queries (those of one dp index) the query at one seed-drawn place has all 16 passages full, and the first passage of the other query holds 56 tokens.
All inputs are finite; a program needn't handle non-finite values.
Results may differ from the reference program's by a relative error of at most 0.04.
Values may be sent and summed in bfloat16 or wider, within the bound.
No kernel may reach another device: no remote copies, remote signals or barrier semaphores. Data moves between devices by JAX's collectives and lax.ppermute only.
A program may use at most 256 MiB of HBM per device.

```python
import jax
import jax.numpy as jnp
from jax import lax

D = 768
FF = 3072
HEADS = 12
HEAD_DIM = 64
SEQS = 2
PASS = 16
SLOTS = 448
DLEN = 1024
QUERIES = 8
ENC = 7168


def draw_lengths(key, part):
    key = jax.random.fold_in(key, 7)
    fill_key, row_key = jax.random.split(key)
    values = jax.random.randint(fill_key, (QUERIES, PASS), SLOTS // 8, SLOTS + 1)
    chosen = jax.random.randint(row_key, (), 0, SEQS)
    rows = jnp.arange(QUERIES)[:, None] % SEQS
    columns = jnp.arange(PASS)[None, :]
    values = jnp.where(rows == chosen, SLOTS, values)
    values = jnp.where((rows == (chosen + 1) % SEQS) & (columns == 0), SLOTS // 8, values)
    return values.astype(jnp.int32)


def level_of(own_key, dims, cuts, smallest, largest):
    loudness, own = 1.0, jax.random.fold_in(own_key, 6)
    for position, shards_of in cuts:
        steps = jnp.exp(jax.random.uniform(jax.random.fold_in(own, position), (shards_of,), jnp.float32, smallest / len(cuts), largest / len(cuts)))
        loudness = loudness * jnp.repeat(steps, dims[position] // shards_of).reshape([-1 if axis == position else 1 for axis in range(len(dims))])
    return loudness


def centred(rng, shape, deviation, most, pieces=(), dtype=jnp.bfloat16):
    entries = deviation * jax.random.normal(rng, shape, jnp.float32)
    if pieces:
        entries = entries * level_of(rng, shape, pieces, -0.22, 0.18)
    return jnp.clip(entries, -most, most).astype(dtype)


def setup_inputs(seed: int = 0) -> dict:
    streams_of = jax.random.split(jax.random.key(seed), 13)
    dec_input = centred(streams_of[0], (DLEN, QUERIES, D), 1.0, 6.0, ((0, 8), (1, 4)))
    enc_output = centred(streams_of[1], (QUERIES, ENC, D), 1.0, 6.0, ((0, 4), (1, 8)))
    lengths = draw_lengths(jax.random.fold_in(streams_of[12], 71), 0)
    gains = jnp.clip(1.0 + 0.15 * jax.random.normal(streams_of[3], (3, D), jnp.float32), 0.25, 1.75).astype(jnp.bfloat16)
    self_qkv = centred(streams_of[4], (3, D, D), D ** -0.5, 0.21875)
    self_out = centred(streams_of[5], (D, D), (D // 16) ** -0.5, 0.875)
    cross_q = centred(streams_of[6], (D, D), D ** -0.5, 0.21875)
    cross_kv = centred(streams_of[7], (2, D, D), D ** -0.5, 0.21875)
    cross_out = centred(streams_of[8], (D, D), ((ENC * 100 // (3 * D)) ** 0.5 * 10 ** -1), 8.0)
    ffn_in = centred(streams_of[9], (D, FF), D ** -0.5, 0.21875)
    ffn_out = centred(streams_of[10], (FF, D), FF ** -0.5, 0.109375)
    cotangent = centred(streams_of[11], (DLEN, QUERIES, D), 1.0, 6.0, ((0, 8), (1, 4)))
    return {"dec_input": dec_input, "enc_output": enc_output, "lengths": lengths, "gains": gains, "self_qkv": self_qkv, "self_out": self_out, "cross_q": cross_q, "cross_kv": cross_kv, "cross_out": cross_out, "ffn_in": ffn_in, "ffn_out": ffn_out, "cotangent": cotangent}


@jax.custom_vjp
def low(v):
    return lax.optimization_barrier(v.astype(jnp.bfloat16)).astype(jnp.float32)

@jax.custom_vjp
def low_back(v):
    return v

def low_keep(v):
    return (low(v), None)

def low_pass(kept, grad):
    return (grad,)

def back_keep(v):
    return (v, None)

def back_low(kept, grad):
    return (low(grad),)
low.defvjp(low_keep, low_pass)
low_back.defvjp(back_keep, back_low)
epsilon = 1e-06
negative_fill = -1e+30
highest = lax.Precision.HIGHEST

def normed(values, gain):
    return values * lax.rsqrt(lax.optimization_barrier(jnp.mean(values * values, axis=-1, keepdims=True)) + epsilon) * gain

def product(left, right):
    return jnp.einsum('...k,kn->...n', left, right, precision=highest)

def attend(query, keys, values, allowed):
    raw = low_back(jnp.einsum('qhe,khe->hqk', query, keys, precision=highest) * 0.125)
    raw = jnp.where(allowed[None], raw, negative_fill)
    top = lax.optimization_barrier(jnp.max(raw, axis=-1, keepdims=True))
    weight = jnp.exp(raw - top)
    prob = low(weight / lax.optimization_barrier(jnp.sum(weight, axis=-1, keepdims=True)))
    return jnp.einsum('hqk,khe->qhe', prob, values, precision=highest)

def layer(inputs, encoded, valid, gains, self_qkv, self_out, cross_q, cross_kv, cross_out, ffn_in, ffn_out):
    length = inputs.shape[0]
    span = min(512, length)
    count = length // span
    first_low = low(normed(inputs, gains[0]))
    query = low(low_back(product(first_low, self_qkv[0]))).reshape(length, HEADS, HEAD_DIM)
    keys = low(low_back(product(first_low, self_qkv[1]))).reshape(length, HEADS, HEAD_DIM)
    values = low(low_back(product(first_low, self_qkv[2]))).reshape(length, HEADS, HEAD_DIM)
    positions = jnp.arange(length).astype(jnp.int32)
    starts = (jnp.arange(count) * span).astype(jnp.int32)

    def self_block(pack):
        block_query, start = pack
        rows = start + jnp.arange(span).astype(jnp.int32)
        return attend(block_query, keys, values, positions[None, :] <= rows[:, None])
    mixed = lax.map(jax.checkpoint(self_block), (query.reshape(count, span, HEADS, HEAD_DIM), starts))
    mixed = low(low_back(mixed.reshape(length, D)))
    after_self = inputs + low_back(product(mixed, self_out))
    second_low = low(normed(after_self, gains[1]))
    cross_query = low(low_back(product(second_low, cross_q))).reshape(count, span, HEADS, HEAD_DIM)
    cross_keys = low(low_back(product(encoded, cross_kv[0]))).reshape(ENC, HEADS, HEAD_DIM)
    cross_values = low(low_back(product(encoded, cross_kv[1]))).reshape(ENC, HEADS, HEAD_DIM)
    allowed = jnp.broadcast_to(valid[None, :], (span, ENC))

    def cross_block(block_query):
        return attend(block_query, cross_keys, cross_values, allowed)
    cross_mix = lax.map(jax.checkpoint(cross_block), cross_query)
    cross_mix = low(low_back(cross_mix.reshape(length, D)))
    after_cross = after_self + low_back(product(cross_mix, cross_out))
    third_low = low(normed(after_cross, gains[2]))
    hidden = low_back(product(third_low, ffn_in))
    activated = low(jax.nn.gelu(hidden))
    return after_cross + low_back(product(activated, ffn_out))

def reference(dec_input, enc_output, lengths, gains, self_qkv, self_out, cross_q, cross_kv, cross_out, ffn_in, ffn_out, cotangent):
    inputs = jnp.transpose(dec_input.astype(jnp.float32), (1, 0, 2))
    encoded = enc_output.astype(jnp.float32)
    slot = jnp.arange(ENC).astype(jnp.int32)
    valid = (slot % SLOTS)[None, :] < jnp.take(lengths, slot // SLOTS, axis=1)
    weights = tuple((item.astype(jnp.float32) for item in (gains, self_qkv, self_out, cross_q, cross_kv, cross_out, ffn_in, ffn_out)))

    def total(inputs, encoded, weights):

        def one(pack):
            seq_in, seq_enc, seq_valid = pack
            return layer(seq_in, seq_enc, seq_valid, *weights)
        return lax.map(one, (inputs, encoded, valid))
    result, pull = jax.vjp(total, inputs, encoded, weights)
    grad_in, grad_enc, grad_weights = pull(jnp.transpose(cotangent.astype(jnp.float32), (1, 0, 2)))
    output = jnp.transpose(result, (1, 0, 2)).astype(jnp.bfloat16)
    dec_grad = jnp.transpose(grad_in, (1, 0, 2)).astype(jnp.bfloat16)
    enc_grad = grad_enc.astype(jnp.bfloat16)
    return (output, dec_grad, enc_grad, grad_weights[0], grad_weights[1], grad_weights[2], grad_weights[3], grad_weights[4], grad_weights[5], grad_weights[6], grad_weights[7])
```

```python
import functools

import jax
import jax.numpy as jnp
from jax import lax
from jax.experimental import pallas as pl
from jax.experimental.pallas import tpu as pltpu
from jax.sharding import PartitionSpec as P

HEAD_DIM = 64
SLOTS = 448
F32 = jnp.float32
BF16 = jnp.bfloat16
epsilon = 1e-06
negative_fill = -1e30
safe_score = 60.0
VMEM_LIMIT = 60 * 1024 * 1024


def dot(left, right, left_dim, right_dim):
    return lax.dot_general(
        left, right, (((left_dim,), (right_dim,)), ((), ())), preferred_element_type=F32
    )


def split_low(value):
    high = value.astype(BF16)
    return high, (value - high.astype(F32)).astype(BF16)


def split_sent(value):
    high = lax.reduce_precision(value, 8, 7)
    return high.astype(BF16), (value - high).astype(BF16)


def normed(values, gain):
    return values * lax.rsqrt(jnp.mean(values * values, axis=-1, keepdims=True) + epsilon) * gain


def norm_pull(values, gain, grad):
    unused, pull = jax.vjp(normed, values, gain)
    return pull(grad)


def params():
    return pltpu.CompilerParams(vmem_limit_bytes=VMEM_LIMIT)


def cross_forward(query, keys, values, bias, width, groups):
    heads = width // HEAD_DIM
    length = query.shape[1]
    tokens = length // groups
    parts = len(keys)
    rows = [k.shape[1] for k in keys]
    starts = [sum(rows[:i]) for i in range(parts)]
    total = sum(rows)
    stat_rows = 16 * ((heads + 15) // 16)

    def kernel(*refs):
        q_ref = refs[0]
        k_refs = refs[1 : 1 + parts]
        v_refs = refs[1 + parts : 1 + 2 * parts]
        b_refs = refs[1 + 2 * parts : 1 + 3 * parts]
        o_ref, p_ref, m_ref, lse_ref = refs[1 + 3 * parts :]
        head = pl.program_id(0)
        query = q_ref[...]
        aug_query = jnp.concatenate([query, jnp.ones((16, length), BF16)], axis=0)
        q_norm = jnp.max(jnp.sum(jnp.square(query.astype(F32)), axis=0, keepdims=True))
        k_norm = jnp.float32(0)
        for k_ref in k_refs:
            k_norm = jnp.maximum(
                k_norm, jnp.max(jnp.sum(jnp.square(k_ref[...].astype(F32)), axis=0, keepdims=True))
            )
        small = q_norm * k_norm < safe_score * safe_score

        def score(i):
            return dot(jnp.concatenate([k_refs[i][...], b_refs[i][...]], axis=0), aug_query, 0, 0)

        def finish(probs, top):
            mixed = None
            for i in range(parts):
                aug_value = jnp.concatenate([v_refs[i][...], jnp.ones((16, rows[i]), BF16)], axis=0)
                term = dot(aug_value, probs[i], 1, 0)
                mixed = term if mixed is None else mixed + term
            norm = mixed[HEAD_DIM : HEAD_DIM + 1]
            out = (mixed[:HEAD_DIM] / norm).astype(BF16)
            where = pl.ds(pl.multiple_of(head * HEAD_DIM, HEAD_DIM), HEAD_DIM)
            for g in range(groups):
                o_ref[g, where, :] = out[:, g * tokens : (g + 1) * tokens]
            lse_ref[pl.ds(head, 1), :] = top + jnp.log(norm)
            m_ref[0] = top

        @pl.when(small)
        def plain():
            probs = []
            for i in range(parts):
                prob = jnp.exp(score(i)).astype(BF16)
                p_ref[0, starts[i] : starts[i] + rows[i], :] = prob
                probs.append(prob)
            finish(probs, jnp.zeros((1, length), F32))

        @pl.when(jnp.logical_not(small))
        def shifted():
            raw = [score(i) for i in range(parts)]
            top = jnp.max(raw[0], axis=0, keepdims=True)
            for i in range(1, parts):
                top = jnp.maximum(top, jnp.max(raw[i], axis=0, keepdims=True))
            probs = []
            for i in range(parts):
                prob = jnp.exp(raw[i] - top).astype(BF16)
                p_ref[0, starts[i] : starts[i] + rows[i], :] = prob
                probs.append(prob)
            finish(probs, top)

        @pl.when(head == heads - 1)
        def stats():
            high, low = split_low(lse_ref[...])
            for g in range(groups):
                o_ref[g, width : width + stat_rows, :] = high[:, g * tokens : (g + 1) * tokens]
                o_ref[g, width + stat_rows :, :] = low[:, g * tokens : (g + 1) * tokens]

    payload = width + 2 * stat_rows
    kv_specs = [pl.BlockSpec((HEAD_DIM, r), lambda h: (h, 0)) for r in rows]
    return pl.pallas_call(
        kernel,
        grid=(heads,),
        in_specs=[pl.BlockSpec((HEAD_DIM, length), lambda h: (h, 0))]
        + kv_specs
        + kv_specs
        + [pl.BlockSpec((16, r), lambda h: (0, 0)) for r in rows],
        out_specs=[
            pl.BlockSpec((groups, payload, tokens), lambda h: (0, 0, 0)),
            pl.BlockSpec((1, total, length), lambda h: (h, 0, 0)),
            pl.BlockSpec((1, 1, length), lambda h: (h, 0, 0)),
        ],
        out_shape=[
            jax.ShapeDtypeStruct((groups, payload, tokens), BF16),
            jax.ShapeDtypeStruct((heads, total, length), BF16),
            jax.ShapeDtypeStruct((heads, 1, length), F32),
        ],
        scratch_shapes=[pltpu.VMEM((stat_rows, length), F32)],
        compiler_params=params(),
        cost_estimate=pl.CostEstimate(
            flops=16 * heads * total * length * HEAD_DIM,
            bytes_accessed=2 * heads * total * length,
            transcendentals=heads * total * length,
        ),
        name="cross_forward",
    )(query, *keys, *values, *bias)


def cross_backward(query, keys, values, prob, grads, weight, delta, width, groups):
    heads = width // HEAD_DIM
    length = query.shape[1]
    tokens = length // groups
    parts = len(keys)
    rows = [k.shape[1] for k in keys]
    starts = [sum(rows[:i]) for i in range(parts)]
    total = sum(rows)
    pair = 2

    def kernel(*refs):
        q_ref = refs[0]
        k_refs = refs[1 : 1 + parts]
        v_refs = refs[1 + parts : 1 + 2 * parts]
        p_ref, g_ref, w_ref, d_ref = refs[1 + 2 * parts : 5 + 2 * parts]
        dq_ref = refs[5 + 2 * parts]
        dk_refs = refs[6 + 2 * parts : 6 + 3 * parts]
        dv_refs = refs[6 + 3 * parts :]
        key_out = [[] for _ in range(parts)]
        value_out = [[] for _ in range(parts)]
        for j in range(pair):
            at = slice(j * HEAD_DIM, (j + 1) * HEAD_DIM)
            grad = jnp.concatenate([g_ref[g, at, :] for g in range(groups)], axis=1).astype(F32)
            scaled = grad * w_ref[j]
            high, low = split_low(-d_ref[j])
            scaled_low = scaled.astype(BF16)
            pad = jnp.zeros((14, length), BF16)
            aug = jnp.concatenate([scaled_low, high, low, pad], axis=0)
            scaled_rows = scaled.T.astype(BF16)
            query_rows = q_ref[at, :].astype(F32).T.astype(BF16)
            query_grad = None
            for i in range(parts):
                aug_value = jnp.concatenate(
                    [v_refs[i][at, :], jnp.ones((16, rows[i]), BF16)], axis=0
                )
                prob = p_ref[j, starts[i] : starts[i] + rows[i], :]
                score = (prob.astype(F32) * dot(aug_value, aug, 0, 0)).astype(BF16)
                value_out[i].append(dot(prob, scaled_rows, 1, 0).astype(BF16))
                key_out[i].append(dot(score, query_rows, 1, 0).astype(BF16))
                term = dot(k_refs[i][at, :], score, 1, 0)
                query_grad = term if query_grad is None else query_grad + term
            query_low = (query_grad * 0.125).astype(BF16)
            for g in range(groups):
                dq_ref[g, at, :] = query_low[:, g * tokens : (g + 1) * tokens]
        for i in range(parts):
            dk_refs[i][...] = jnp.concatenate(key_out[i], axis=1)
            dv_refs[i][...] = jnp.concatenate(value_out[i], axis=1)

    size = pair * HEAD_DIM
    kv_specs = [pl.BlockSpec((size, r), lambda h: (h, 0)) for r in rows]
    kv_grads = [pl.BlockSpec((r, size), lambda h: (0, h)) for r in rows]
    outs = pl.pallas_call(
        kernel,
        grid=(heads // pair,),
        in_specs=[pl.BlockSpec((size, length), lambda h: (h, 0))]
        + kv_specs
        + kv_specs
        + [
            pl.BlockSpec((pair, total, length), lambda h: (h, 0, 0)),
            pl.BlockSpec((groups, size, tokens), lambda h: (0, h, 0)),
            pl.BlockSpec((pair, 1, length), lambda h: (h, 0, 0)),
            pl.BlockSpec((pair, 1, length), lambda h: (h, 0, 0)),
        ],
        out_specs=[pl.BlockSpec((groups, size, tokens), lambda h: (0, h, 0))] + kv_grads + kv_grads,
        out_shape=[jax.ShapeDtypeStruct((groups, width, tokens), BF16)]
        + [jax.ShapeDtypeStruct((r, width), BF16) for r in rows] * 2,
        compiler_params=params(),
        cost_estimate=pl.CostEstimate(
            flops=32 * heads * total * length * HEAD_DIM,
            bytes_accessed=2 * heads * total * length,
            transcendentals=0,
        ),
        name="cross_backward",
    )(query, *keys, *values, prob, grads, weight, delta)
    return outs[0], list(outs[1 : 1 + parts]), list(outs[1 + parts :])


def self_forward(projected, key_pos, query_pos):
    own, length = projected.shape[1:]
    heads = own // HEAD_DIM

    def kernel(q_ref, k_ref, v_ref, kp_ref, qp_ref, o_ref, p_ref, w_ref):
        raw = dot(k_ref[0], q_ref[0], 0, 0) * 0.125
        raw = jnp.where(kp_ref[...] <= qp_ref[...], raw, negative_fill)
        top = jnp.max(raw, axis=0, keepdims=True)
        prob = jnp.exp(raw - top).astype(BF16)
        p_ref[0] = prob
        aug_value = jnp.concatenate([v_ref[0], jnp.ones((16, length), BF16)], axis=0)
        mixed = dot(aug_value, prob, 1, 0)
        inverse = 1.0 / mixed[HEAD_DIM : HEAD_DIM + 1]
        o_ref[...] = (mixed[:HEAD_DIM] * inverse).astype(BF16)
        w_ref[0] = inverse

    spec = lambda c: pl.BlockSpec((1, HEAD_DIM, length), lambda h: (c, h, 0))
    return pl.pallas_call(
        kernel,
        grid=(heads,),
        in_specs=[
            spec(0),
            spec(1),
            spec(2),
            pl.BlockSpec((length, 1), lambda h: (0, 0)),
            pl.BlockSpec((1, length), lambda h: (0, 0)),
        ],
        out_specs=[
            pl.BlockSpec((HEAD_DIM, length), lambda h: (h, 0)),
            pl.BlockSpec((1, length, length), lambda h: (h, 0, 0)),
            pl.BlockSpec((1, 1, length), lambda h: (h, 0, 0)),
        ],
        out_shape=[
            jax.ShapeDtypeStruct((own, length), BF16),
            jax.ShapeDtypeStruct((heads, length, length), BF16),
            jax.ShapeDtypeStruct((heads, 1, length), F32),
        ],
        compiler_params=params(),
        cost_estimate=pl.CostEstimate(
            flops=16 * heads * length * length * HEAD_DIM,
            bytes_accessed=2 * heads * length * length,
            transcendentals=heads * length * length,
        ),
        name="self_forward",
    )(projected, projected, projected, key_pos, query_pos)


def self_backward(projected, mixed, grads, prob, weight, groups):
    own, length = projected.shape[1:]
    heads = own // HEAD_DIM
    tokens = length // groups

    def kernel(q_ref, k_ref, v_ref, o_ref, g_ref, p_ref, w_ref, out_ref):
        grad = jnp.concatenate([g_ref[g] for g in range(groups)], axis=1).astype(F32)
        scaled = grad * w_ref[0]
        high, low = split_low(-jnp.sum(scaled * o_ref[...].astype(F32), axis=0, keepdims=True))
        scaled_low = scaled.astype(BF16)
        aug = jnp.concatenate([scaled_low, high, low, jnp.zeros((14, length), BF16)], axis=0)
        aug_value = jnp.concatenate([v_ref[0], jnp.ones((16, length), BF16)], axis=0)
        prob = p_ref[0]
        score = (prob.astype(F32) * dot(aug_value, aug, 0, 0)).astype(BF16)
        results = (
            dot(k_ref[0], score, 1, 0) * 0.125,
            dot(q_ref[0], score, 1, 1) * 0.125,
            dot(scaled_low, prob, 1, 1),
        )
        for c in range(3):
            result = results[c].astype(BF16)
            for g in range(groups):
                out_ref[g, c] = result[:, g * tokens : (g + 1) * tokens]

    spec = lambda c: pl.BlockSpec((1, HEAD_DIM, length), lambda h: (c, h, 0))
    return pl.pallas_call(
        kernel,
        grid=(heads,),
        in_specs=[
            spec(0),
            spec(1),
            spec(2),
            pl.BlockSpec((HEAD_DIM, length), lambda h: (h, 0)),
            pl.BlockSpec((groups, HEAD_DIM, tokens), lambda h: (0, h, 0)),
            pl.BlockSpec((1, length, length), lambda h: (h, 0, 0)),
            pl.BlockSpec((1, 1, length), lambda h: (h, 0, 0)),
        ],
        out_specs=pl.BlockSpec((groups, 3, HEAD_DIM, tokens), lambda h: (0, 0, h, 0)),
        out_shape=jax.ShapeDtypeStruct((groups, 3, own, tokens), BF16),
        compiler_params=params(),
        cost_estimate=pl.CostEstimate(
            flops=32 * heads * length * length * HEAD_DIM,
            bytes_accessed=2 * heads * length * length,
            transcendentals=0,
        ),
        name="self_backward",
    )(projected, projected, projected, mixed, grads, prob, weight)


def body(
    dec_input,
    enc_output,
    lengths,
    gains,
    self_qkv,
    self_out,
    cross_q,
    cross_kv,
    cross_out,
    ffn_in,
    ffn_out,
    cotangent,
):
    seg, seqs, width = dec_input.shape
    heads = width // HEAD_DIM
    blocks = lax.axis_size("blk")
    place = lax.axis_index("blk")
    groups = blocks // seqs
    mine = place // groups
    slot_of = lax.rem(place, groups)
    members = [[s * groups + g for g in range(groups)] for s in range(seqs)]
    own_heads = -(-heads // groups)
    own = own_heads * HEAD_DIM
    padded = own * groups
    tokens = seqs * seg
    length = groups * tokens
    enc_rows = enc_output.shape[1]
    gain_values = gains.astype(F32)

    def shifted(step):
        return [(b, (b + step * groups) % blocks) for b in range(blocks)]

    def exchange(pieces):
        parts = [pieces(mine)]
        for step in range(1, seqs):
            parts.append(lax.ppermute(pieces(lax.rem(mine + step, seqs)), "blk", shifted(step)))
        return parts

    def in_order(parts):
        ordered = []
        for s in range(seqs):
            choice = parts[0]
            for step in range(1, seqs):
                from_there = lax.rem(mine - step + seqs, seqs) == s
                choice = jnp.where(from_there, parts[step], choice)
            ordered.append(choice)
        return ordered

    def spread(array):
        return lax.all_to_all(
            jnp.broadcast_to(array[None], (groups,) + array.shape),
            "blk",
            0,
            0,
            axis_index_groups=members,
        )

    def traded(array):
        return lax.all_to_all(array, "blk", 0, 0, axis_index_groups=members)

    def gathered(array):
        take = lambda s: lax.dynamic_index_in_dim(array, s, 1, False)
        return jnp.concatenate(in_order(exchange(take)), axis=0)

    def returned(array):
        split = array.reshape(seqs, seg, width)
        take = lambda s: lax.dynamic_index_in_dim(split, s, 0, False)
        return jnp.stack(in_order(exchange(take)), axis=1)

    own_inputs = gathered(dec_input)
    all_inputs = spread(own_inputs).reshape(length, width).astype(F32)
    encoded = exchange(lambda s: lax.dynamic_index_in_dim(enc_output, s, 0, False))
    own_cotangent = gathered(cotangent)

    row_lengths = lax.dynamic_index_in_dim(lengths, mine, 0, False)
    bias = []
    for step in range(seqs):
        source = lax.rem(place - step * groups + blocks, blocks)
        slot = source * enc_rows + jnp.arange(enc_rows)
        match = (slot // SLOTS)[:, None] == jnp.arange(lengths.shape[1])[None, :]
        filled = jnp.sum(jnp.where(match, row_lengths[None, :], 0), axis=-1)
        row = jnp.where((slot % SLOTS) < filled, 0.0, negative_fill).astype(BF16)
        bias.append(jnp.concatenate([row[None], jnp.zeros((15, enc_rows), BF16)], axis=0))
    cross_keys = [dot(cross_kv[0], e, 0, 1).astype(BF16) for e in encoded]
    cross_values = [dot(cross_kv[1], e, 0, 1).astype(BF16) for e in encoded]

    first_low = normed(all_inputs, gain_values[0]).astype(BF16)
    extra = [(0, 0), (0, 0), (0, padded - width)]
    own_qkv = lax.dynamic_slice_in_dim(jnp.pad(self_qkv, extra), slot_of * own, own, 2)
    projected = jnp.stack([dot(own_qkv[c], first_low, 0, 1).astype(BF16) for c in range(3)])
    index = jnp.arange(length)
    block = index // seg
    position = ((block % seqs) * groups + block // seqs) * seg + index % seg
    position = position.astype(jnp.int32)
    own_mix, self_prob, self_weight = self_forward(projected, position[:, None], position[None, :])
    self_mix = spread(own_mix).reshape(padded, length)[:width]
    after_self_all = all_inputs + dot(self_mix, self_out, 0, 0)
    second_low_all = normed(after_self_all, gain_values[1]).astype(BF16)
    cross_query = dot(cross_q, second_low_all, 0, 1).astype(BF16) * jnp.asarray(0.125, BF16)

    def own_rows(array):
        return lax.dynamic_slice_in_dim(array, slot_of * tokens, tokens, 0)

    after_self = own_rows(after_self_all)
    second_low = own_rows(second_low_all)
    own_self_mix = lax.dynamic_slice_in_dim(self_mix, slot_of * tokens, tokens, 1)

    part_mix, cross_prob, local_top = cross_forward(
        cross_query, cross_keys, cross_values, bias, width, groups
    )
    stat_rows = (part_mix.shape[1] - width) // 2
    parts = traded(part_mix).astype(F32)
    part_lse = (parts[:, width : width + stat_rows] + parts[:, width + stat_rows :])[:, :heads]
    top = jnp.max(part_lse, axis=0)
    part_weight = jnp.exp(part_lse - top[None])
    weight_sum = jnp.sum(part_weight, axis=0)
    cross_lse = top + jnp.log(weight_sum)
    part_weight = part_weight / weight_sum[None]
    cross_mix = (
        jnp.sum(
            parts[:, :width].reshape(groups, heads, HEAD_DIM, tokens) * part_weight[:, :, None],
            axis=0,
        )
        .reshape(width, tokens)
        .astype(BF16)
    )

    after_cross = after_self + dot(cross_mix, cross_out, 0, 0)
    third_low = normed(after_cross, gain_values[2]).astype(BF16)
    hidden_pre = dot(third_low, ffn_in, 1, 0)
    hidden_low = jax.nn.gelu(hidden_pre).astype(BF16)
    output = returned((after_cross + dot(hidden_low, ffn_out, 1, 0)).astype(BF16))
    upstream = own_cotangent.astype(F32)
    hidden_grad = dot(own_cotangent, ffn_out, 1, 1)
    unused, gelu_pull = jax.vjp(jax.nn.gelu, hidden_pre)
    pre_low = gelu_pull(hidden_grad)[0].astype(BF16)
    step_grad, gain_three = norm_pull(after_cross, gain_values[2], dot(pre_low, ffn_in, 1, 1))
    cross_grad = upstream + step_grad
    cross_grad_low = cross_grad.astype(BF16)
    mix_grad = dot(cross_out, cross_grad_low, 1, 1).astype(BF16)
    row_term = jnp.sum(
        (mix_grad.astype(F32) * cross_mix.astype(F32)).reshape(heads, HEAD_DIM, tokens), axis=1
    )
    stats = jnp.concatenate([*split_sent(cross_lse), *split_sent(row_term)], axis=0)
    fill = jnp.zeros((-stats.shape[0] % 16, tokens), BF16)
    packed = spread(jnp.concatenate([mix_grad, stats, fill], axis=0))

    def whole_rows(start):
        rows = packed[:, start : start + 2 * heads].astype(F32)
        rows = rows[:, :heads] + rows[:, heads:]
        return rows.transpose(1, 0, 2).reshape(heads, 1, length)

    scale = jnp.exp(local_top - whole_rows(width))
    query_parts, key_low, value_low = cross_backward(
        cross_query,
        cross_keys,
        cross_values,
        cross_prob,
        packed,
        scale,
        whole_rows(width + 2 * heads) * scale,
        width,
        groups,
    )
    query_grad = jnp.sum(traded(query_parts).astype(F32), axis=0).astype(BF16)

    ffn_out_grad = dot(hidden_low, own_cotangent, 0, 0)
    ffn_in_grad = dot(third_low, pre_low, 0, 0)
    cross_out_grad = dot(cross_mix, cross_grad_low, 1, 0)
    cross_q_grad = dot(second_low, query_grad, 0, 1)
    key_weight_grad = sum(dot(e, g, 0, 0) for e, g in zip(encoded, key_low))
    value_weight_grad = sum(dot(e, g, 0, 0) for e, g in zip(encoded, value_low))
    enc_parts = [
        (dot(k, cross_kv[0], 1, 1) + dot(v, cross_kv[1], 1, 1)).astype(BF16)
        for k, v in zip(key_low, value_low)
    ]
    enc_back = [enc_parts[0]]
    for step in range(1, seqs):
        enc_back.append(
            lax.ppermute(enc_parts[step], "blk", [(b, a) for a, b in shifted(step)])
        )
    enc_grad = []
    for s in range(seqs):
        choice = enc_back[0]
        for step in range(1, seqs):
            choice = jnp.where(lax.rem(mine + step, seqs) == s, enc_back[step], choice)
        enc_grad.append(choice)
    enc_grad = jnp.stack(enc_grad, axis=0)

    step_grad, gain_two = norm_pull(after_self, gain_values[1], dot(query_grad, cross_q, 0, 1))
    self_grad = cross_grad + step_grad
    self_grad_low = self_grad.astype(BF16)
    self_out_grad = dot(own_self_mix, self_grad_low, 1, 0)
    mixed_grad = dot(self_out, self_grad_low, 1, 1).astype(BF16)
    mixed_grad = jnp.pad(mixed_grad, [(0, padded - width), (0, 0)])
    grads = traded(mixed_grad.reshape(groups, own, tokens))
    own_grads = self_backward(projected, own_mix, grads, self_prob, self_weight, groups)
    back = traded(own_grads)
    back = back.transpose(1, 0, 2, 3).reshape(3, padded, tokens)[:, :width]
    own_first = own_rows(first_low)
    self_qkv_grad = jnp.stack([dot(own_first, back[c], 0, 1) for c in range(3)])
    first_back = sum(dot(back[c], self_qkv[c], 0, 1) for c in range(3))
    step_grad, gain_one = norm_pull(own_rows(all_inputs), gain_values[0], first_back)
    dec_grad = returned((self_grad + step_grad).astype(BF16))

    gain_grads = lax.psum(jnp.stack([gain_one, gain_two, gain_three]), ("blk", "dp"))

    def scattered(grad, axis):
        grad = lax.psum_scatter(grad.astype(BF16), "blk", scatter_dimension=axis, tiled=True)
        return lax.psum_scatter(grad, "dp", scatter_dimension=axis + 1, tiled=True).astype(F32)

    return (
        output,
        dec_grad,
        enc_grad,
        gain_grads,
        scattered(self_qkv_grad, 1),
        scattered(self_out_grad, 0),
        scattered(cross_q_grad, 0),
        scattered(jnp.stack([key_weight_grad, value_weight_grad]), 1),
        scattered(cross_out_grad, 0),
        scattered(ffn_in_grad, 0),
        scattered(ffn_out_grad, 0),
    )


def solution(mesh):
    placed = (
        P("blk", "dp", None),
        P("dp", "blk", None),
        P("dp", None),
        P(),
        P(),
        P(),
        P(),
        P(),
        P(),
        P(),
        P(),
        P("blk", "dp", None),
    )
    return jax.shard_map(
        body,
        mesh=mesh,
        in_specs=placed,
        out_specs=(
            P("blk", "dp", None),
            P("blk", "dp", None),
            P("dp", "blk", None),
            P(),
            P(None, "blk", "dp"),
            P("blk", "dp"),
            P("blk", "dp"),
            P(None, "blk", "dp"),
            P("blk", "dp"),
            P("blk", "dp"),
            P("blk", "dp"),
        ),
        check_vma=False,
    )
```

```python
import functools

import jax
import jax.numpy as jnp
from jax import lax
from jax.experimental import pallas as pl
from jax.experimental.pallas import tpu as pltpu
from jax.sharding import PartitionSpec as P

HEAD_DIM = 64
SLOTS = 448
F32 = jnp.float32
BF16 = jnp.bfloat16
epsilon = 1e-06
negative_fill = -1e30
safe_score = 60.0
VMEM_LIMIT = 60 * 1024 * 1024


def dot(left, right, left_dim, right_dim):
    return lax.dot_general(
        left, right, (((left_dim,), (right_dim,)), ((), ())), preferred_element_type=F32
    )


def split_low(value):
    high = value.astype(BF16)
    return high, (value - high.astype(F32)).astype(BF16)


def normed(values, gain):
    return values * lax.rsqrt(jnp.mean(values * values, axis=-1, keepdims=True) + epsilon) * gain


def parted(array, axis, dim):
    size = lax.axis_size(axis)
    shape = array.shape
    above = size // shape[dim]
    split = array.reshape(shape[:dim] + (shape[dim] // 2, 2) + shape[dim + 1 :])
    bit = lax.rem(lax.axis_index(axis) // above, 2)
    kept = lax.dynamic_index_in_dim(split, bit, dim + 1, False)
    sent = lax.dynamic_index_in_dim(split, 1 - bit, dim + 1, False)
    return kept, sent, [(i, i ^ above) for i in range(size)]


def added(kept, got):
    return (kept.astype(F32) + got.astype(F32)).astype(BF16)


class Halving:
    def __init__(self, array):
        self.array = array

    def send(self, axis, dim):
        self.kept, sent, pairs = parted(self.array, axis, dim)
        self.got = lax.ppermute(sent, axis, pairs)

    def take(self):
        self.array = added(self.kept, self.got)


def after(value, *halvings):
    value, got = lax.optimization_barrier((value, [h.got for h in halvings]))
    for halving, piece in zip(halvings, got):
        halving.got = piece
        halving.take()
    return value


def halved(array, axis, dim):
    while array.shape[dim] > 1:
        kept, sent, pairs = parted(array, axis, dim)
        array = added(kept, lax.ppermute(sent, axis, pairs))
    return jnp.squeeze(array, dim)


def total_of(array):
    for axis in ("dp", "blk"):
        size = lax.axis_size(axis)
        copies = jnp.broadcast_to(array[None], (size,) + array.shape)
        array = jnp.sum(lax.all_to_all(copies, axis, 0, 0), axis=0)
    return array


def estimate(flops, bytes_accessed, transcendentals):
    scale = 10**9
    return pl.CostEstimate(
        flops=max(flops // scale, 1),
        bytes_accessed=max(bytes_accessed // scale, 1),
        transcendentals=transcendentals // scale,
    )


def params():
    return pltpu.CompilerParams(vmem_limit_bytes=VMEM_LIMIT)


def cross_forward(query, pairs, bias, width, groups):
    heads = width // HEAD_DIM
    length = query.shape[1]
    tokens = length // groups
    parts = len(pairs)
    rows = [p.shape[2] for p in pairs]
    starts = [sum(rows[:i]) for i in range(parts)]
    total = sum(rows)
    stat_rows = 16 * ((heads + 15) // 16)

    def kernel(*refs):
        q_ref = refs[0]
        k_refs = refs[1 : 1 + parts]
        v_refs = refs[1 + parts : 1 + 2 * parts]
        b_refs = refs[1 + 2 * parts : 1 + 3 * parts]
        o_ref, p_ref, m_ref, lse_ref = refs[1 + 3 * parts :]
        head = pl.program_id(0)
        query = q_ref[...]
        aug_query = jnp.concatenate([query, jnp.ones((16, length), BF16)], axis=0)
        q_norm = jnp.max(jnp.sum(jnp.square(query.astype(F32)), axis=0, keepdims=True))
        k_norm = jnp.float32(0)
        for k_ref in k_refs:
            k_norm = jnp.maximum(
                k_norm, jnp.max(jnp.sum(jnp.square(k_ref[0].astype(F32)), axis=0, keepdims=True))
            )
        small = q_norm * k_norm < safe_score * safe_score

        def score(i):
            return dot(jnp.concatenate([k_refs[i][0], b_refs[i][...]], axis=0), aug_query, 0, 0)

        def finish(probs, top):
            mixed = None
            for i in range(parts):
                aug_value = jnp.concatenate([v_refs[i][0], jnp.ones((16, rows[i]), BF16)], axis=0)
                term = dot(aug_value, probs[i], 1, 0)
                mixed = term if mixed is None else mixed + term
            norm = mixed[HEAD_DIM : HEAD_DIM + 1]
            out = (mixed[:HEAD_DIM] / norm).astype(BF16)
            where = pl.ds(pl.multiple_of(head * HEAD_DIM, HEAD_DIM), HEAD_DIM)
            for g in range(groups):
                o_ref[g, where, :] = out[:, g * tokens : (g + 1) * tokens]
            lse_ref[pl.ds(head, 1), :] = top + jnp.log(norm)
            m_ref[0] = top

        @pl.when(small)
        def plain():
            probs = []
            for i in range(parts):
                prob = jnp.exp(score(i)).astype(BF16)
                p_ref[0, starts[i] : starts[i] + rows[i], :] = prob
                probs.append(prob)
            finish(probs, jnp.zeros((1, length), F32))

        @pl.when(jnp.logical_not(small))
        def shifted():
            raw = [score(i) for i in range(parts)]
            top = jnp.max(raw[0], axis=0, keepdims=True)
            for i in range(1, parts):
                top = jnp.maximum(top, jnp.max(raw[i], axis=0, keepdims=True))
            probs = []
            for i in range(parts):
                prob = jnp.exp(raw[i] - top).astype(BF16)
                p_ref[0, starts[i] : starts[i] + rows[i], :] = prob
                probs.append(prob)
            finish(probs, top)

        @pl.when(head == heads - 1)
        def stats():
            high, low = split_low(lse_ref[...])
            for g in range(groups):
                o_ref[g, width : width + stat_rows, :] = high[:, g * tokens : (g + 1) * tokens]
                o_ref[g, width + stat_rows :, :] = low[:, g * tokens : (g + 1) * tokens]

    payload = width + 2 * stat_rows
    key_specs = [pl.BlockSpec((1, HEAD_DIM, r), lambda h: (0, h, 0)) for r in rows]
    value_specs = [pl.BlockSpec((1, HEAD_DIM, r), lambda h: (1, h, 0)) for r in rows]
    return pl.pallas_call(
        kernel,
        grid=(heads,),
        in_specs=[pl.BlockSpec((HEAD_DIM, length), lambda h: (h, 0))]
        + key_specs
        + value_specs
        + [pl.BlockSpec((16, r), lambda h: (0, 0)) for r in rows],
        out_specs=[
            pl.BlockSpec((groups, payload, tokens), lambda h: (0, 0, 0)),
            pl.BlockSpec((1, total, length), lambda h: (h, 0, 0)),
            pl.BlockSpec((1, 1, length), lambda h: (h, 0, 0)),
        ],
        out_shape=[
            jax.ShapeDtypeStruct((groups, payload, tokens), BF16),
            jax.ShapeDtypeStruct((heads, total, length), BF16),
            jax.ShapeDtypeStruct((heads, 1, length), F32),
        ],
        scratch_shapes=[pltpu.VMEM((stat_rows, length), F32)],
        compiler_params=params(),
        cost_estimate=estimate(
            flops=16 * heads * total * length * HEAD_DIM,
            bytes_accessed=2 * heads * total * length,
            transcendentals=heads * total * length,
        ),
        name="cross_forward",
    )(query, *pairs, *pairs, *bias)


def cross_backward(query, pairs, prob, grads, weight, delta, width, groups):
    heads = width // HEAD_DIM
    length = query.shape[1]
    tokens = length // groups
    parts = len(pairs)
    rows = [p.shape[2] for p in pairs]
    starts = [sum(rows[:i]) for i in range(parts)]
    total = sum(rows)
    pair = 2

    def kernel(*refs):
        q_ref = refs[0]
        k_refs = refs[1 : 1 + parts]
        v_refs = refs[1 + parts : 1 + 2 * parts]
        p_ref, g_ref, w_ref, d_ref = refs[1 + 2 * parts : 5 + 2 * parts]
        dq_ref = refs[5 + 2 * parts]
        dk_refs = refs[6 + 2 * parts : 6 + 3 * parts]
        dv_refs = refs[6 + 3 * parts :]
        key_out = [[] for _ in range(parts)]
        value_out = [[] for _ in range(parts)]
        for j in range(pair):
            at = slice(j * HEAD_DIM, (j + 1) * HEAD_DIM)
            grad = jnp.concatenate([g_ref[g, at, :] for g in range(groups)], axis=1).astype(F32)
            scaled = grad * w_ref[j]
            high, low = split_low(-d_ref[j])
            scaled_low = scaled.astype(BF16)
            pad = jnp.zeros((14, length), BF16)
            aug = jnp.concatenate([scaled_low, high, low, pad], axis=0)
            scaled_rows = scaled.T.astype(BF16)
            query_rows = q_ref[at, :].astype(F32).T.astype(BF16)
            query_grad = None
            for i in range(parts):
                aug_value = jnp.concatenate(
                    [v_refs[i][0, at, :], jnp.ones((16, rows[i]), BF16)], axis=0
                )
                prob = p_ref[j, starts[i] : starts[i] + rows[i], :]
                score = (prob.astype(F32) * dot(aug_value, aug, 0, 0)).astype(BF16)
                value_out[i].append(dot(prob, scaled_rows, 1, 0).astype(BF16))
                key_out[i].append(dot(score, query_rows, 1, 0).astype(BF16))
                term = dot(k_refs[i][0, at, :], score, 1, 0)
                query_grad = term if query_grad is None else query_grad + term
            query_low = (query_grad * 0.125).astype(BF16)
            for g in range(groups):
                dq_ref[g, at, :] = query_low[:, g * tokens : (g + 1) * tokens]
        for i in range(parts):
            dk_refs[i][...] = jnp.concatenate(key_out[i], axis=1)
            dv_refs[i][...] = jnp.concatenate(value_out[i], axis=1)

    size = pair * HEAD_DIM
    key_specs = [pl.BlockSpec((1, size, r), lambda h: (0, h, 0)) for r in rows]
    value_specs = [pl.BlockSpec((1, size, r), lambda h: (1, h, 0)) for r in rows]
    kv_grads = [pl.BlockSpec((r, size), lambda h: (0, h)) for r in rows]
    outs = pl.pallas_call(
        kernel,
        grid=(heads // pair,),
        in_specs=[pl.BlockSpec((size, length), lambda h: (h, 0))]
        + key_specs
        + value_specs
        + [
            pl.BlockSpec((pair, total, length), lambda h: (h, 0, 0)),
            pl.BlockSpec((groups, size, tokens), lambda h: (0, h, 0)),
            pl.BlockSpec((pair, 1, length), lambda h: (h, 0, 0)),
            pl.BlockSpec((pair, 1, length), lambda h: (h, 0, 0)),
        ],
        out_specs=[pl.BlockSpec((groups, size, tokens), lambda h: (0, h, 0))] + kv_grads + kv_grads,
        out_shape=[jax.ShapeDtypeStruct((groups, width, tokens), BF16)]
        + [jax.ShapeDtypeStruct((r, width), BF16) for r in rows] * 2,
        compiler_params=params(),
        cost_estimate=estimate(
            flops=32 * heads * total * length * HEAD_DIM,
            bytes_accessed=2 * heads * total * length,
            transcendentals=0,
        ),
        name="cross_backward",
    )(query, *pairs, *pairs, prob, grads, weight, delta)
    return outs[0], list(outs[1 : 1 + parts]), list(outs[1 + parts :])


def self_forward(inputs, gain, weights, key_pos, query_pos, groups):
    length, width = inputs.shape
    own = weights.shape[1]
    heads = own // HEAD_DIM

    def kernel(x_ref, g_ref, w_ref, kp_ref, qp_ref, a_ref, pr_ref, o_ref, p_ref, n_ref):
        head = pl.program_id(0)

        @pl.when(head == 0)
        def project():
            low = normed(x_ref[...].astype(F32), g_ref[...]).astype(BF16)
            a_ref[...] = low
            for c in range(3):
                pr_ref[c] = dot(w_ref[c], low, 1, 1).astype(BF16)

        at = pl.ds(pl.multiple_of(head * HEAD_DIM, HEAD_DIM), HEAD_DIM)
        raw = dot(pr_ref[1, at, :], pr_ref[0, at, :], 0, 0) * 0.125
        raw = jnp.where(kp_ref[...] <= qp_ref[...], raw, negative_fill)
        top = jnp.max(raw, axis=0, keepdims=True)
        prob = jnp.exp(raw - top).astype(BF16)
        p_ref[0] = prob
        aug_value = jnp.concatenate([pr_ref[2, at, :], jnp.ones((16, length), BF16)], axis=0)
        mixed = dot(aug_value, prob, 1, 0)
        inverse = 1.0 / mixed[HEAD_DIM : HEAD_DIM + 1]
        out = (mixed[:HEAD_DIM] * inverse).astype(BF16)
        for g in range(groups):
            o_ref[g] = out
        n_ref[0] = inverse

    whole = lambda *shape: pl.BlockSpec(shape, lambda h: (0,) * len(shape))
    return pl.pallas_call(
        kernel,
        grid=(heads,),
        in_specs=[
            whole(length, width),
            whole(1, width),
            whole(3, own, width),
            whole(length, 1),
            whole(1, length),
        ],
        out_specs=[
            whole(length, width),
            whole(3, own, length),
            pl.BlockSpec((groups, HEAD_DIM, length), lambda h: (0, h, 0)),
            pl.BlockSpec((1, length, length), lambda h: (h, 0, 0)),
            pl.BlockSpec((1, 1, length), lambda h: (h, 0, 0)),
        ],
        out_shape=[
            jax.ShapeDtypeStruct((length, width), BF16),
            jax.ShapeDtypeStruct((3, own, length), BF16),
            jax.ShapeDtypeStruct((groups, own, length), BF16),
            jax.ShapeDtypeStruct((heads, length, length), BF16),
            jax.ShapeDtypeStruct((heads, 1, length), F32),
        ],
        compiler_params=params(),
        cost_estimate=estimate(
            flops=16 * heads * length * length * HEAD_DIM,
            bytes_accessed=2 * heads * length * length,
            transcendentals=heads * length * length,
        ),
        name="self_forward",
    )(inputs, gain, weights, key_pos, query_pos)


def project_rows(pieces, weights):
    counts = [p.shape[0] for p in pieces]
    total, width = sum(counts), pieces[0].shape[1]

    def kernel(*refs):
        w_ref, out_ref = refs[len(counts) :]
        start = 0
        for e_ref, count in zip(refs, counts):
            out_ref[0, :, start : start + count] = dot(w_ref[0], e_ref[...], 1, 1).astype(BF16)
            start += count

    return pl.pallas_call(
        kernel,
        grid=(2,),
        in_specs=[pl.BlockSpec((count, width), lambda c: (0, 0)) for count in counts]
        + [pl.BlockSpec((1, width, width), lambda c: (c, 0, 0))],
        out_specs=pl.BlockSpec((1, width, total), lambda c: (c, 0, 0)),
        out_shape=jax.ShapeDtypeStruct((2, width, total), BF16),
        compiler_params=params(),
        cost_estimate=estimate(
            flops=4 * total * width * width, bytes_accessed=8 * total * width, transcendentals=0
        ),
        name="project_rows",
    )(*pieces, weights)


def query_stage(inputs, mixed, out_weight, gain, query_weight, slot, groups):
    length, width = inputs.shape
    tokens = length // groups
    rows = mixed.shape[0]

    def kernel(s_ref, x_ref, o_ref, w_ref, g_ref, q_ref, qc_ref, h_ref, a_ref):
        after = x_ref[...].astype(F32) + dot(o_ref[...], w_ref[...], 0, 0)
        low = normed(after, g_ref[...]).astype(BF16)
        scaled = dot(q_ref[...], low, 1, 1).astype(BF16)
        qc_ref[...] = (scaled.astype(F32) * 0.125).astype(BF16)

        @pl.when(pl.program_id(0) == s_ref[0])
        def keep():
            h_ref[...] = after
            a_ref[...] = low

    whole = lambda *shape: pl.BlockSpec(shape, lambda i, s: (0,) * len(shape))
    return pl.pallas_call(
        kernel,
        grid_spec=pltpu.PrefetchScalarGridSpec(
            num_scalar_prefetch=1,
            grid=(groups,),
            in_specs=[
                pl.BlockSpec((tokens, width), lambda i, s: (i, 0)),
                pl.BlockSpec((rows, tokens), lambda i, s: (0, i)),
                whole(rows, width),
                whole(1, width),
                whole(width, width),
            ],
            out_specs=[
                pl.BlockSpec((width, tokens), lambda i, s: (0, i)),
                whole(tokens, width),
                whole(tokens, width),
            ],
        ),
        out_shape=[
            jax.ShapeDtypeStruct((width, length), BF16),
            jax.ShapeDtypeStruct((tokens, width), F32),
            jax.ShapeDtypeStruct((tokens, width), BF16),
        ],
        compiler_params=params(),
        cost_estimate=estimate(
            flops=8 * length * width * width, bytes_accessed=8 * width * width, transcendentals=0
        ),
        name="query_stage",
    )(slot, inputs, mixed, out_weight, gain, query_weight)


def gelu_parts(value):
    root = 0.7978845608028654
    cubic = 0.044715
    square = value * value
    bent = jnp.tanh(root * value * (1.0 + cubic * square))
    half = 0.5 * (1.0 + bent)
    slope = half + 0.5 * value * (1.0 - bent * bent) * root * (1.0 + 3.0 * cubic * square)
    return value * half, slope


def pulled_norm(values, gain, grad):
    inverse = lax.rsqrt(jnp.mean(values * values, axis=-1, keepdims=True) + epsilon)
    scaled = values * inverse
    gain_grad = jnp.sum(grad * scaled, axis=0, keepdims=True)
    weighted = grad * gain
    back = inverse * (weighted - scaled * jnp.mean(weighted * scaled, axis=-1, keepdims=True))
    return back, gain_grad


def token_stage(parts, after_self, cross_out, gain, ffn_in, ffn_out, cotangent, groups):
    tokens, width = after_self.shape
    heads = width // HEAD_DIM
    stat_rows = (parts.shape[1] - width) // 2
    hidden = ffn_in.shape[1]
    piece = 384
    steps = hidden // piece
    payload = width + 4 * stat_rows

    def kernel(
        r_ref, h_ref, co_ref, g_ref, w1_ref, w2_ref, c_ref,
        out_ref, dh_ref, g2_ref, a_ref, z_ref, du_ref, o_ref, pay_ref, gain_ref,
        after_ref, acc_ref, back_ref, lse_ref,
    ):
        step = pl.program_id(0)

        @pl.when(step == 0)
        def join():
            lse = [
                r_ref[g, width : width + stat_rows, :].astype(F32)
                + r_ref[g, width + stat_rows :, :].astype(F32)
                for g in range(groups)
            ]
            top = functools.reduce(jnp.maximum, lse)
            share = [jnp.exp(l - top) for l in lse]
            total = functools.reduce(jnp.add, share)
            lse_ref[...] = top + jnp.log(total)
            share = [s / total for s in share]
            for h in range(heads):
                at = slice(h * HEAD_DIM, (h + 1) * HEAD_DIM)
                mixed = None
                for g in range(groups):
                    term = r_ref[g, at, :].astype(F32) * share[g][h : h + 1]
                    mixed = term if mixed is None else mixed + term
                o_ref[at, :] = mixed.astype(BF16)
            after = h_ref[...] + dot(o_ref[...], co_ref[...], 0, 0)
            after_ref[...] = after
            a_ref[...] = normed(after, g_ref[...]).astype(BF16)
            acc_ref[...] = jnp.zeros_like(acc_ref)
            back_ref[...] = jnp.zeros_like(back_ref)

        pre = dot(a_ref[...], w1_ref[...], 1, 0)
        act, slope = gelu_parts(pre)
        act = act.astype(BF16)
        z_ref[...] = act
        acc_ref[...] += dot(act, w2_ref[...], 1, 0)
        pre_grad = (dot(c_ref[...], w2_ref[...], 1, 1) * slope).astype(BF16)
        du_ref[...] = pre_grad
        back_ref[...] += dot(pre_grad, w1_ref[...], 1, 1)

        @pl.when(step == steps - 1)
        def finish():
            after = after_ref[...]
            out_ref[...] = (after + acc_ref[...]).astype(BF16)
            back, gain_grad = pulled_norm(after, g_ref[...], back_ref[...])
            gain_ref[...] = gain_grad
            grad = c_ref[...].astype(F32) + back
            dh_ref[...] = grad
            low = grad.astype(BF16)
            g2_ref[...] = low
            mix_grad = dot(co_ref[...], low, 1, 1).astype(BF16)
            both = mix_grad.astype(F32) * o_ref[...].astype(F32)
            rows = [
                jnp.sum(both[h * HEAD_DIM : (h + 1) * HEAD_DIM], axis=0, keepdims=True)
                for h in range(heads)
            ]
            rows.append(jnp.zeros((stat_rows - heads, tokens), F32))
            stats = [*split_low(lse_ref[...]), *split_low(jnp.concatenate(rows, axis=0))]
            for g in range(groups):
                pay_ref[g, :width, :] = mix_grad
                for i in range(4):
                    start = width + i * stat_rows
                    pay_ref[g, start : start + stat_rows, :] = stats[i]

    whole = lambda *shape: pl.BlockSpec(shape, lambda i: (0,) * len(shape))
    flat = lambda rows, kind: jax.ShapeDtypeStruct((rows, width), kind)
    return pl.pallas_call(
        kernel,
        grid=(steps,),
        in_specs=[
            whole(*parts.shape),
            whole(tokens, width),
            whole(width, width),
            whole(1, width),
            pl.BlockSpec((width, piece), lambda i: (0, i)),
            pl.BlockSpec((piece, width), lambda i: (i, 0)),
            whole(tokens, width),
        ],
        out_specs=[
            whole(tokens, width),
            whole(tokens, width),
            whole(tokens, width),
            whole(tokens, width),
            pl.BlockSpec((tokens, piece), lambda i: (0, i)),
            pl.BlockSpec((tokens, piece), lambda i: (0, i)),
            whole(width, tokens),
            whole(groups, payload, tokens),
            whole(1, width),
        ],
        out_shape=[
            flat(tokens, BF16),
            flat(tokens, F32),
            flat(tokens, BF16),
            flat(tokens, BF16),
            jax.ShapeDtypeStruct((tokens, hidden), BF16),
            jax.ShapeDtypeStruct((tokens, hidden), BF16),
            jax.ShapeDtypeStruct((width, tokens), BF16),
            jax.ShapeDtypeStruct((groups, payload, tokens), BF16),
            flat(1, F32),
        ],
        scratch_shapes=[pltpu.VMEM((tokens, width), F32)] * 3
        + [pltpu.VMEM((stat_rows, tokens), F32)],
        compiler_params=params(),
        cost_estimate=estimate(
            flops=8 * tokens * width * hidden,
            bytes_accessed=4 * width * hidden,
            transcendentals=tokens * hidden,
        ),
        name="token_stage",
    )(parts, after_self, cross_out, gain, ffn_in, ffn_out, cotangent)


def hidden_weight_grads(low, pre_grad, act, cotangent, columns, blocks):
    tokens, width = low.shape
    hidden = act.shape[1]
    piece = hidden // blocks
    in_rows, out_rows = width // blocks, piece // columns
    per = width // piece

    def kernel(a_ref, du_ref, z_ref, c_ref, in_ref, out_ref):
        first = dot(a_ref[...], du_ref[...], 0, 0).astype(BF16)
        for b in range(blocks):
            in_ref[0, b] = first[b * in_rows : (b + 1) * in_rows]
        second = dot(z_ref[...], c_ref[...], 0, 0).astype(BF16)
        for d in range(columns):
            out_ref[d, 0] = second[d * out_rows : (d + 1) * out_rows]

    whole = lambda *shape: pl.BlockSpec(shape, lambda i: (0,) * len(shape))
    return pl.pallas_call(
        kernel,
        grid=(blocks,),
        in_specs=[
            whole(tokens, width),
            pl.BlockSpec((tokens, piece), lambda i: (0, i)),
            pl.BlockSpec((tokens, piece), lambda i: (0, i)),
            whole(tokens, width),
        ],
        out_specs=[
            pl.BlockSpec((1, blocks, in_rows, piece), lambda i: (i // per, 0, 0, i % per)),
            pl.BlockSpec((columns, 1, out_rows, width), lambda i: (0, i, 0, 0)),
        ],
        out_shape=[
            jax.ShapeDtypeStruct((columns, blocks, in_rows, width), BF16),
            jax.ShapeDtypeStruct((columns, blocks, out_rows, width), BF16),
        ],
        compiler_params=params(),
        cost_estimate=estimate(
            flops=4 * tokens * width * hidden,
            bytes_accessed=4 * width * hidden,
            transcendentals=0,
        ),
        name="hidden_weight_grads",
    )(low, pre_grad, act, cotangent)


def mixed_stage(parts, cross_q, after_self, gain, cross_grad, self_out, groups, own):
    tokens, width = after_self.shape
    rows = self_out.shape[0]

    def kernel(r_ref, q_ref, h_ref, g_ref, dh_ref, w_ref, dq_ref, out_ref, g1_ref, do_ref, gain_ref):
        total = r_ref[0].astype(F32)
        for g in range(1, groups):
            total = total + r_ref[g].astype(F32)
        query_grad = total.astype(BF16)
        dq_ref[...] = query_grad
        back, gain_grad = pulled_norm(h_ref[...], g_ref[...], dot(query_grad, q_ref[...], 0, 1))
        gain_ref[...] = gain_grad
        grad = dh_ref[...] + back
        out_ref[...] = grad
        low = grad.astype(BF16)
        g1_ref[...] = low
        mixed = dot(w_ref[...], low, 1, 1).astype(BF16)
        for g in range(groups):
            do_ref[g] = mixed[g * own : (g + 1) * own]

    return pl.pallas_call(
        kernel,
        out_shape=[
            jax.ShapeDtypeStruct((width, tokens), BF16),
            jax.ShapeDtypeStruct((tokens, width), F32),
            jax.ShapeDtypeStruct((tokens, width), BF16),
            jax.ShapeDtypeStruct((groups, own, tokens), BF16),
            jax.ShapeDtypeStruct((1, width), F32),
        ],
        compiler_params=params(),
        cost_estimate=estimate(
            flops=4 * tokens * width * width, bytes_accessed=8 * width * width, transcendentals=0
        ),
        name="mixed_stage",
    )(parts, cross_q, after_self, gain, cross_grad, self_out)


def input_stage(back, weights, inputs, gain, self_grad, groups):
    own, tokens = back.shape[2:]
    width = inputs.shape[1]
    padded = groups * own

    def kernel(b_ref, w_ref, x_ref, g_ref, h_ref, out_ref, acc_ref):
        step = pl.program_id(0)
        grads = jnp.concatenate([b_ref[g, 0] for g in range(groups)], axis=0)
        term = dot(grads, w_ref[0], 0, 1)

        @pl.when(step == 0)
        def first():
            acc_ref[...] = term

        @pl.when(step > 0)
        def more():
            acc_ref[...] += term

        @pl.when(step == 2)
        def last():
            back, unused = pulled_norm(x_ref[...].astype(F32), g_ref[...], acc_ref[...])
            out_ref[...] = (h_ref[...] + back).astype(BF16)

    whole = lambda *shape: pl.BlockSpec(shape, lambda i: (0,) * len(shape))
    return pl.pallas_call(
        kernel,
        grid=(3,),
        in_specs=[
            pl.BlockSpec((groups, 1, own, tokens), lambda i: (0, i, 0, 0)),
            pl.BlockSpec((1, width, padded), lambda i: (i, 0, 0)),
            whole(tokens, width),
            whole(1, width),
            whole(tokens, width),
        ],
        out_specs=whole(tokens, width),
        out_shape=jax.ShapeDtypeStruct((tokens, width), BF16),
        scratch_shapes=[pltpu.VMEM((tokens, width), F32)],
        compiler_params=params(),
        cost_estimate=estimate(
            flops=6 * tokens * width * width, bytes_accessed=6 * width * width, transcendentals=0
        ),
        name="input_stage",
    )(back, weights, inputs, gain, self_grad)


def both_queries(own, pieces, mine):
    rows, width = own.shape

    def kernel(s_ref, own_ref, *refs):
        out_ref = refs[-1]

        @pl.when(pl.program_id(0) == s_ref[0])
        def here():
            out_ref[0] = own_ref[...]

        @pl.when(pl.program_id(0) != s_ref[0])
        def there():
            start = 0
            for ref in refs[:-1]:
                out_ref[0, start : start + ref.shape[0], :] = ref[...]
                start += ref.shape[0]

    whole = lambda *shape: pl.BlockSpec(shape, lambda i, s: (0,) * len(shape))
    return pl.pallas_call(
        kernel,
        grid_spec=pltpu.PrefetchScalarGridSpec(
            num_scalar_prefetch=1,
            grid=(2,),
            in_specs=[whole(*own.shape)] + [whole(*p.shape) for p in pieces],
            out_specs=pl.BlockSpec((1, rows, width), lambda i, s: (i, 0, 0)),
        ),
        out_shape=jax.ShapeDtypeStruct((2, rows, width), own.dtype),
        compiler_params=params(),
        cost_estimate=estimate(flops=0, bytes_accessed=8 * rows * width, transcendentals=0),
        name="both_queries",
    )(mine, own, *pieces)


def own_weight_grads(low, inputs, grads, weights, blocks):
    length, width = inputs.shape
    groups, _, own, tokens = grads.shape
    rows = width // blocks

    def kernel(a_ref, x_ref, d_ref, w_ref, out_ref, gain_ref, acc_ref):
        step = pl.program_id(0)
        grads = jnp.concatenate([d_ref[g, 0] for g in range(groups)], axis=1)
        weight = dot(grads, a_ref[...], 1, 0).T.astype(BF16)
        for b in range(blocks):
            out_ref[b, 0] = weight[b * rows : (b + 1) * rows]
        term = dot(grads, w_ref[0], 0, 0)

        @pl.when(step == 0)
        def first():
            acc_ref[...] = term

        @pl.when(step > 0)
        def more():
            acc_ref[...] += term

        @pl.when(step == 2)
        def last():
            values = x_ref[...].astype(F32)
            inverse = lax.rsqrt(jnp.mean(values * values, axis=-1, keepdims=True) + epsilon)
            gain_ref[...] = jnp.sum(acc_ref[...] * values * inverse, axis=0, keepdims=True)

    whole = lambda *shape: pl.BlockSpec(shape, lambda i: (0,) * len(shape))
    return pl.pallas_call(
        kernel,
        grid=(3,),
        in_specs=[
            whole(length, width),
            whole(length, width),
            pl.BlockSpec((groups, 1, own, tokens), lambda i: (0, i, 0, 0)),
            pl.BlockSpec((1, own, width), lambda i: (i, 0, 0)),
        ],
        out_specs=[pl.BlockSpec((blocks, 1, rows, own), lambda i: (0, i, 0, 0)), whole(1, width)],
        out_shape=[
            jax.ShapeDtypeStruct((blocks, 3, rows, own), BF16),
            jax.ShapeDtypeStruct((1, width), F32),
        ],
        scratch_shapes=[pltpu.VMEM((length, width), F32)],
        compiler_params=params(),
        cost_estimate=estimate(
            flops=12 * length * width * own, bytes_accessed=4 * length * width, transcendentals=0
        ),
        name="own_weight_grads",
    )(low, inputs, grads, weights)


def self_backward(projected, mixed, grads, prob, weight, groups):
    own, length = projected.shape[1:]
    heads = own // HEAD_DIM
    tokens = length // groups

    def kernel(q_ref, k_ref, v_ref, o_ref, g_ref, p_ref, w_ref, out_ref):
        grad = jnp.concatenate([g_ref[g] for g in range(groups)], axis=1).astype(F32)
        scaled = grad * w_ref[0]
        high, low = split_low(-jnp.sum(scaled * o_ref[0].astype(F32), axis=0, keepdims=True))
        scaled_low = scaled.astype(BF16)
        aug = jnp.concatenate([scaled_low, high, low, jnp.zeros((14, length), BF16)], axis=0)
        aug_value = jnp.concatenate([v_ref[0], jnp.ones((16, length), BF16)], axis=0)
        prob = p_ref[0]
        score = (prob.astype(F32) * dot(aug_value, aug, 0, 0)).astype(BF16)
        results = (
            dot(k_ref[0], score, 1, 0) * 0.125,
            dot(q_ref[0], score, 1, 1) * 0.125,
            dot(scaled_low, prob, 1, 1),
        )
        for c in range(3):
            result = results[c].astype(BF16)
            for g in range(groups):
                out_ref[g, c] = result[:, g * tokens : (g + 1) * tokens]

    spec = lambda c: pl.BlockSpec((1, HEAD_DIM, length), lambda h: (c, h, 0))
    return pl.pallas_call(
        kernel,
        grid=(heads,),
        in_specs=[
            spec(0),
            spec(1),
            spec(2),
            pl.BlockSpec((1, HEAD_DIM, length), lambda h: (0, h, 0)),
            pl.BlockSpec((groups, HEAD_DIM, tokens), lambda h: (0, h, 0)),
            pl.BlockSpec((1, length, length), lambda h: (h, 0, 0)),
            pl.BlockSpec((1, 1, length), lambda h: (h, 0, 0)),
        ],
        out_specs=pl.BlockSpec((groups, 3, HEAD_DIM, tokens), lambda h: (0, 0, h, 0)),
        out_shape=jax.ShapeDtypeStruct((groups, 3, own, tokens), BF16),
        compiler_params=params(),
        cost_estimate=estimate(
            flops=32 * heads * length * length * HEAD_DIM,
            bytes_accessed=2 * heads * length * length,
            transcendentals=0,
        ),
        name="self_backward",
    )(projected, projected, projected, mixed, grads, prob, weight)


def body(
    dec_input,
    enc_output,
    lengths,
    gains,
    self_qkv,
    self_out,
    cross_q,
    cross_kv,
    cross_out,
    ffn_in,
    ffn_out,
    cotangent,
):
    seg, seqs, width = dec_input.shape
    heads = width // HEAD_DIM
    blocks = lax.axis_size("blk")
    place = lax.axis_index("blk")
    groups = blocks // seqs
    mine = place // groups
    slot_of = lax.rem(place, groups)
    members = [[s * groups + g for g in range(groups)] for s in range(seqs)]
    own_heads = -(-heads // groups)
    own = own_heads * HEAD_DIM
    padded = own * groups
    tokens = seqs * seg
    length = groups * tokens
    enc_rows = enc_output.shape[1]
    columns = lax.axis_size("dp")
    gain_rows = gains.astype(F32)[:, None, :]

    def shifted(step):
        return [(b, (b + step * groups) % blocks) for b in range(blocks)]

    def exchange(pieces):
        parts = [pieces(mine)]
        for step in range(1, seqs):
            parts.append(lax.ppermute(pieces(lax.rem(mine + step, seqs)), "blk", shifted(step)))
        return parts

    def in_order(parts):
        ordered = []
        for s in range(seqs):
            choice = parts[0]
            for step in range(1, seqs):
                from_there = lax.rem(mine - step + seqs, seqs) == s
                choice = jnp.where(from_there, parts[step], choice)
            ordered.append(choice)
        return ordered

    def spread(array):
        return lax.all_to_all(
            jnp.broadcast_to(array[None], (groups,) + array.shape),
            "blk",
            0,
            0,
            axis_index_groups=members,
        )

    def traded(array):
        return lax.all_to_all(array, "blk", 0, 0, axis_index_groups=members)

    def gathered(array):
        by_query = lax.optimization_barrier(array.swapaxes(0, 1))
        take = lambda s: lax.dynamic_index_in_dim(by_query, s, 0, False)
        return jnp.concatenate(in_order(exchange(take)), axis=0)

    def leaving(array):
        split = array.reshape(seqs, seg, width)
        return exchange(lambda s: lax.dynamic_index_in_dim(split, s, 0, False))

    def returned(parts):
        return jnp.stack(in_order(parts), axis=1)

    own_inputs = gathered(dec_input)
    all_inputs = spread(own_inputs).reshape(length, width)

    pick = lambda s: lax.dynamic_index_in_dim(enc_output, s, 0, False)
    cuts = [max(enc_rows * 3 // 7 // 128 * 128, 128)]
    cuts.append(cuts[0] + 128)
    spans = [(0, 0, enc_rows)]
    arrived = []
    for step in range(1, seqs):
        sent = pick(lax.rem(mine + step, seqs))
        arrived.append([lax.ppermute(sent[: cuts[0]], "blk", shifted(step))])
        spans += [(step, 0, cuts[0]), (step, cuts[0], enc_rows)]
        for start, stop in ((cuts[0], cuts[1]), (cuts[1], enc_rows)):
            piece, unused = lax.optimization_barrier((sent[start:stop], arrived[-1][-1]))
            arrived[-1].append(lax.ppermute(piece, "blk", shifted(step)))
    own_rows_low = pick(mine)
    turned_kv = cross_kv.swapaxes(1, 2)
    first_pair = project_rows([own_rows_low], turned_kv)
    all_inputs, first_pair, firsts = lax.optimization_barrier(
        (all_inputs, first_pair, [a[0] for a in arrived])
    )

    row_lengths = lax.dynamic_index_in_dim(lengths, mine, 0, False)
    bias = []
    for step, start, stop in spans:
        source = lax.rem(place - step * groups + blocks, blocks)
        slot = source * enc_rows + jnp.arange(start, stop)
        match = (slot // SLOTS)[:, None] == jnp.arange(lengths.shape[1])[None, :]
        filled = jnp.sum(jnp.where(match, row_lengths[None, :], 0), axis=-1)
        row = jnp.where((slot % SLOTS) < filled, 0.0, negative_fill).astype(BF16)
        bias.append(jnp.concatenate([row[None], jnp.zeros((15, stop - start), BF16)], axis=0))

    extra = [(0, 0), (0, 0), (0, padded - width)]
    padded_qkv = jnp.pad(self_qkv, extra)
    own_qkv = lax.dynamic_slice_in_dim(padded_qkv, slot_of * own, own, 2).swapaxes(1, 2)
    padded_out = jnp.pad(self_out, [(0, padded - width), (0, 0)])
    index = jnp.arange(length)
    block = index // seg
    position = ((block % seqs) * groups + block // seqs) * seg + index % seg
    position = position.astype(jnp.int32)
    first_low, projected, sent_mix, self_prob, self_weight = self_forward(
        all_inputs,
        gain_rows[0],
        own_qkv,
        position[:, None],
        position[None, :],
        groups,
    )
    sent_mix, seconds = lax.optimization_barrier((sent_mix, [a[1] for a in arrived]))
    self_mix = traded(sent_mix).reshape(padded, length)
    slot = jnp.full((1,), slot_of, jnp.int32)
    cross_query, after_self, second_low = query_stage(
        all_inputs, self_mix, padded_out, gain_rows[1], cross_q.T, slot, groups
    )

    cross_query, thirds = lax.optimization_barrier((cross_query, [a[2] for a in arrived]))
    encoded = [own_rows_low]
    pairs = [first_pair]
    for first, second, third in zip(firsts, seconds, thirds):
        pairs.append(project_rows([first], turned_kv))
        pairs.append(project_rows([second, third], turned_kv))
        encoded += [first, jnp.concatenate([second, third], axis=0)]

    def own_rows(array):
        return lax.dynamic_slice_in_dim(array, slot_of * tokens, tokens, 0)

    own_self_mix = lax.dynamic_slice_in_dim(self_mix, slot_of * tokens, tokens, 1)

    part_mix, cross_prob, local_top = cross_forward(cross_query, pairs, bias, width, groups)
    stat_rows = (part_mix.shape[1] - width) // 2

    own_cotangent = gathered(cotangent)
    (
        own_output,
        cross_grad,
        cross_grad_low,
        third_low,
        hidden_low,
        pre_low,
        cross_mix,
        payload,
        gain_three,
    ) = token_stage(
        traded(part_mix),
        after_self,
        cross_out,
        gain_rows[2],
        ffn_in,
        ffn_out,
        own_cotangent,
        groups,
    )
    packed = traded(payload)

    def by_rows(grad):
        return grad.astype(BF16).reshape(blocks, columns, -1, grad.shape[-1]).swapaxes(0, 1)

    def placed(rows, counts):
        count, full = rows.shape
        split = rows.reshape(count, columns, full // columns).swapaxes(0, 1)
        moved = lax.all_to_all(split, "dp", 0, 0).astype(F32)
        ends = [sum(counts[: i + 1]) for i in range(len(counts) - 1)]
        return [p.reshape(-1, full // columns) for p in jnp.split(moved, ends, axis=1)]

    cross_out_chunks = by_rows(dot(cross_mix, cross_grad_low, 1, 0))
    unit = width // blocks // columns
    staged = (
        padded == width
        and columns * own == width
        and columns * seqs == blocks
        and ffn_in.shape[1] == columns * width
        and width % (ffn_in.shape[1] // blocks) == 0
    )
    if staged:
        in_chunks, out_chunks = hidden_weight_grads(
            third_low, pre_low, hidden_low, own_cotangent, columns, blocks
        )
        chunks = jnp.concatenate([in_chunks, out_chunks], axis=2)
        packed, chunks, own_output = lax.optimization_barrier((packed, chunks, own_output))
        inner = chunks.shape[1:]
        hidden = lax.psum_scatter(
            chunks.reshape(-1, width), "dp", scatter_dimension=0, tiled=True
        )
    else:
        in_chunks = dot(third_low, pre_low, 0, 0).astype(BF16)
        in_chunks = in_chunks.reshape(blocks, width // blocks, columns, -1).transpose(2, 0, 1, 3)
        out_chunks = by_rows(dot(hidden_low, own_cotangent, 0, 0))
    output_parts = leaving(own_output)

    def whole_rows(start):
        rows = packed[:, start : start + 2 * stat_rows].astype(F32)
        rows = (rows[:, :stat_rows] + rows[:, stat_rows:])[:, :heads]
        return rows.transpose(1, 0, 2).reshape(heads, 1, length)

    scale = jnp.exp(local_top - whole_rows(width))
    query_parts, key_low, value_low = cross_backward(
        cross_query,
        pairs,
        cross_prob,
        packed,
        scale,
        whole_rows(width + 2 * stat_rows) * scale,
        width,
        groups,
    )
    query_parts, output_parts = lax.optimization_barrier((query_parts, output_parts))
    joined = traded(query_parts)
    enc_parts = [
        (dot(k, cross_kv[0], 1, 1) + dot(v, cross_kv[1], 1, 1)).astype(BF16)
        for k, v in zip(key_low, value_low)
    ]
    shares = [0, 4, 6, 8, 14]
    marks = [enc_rows * share // 14 // 16 * 16 for share in shares]
    enc_rest = [
        jnp.concatenate(enc_parts[2 * step - 1 : 2 * step + 1], axis=0) for step in range(1, seqs)
    ]
    enc_back = [[] for _ in enc_rest]

    def send_back(number):
        for step, rest in enumerate(enc_rest, 1):
            piece = rest[marks[number] : marks[number + 1]]
            if number:
                piece, unused = lax.optimization_barrier((piece, enc_back[step - 1][-1]))
            moved = lax.ppermute(piece, "blk", [(b, a) for a, b in shifted(step)])
            enc_back[step - 1].append(moved)

    def wait_back(value):
        value, last = lax.optimization_barrier((value, [back[-1] for back in enc_back]))
        for back, piece in zip(enc_back, last):
            back[-1] = piece
        return value

    send_back(0)
    key_chunks = by_rows(sum(dot(e, g, 0, 0) for e, g in zip(encoded, key_low)))
    value_chunks = by_rows(sum(dot(e, g, 0, 0) for e, g in zip(encoded, value_low)))
    if staged:
        firsts = Halving(jnp.concatenate([key_chunks, value_chunks], axis=2))
        joined, firsts.array, hidden = lax.optimization_barrier((joined, firsts.array, hidden))
    joined = wait_back(joined)
    send_back(1)
    if staged:
        hidden = lax.psum_scatter(hidden, "blk", scatter_dimension=0, tiled=True)
        firsts.send("dp", 0)

    query_grad, self_grad, self_grad_low, mixed_grad, gain_two = mixed_stage(
        joined, cross_q, after_self, gain_rows[1], cross_grad, padded_out, groups, own
    )
    own_mixed = traded(mixed_grad)
    cross_q_chunks = by_rows(dot(second_low, query_grad, 0, 1))
    self_out_chunks = by_rows(dot(own_self_mix[:width], self_grad_low, 1, 0))
    own_mixed, cross_q_chunks, self_out_chunks = wait_back(
        (own_mixed, cross_q_chunks, self_out_chunks)
    )
    send_back(2)
    if staged:
        seconds = Halving(
            jnp.concatenate([cross_out_chunks, cross_q_chunks, self_out_chunks], axis=2)
        )
        own_mixed = after(own_mixed, firsts)
        firsts.send("dp", 0)
        seconds.send("dp", 0)
    own_grads = self_backward(projected, sent_mix, own_mixed, self_prob, self_weight, groups)
    own_grads = wait_back(own_grads)
    if staged:
        own_grads = after(own_grads, firsts, seconds)
    send_back(3)
    back = traded(own_grads)
    if staged:
        firsts.array = jnp.squeeze(firsts.array, 0)
        firsts.send("blk", 0)
        seconds.send("dp", 0)
        part, gain_one = own_weight_grads(first_low, all_inputs, own_grads, own_qkv, blocks)
        back, part, gain_one = wait_back((back, part, gain_one))
        back = after(back, firsts, seconds)
        part = halved(part.reshape((columns, seqs) + part.shape[1:]), "dp", 0)
        seconds.array = jnp.squeeze(seconds.array, 0)
        seconds.send("blk", 0)
    own_grad = input_stage(
        back, padded_qkv, own_rows(all_inputs), gain_rows[0], self_grad, groups
    )
    if not staged:
        own_first = own_rows(first_low)
        full = back.transpose(1, 0, 2, 3).reshape(3, padded, tokens)[:, :width]
        first_back = sum(dot(full[c], self_qkv[c], 0, 1) for c in range(3))
        unused, gain_one = pulled_norm(
            own_rows(all_inputs).astype(F32), gain_rows[0], first_back
        )
        part = jnp.concatenate([by_rows(dot(own_first, full[c], 0, 1)) for c in range(3)], axis=2)
    gain_grads = total_of(jnp.concatenate([gain_one, gain_two, gain_three], axis=0))
    dec_grad = returned(leaving(own_grad))
    output = returned(output_parts)
    if seqs == 2:
        enc_grad = both_queries(enc_parts[0], enc_back[0], jnp.full((1,), mine, jnp.int32))
    else:
        enc_back = [enc_parts[0]] + [jnp.concatenate(pieces, axis=0) for pieces in enc_back]
        enc_grad = []
        for s in range(seqs):
            choice = enc_back[0]
            for step in range(1, seqs):
                choice = jnp.where(lax.rem(mine + step, seqs) == s, enc_back[step], choice)
            enc_grad.append(choice)
        enc_grad = jnp.stack(enc_grad, axis=0)

    if staged:
        seconds.take()
        rest = jnp.concatenate([firsts.array, seconds.array], axis=1)
        rest = halved(rest, "blk", 0)
        ffn_in_rows = hidden[: width // blocks]
        placed_rows = placed(
            jnp.concatenate([hidden[width // blocks :], rest], axis=0),
            [width // blocks] + [unit] * 5,
        )
        ffn_out_own, key_own, value_own, cross_out_own, cross_q_own, self_out_own = placed_rows
        qkv = 0.0
        for step in range(seqs):
            pairs = []
            for b in range(blocks):
                row = (b // groups + step) % seqs
                for d in range(columns):
                    pairs.append((b * columns + d, (d * seqs + row) * columns + b % groups))
            piece = lax.dynamic_index_in_dim(part, lax.rem(mine + step, seqs), 0, False)
            qkv = qkv + lax.ppermute(piece, ("blk", "dp"), pairs).astype(F32)
    else:
        reduced = lambda array: halved(halved(array, "dp", 0), "blk", 0)
        ffn_in_rows = reduced(in_chunks)
        chunks = [out_chunks, cross_out_chunks, key_chunks, value_chunks]
        chunks += [cross_q_chunks, self_out_chunks, part]
        counts = [out_chunks.shape[2]] + [unit] * 8
        rows = placed(reduced(jnp.concatenate(chunks, axis=2)), counts)
        ffn_out_own, cross_out_own, key_own, value_own, cross_q_own, self_out_own = rows[:6]
        qkv = jnp.stack(rows[6:])

    return (
        output,
        dec_grad,
        enc_grad,
        gain_grads,
        qkv,
        self_out_own,
        cross_q_own,
        jnp.stack([key_own, value_own]),
        cross_out_own,
        ffn_in_rows.astype(F32),
        ffn_out_own,
    )


def solution(mesh):
    placed = (
        P("blk", "dp", None),
        P("dp", "blk", None),
        P("dp", None),
        P(),
        P(),
        P(),
        P(),
        P(),
        P(),
        P(),
        P(),
        P("blk", "dp", None),
    )
    return jax.shard_map(
        body,
        mesh=mesh,
        in_specs=placed,
        out_specs=(
            P("blk", "dp", None),
            P("blk", "dp", None),
            P("dp", "blk", None),
            P(),
            P(None, "blk", "dp"),
            P("blk", "dp"),
            P("blk", "dp"),
            P(None, "blk", "dp"),
            P("blk", "dp"),
            P("blk", "dp"),
            P("blk", "dp"),
        ),
        check_vma=False,
    )
```

```python
import functools

import jax
import jax.numpy as jnp
from jax import lax
from jax.experimental import pallas as pl
from jax.experimental.pallas import tpu as pltpu
from jax.sharding import PartitionSpec as P

HEAD_DIM = 64
SLOTS = 448
F32 = jnp.float32
BF16 = jnp.bfloat16
epsilon = 1e-06
negative_fill = -1e30
safe_score = 60.0
VMEM_LIMIT = 60 * 1024 * 1024


def dot(left, right, left_dim, right_dim):
    return lax.dot_general(
        left, right, (((left_dim,), (right_dim,)), ((), ())), preferred_element_type=F32
    )


def split_low(value):
    high = value.astype(BF16)
    return high, (value - high.astype(F32)).astype(BF16)


def normed(values, gain):
    return values * lax.rsqrt(jnp.mean(values * values, axis=-1, keepdims=True) + epsilon) * gain


def parted(array, axis, dim):
    size = lax.axis_size(axis)
    shape = array.shape
    above = size // shape[dim]
    split = array.reshape(shape[:dim] + (shape[dim] // 2, 2) + shape[dim + 1 :])
    bit = lax.rem(lax.axis_index(axis) // above, 2)
    kept = lax.dynamic_index_in_dim(split, bit, dim + 1, False)
    sent = lax.dynamic_index_in_dim(split, 1 - bit, dim + 1, False)
    return kept, sent, [(i, i ^ above) for i in range(size)]


def added(kept, got):
    return (kept.astype(F32) + got.astype(F32)).astype(BF16)


def fold(pairs, bit, low):
    count, _, width = pairs[0][0].shape
    rows = [k.shape[1] for k, _ in pairs]
    high, total = count // 2 // low, sum(rows)

    def kernel(s_ref, *refs):
        start = 0
        for i, size in enumerate(rows):
            for side in range(2):
                kept, got = refs[4 * i + 2 * side], refs[4 * i + 2 * side + 1]
                both = kept[...].astype(F32) + got[...].astype(F32)
                refs[4 * len(rows) + side][:, start : start + size, :] = both.reshape(
                    high * low, size, width
                ).astype(BF16)
            start += size

    def spec(size, side):
        return pl.BlockSpec(
            (high, 1, low, size, width), lambda j, s: (0, (s[0] + side) % 2, 0, 0, 0)
        )

    split = lambda array: array.reshape(high, 2, low, array.shape[1], width)
    out = pl.BlockSpec((high * low, total, width), lambda j, s: (0, 0, 0))
    return pl.pallas_call(
        kernel,
        grid_spec=pltpu.PrefetchScalarGridSpec(
            num_scalar_prefetch=1,
            grid=(1,),
            in_specs=[spec(size, side) for size in rows for side in range(2) for _ in range(2)],
            out_specs=[out] * 2,
        ),
        out_shape=[jax.ShapeDtypeStruct((high * low, total, width), BF16)] * 2,
        compiler_params=params(),
        cost_estimate=estimate(flops=0, bytes_accessed=0, transcendentals=0),
        name="fold",
    )(bit, *[split(array) for k, g in pairs for array in (k, g, k, g)])


def evens(array, bit, sizes):
    count, rows, width = array.shape
    half = count // 2

    def kernel(s_ref, here_ref, there_ref, *out_refs):
        start = 0
        for i, size in enumerate(sizes):
            for side, ref in enumerate((here_ref, there_ref)):
                out_refs[2 * i + side][...] = ref[:, 0, start : start + size]
            start += size

    spec = lambda side: pl.BlockSpec(
        (half, 1, rows, width), lambda j, s: (0, (s[0] + side) % 2, 0, 0)
    )
    out = lambda size: pl.BlockSpec((half, size, width), lambda j, s: (0, 0, 0))
    split = array.reshape(half, 2, rows, width)
    outs = pl.pallas_call(
        kernel,
        grid_spec=pltpu.PrefetchScalarGridSpec(
            num_scalar_prefetch=1,
            grid=(1,),
            in_specs=[spec(0), spec(1)],
            out_specs=[out(size) for size in sizes for _ in range(2)],
        ),
        out_shape=[
            jax.ShapeDtypeStruct((half, size, width), BF16) for size in sizes for _ in range(2)
        ],
        compiler_params=params(),
        cost_estimate=estimate(flops=0, bytes_accessed=0, transcendentals=0),
        name="evens",
    )(bit, split, split)
    return list(zip(outs[::2], outs[1::2]))


def weight_chunks(kernel_dots, operands, specs, core, slot, columns, blocks, width):
    number = len(kernel_dots)
    size, piece = width // blocks, width // columns
    rows = number // 2 * size + number % 2 * size // 2
    shape = (columns // 2 * blocks, rows, 2 * piece)

    def kernel(c_ref, n_ref, *refs):
        kept_ref, sent_ref = refs[-2:]
        grads = [one(refs[:-2]).astype(BF16) for one in kernel_dots]

        def chunk(b, d):
            cut = lambda g, start, stop: g[
                b * size + start : b * size + stop, d * piece : (d + 1) * piece
            ]
            sides = [
                jnp.concatenate([cut(g, 0, size), cut(h, 0, size)], axis=1)
                for g, h in zip(grads[::2], grads[1::2])
            ]
            if number % 2:
                g = grads[-1]
                sides.append(
                    jnp.concatenate([cut(g, 0, size // 2), cut(g, size // 2, size)], axis=1)
                )
            return sides[0] if len(sides) == 1 else jnp.concatenate(sides, axis=0)

        for bit in range(2):

            @pl.when(c_ref[0] == bit)
            def put():
                for b in range(blocks):
                    for d in range(columns):
                        ref = kept_ref if d % 2 == bit else sent_ref
                        ref[d // 2 * blocks + b] = chunk(b, d)

    whole = lambda *shape: pl.BlockSpec(shape, lambda i, c, n: (0,) * len(shape))
    in_specs = [spec or whole(*array.shape) for array, spec in zip(operands, specs)]
    return pl.pallas_call(
        kernel,
        grid_spec=pltpu.PrefetchScalarGridSpec(
            num_scalar_prefetch=2,
            grid=(1,),
            in_specs=in_specs,
            out_specs=[whole(*shape)] * 2,
        ),
        out_shape=[jax.ShapeDtypeStruct(shape, BF16)] * 2,
        compiler_params=params(),
        cost_estimate=estimate(flops=0, bytes_accessed=0, transcendentals=0),
        name="weight_chunks",
    )(core, slot, *operands)


def row_grads(keys, values, weights, marks):
    rows, width = keys.shape
    sizes = [b - a for a, b in zip(marks, marks[1:])]

    def kernel(k_ref, v_ref, w_ref, *out_refs):
        total = dot(k_ref[...], w_ref[0], 1, 1) + dot(v_ref[...], w_ref[1], 1, 1)
        for ref, start, size in zip(out_refs, marks, sizes):
            ref[...] = total[start : start + size].astype(BF16)

    return pl.pallas_call(
        kernel,
        out_shape=[jax.ShapeDtypeStruct((size, width), BF16) for size in sizes],
        compiler_params=params(),
        cost_estimate=estimate(flops=0, bytes_accessed=0, transcendentals=0),
        name="row_grads",
    )(keys, values, weights)


def unpacked(hidden, late, size, piece):
    half = size // 2

    def kernel(hk_ref, hg_ref, lk_ref, lg_ref, in_ref, out_ref, kv_ref, co_ref, cq_ref, so_ref):
        first = hk_ref[...].astype(F32) + hg_ref[...].astype(F32)
        in_ref[...] = jnp.concatenate([first[:size], first[size : 2 * size]], axis=1)
        turned = first[2 * size :].T
        out_ref[...] = jnp.concatenate([turned[:piece], turned[piece:]], axis=1)
        second = lk_ref[...].astype(F32) + lg_ref[...].astype(F32)
        kv_ref[0] = second[:size, :piece]
        kv_ref[1] = second[:size, piece:]
        co_ref[:half, :] = second[size : size + half, :piece]
        co_ref[half:, :] = second[size : size + half, piece:]
        cq_ref[...] = second[size + half :, :piece]
        so_ref[...] = second[size + half :, piece:]

    flat = lambda *shape: jax.ShapeDtypeStruct(shape, F32)
    outs = pl.pallas_call(
        kernel,
        out_shape=[
            flat(size, 4 * piece),
            flat(piece, 4 * size),
            flat(2, size, piece),
            flat(size, piece),
            flat(size, piece),
            flat(size, piece),
        ],
        compiler_params=params(),
        cost_estimate=estimate(flops=0, bytes_accessed=0, transcendentals=0),
        name="unpacked",
    )(*hidden, *late)
    return (outs[0], outs[1].T) + tuple(outs[2:])


def halved(array, axis, dim):
    while array.shape[dim] > 1:
        kept, sent, pairs = parted(array, axis, dim)
        array = added(kept, lax.ppermute(sent, axis, pairs))
    return jnp.squeeze(array, dim)


def total_of(array, axis):
    size = lax.axis_size(axis)
    copies = jnp.broadcast_to(array[None], (size,) + array.shape)
    return jnp.sum(lax.all_to_all(copies, axis, 0, 0), axis=0)


def estimate(flops, bytes_accessed, transcendentals):
    scale = 10**9
    return pl.CostEstimate(
        flops=max(flops // scale, 1),
        bytes_accessed=max(bytes_accessed // scale, 1),
        transcendentals=transcendentals // scale,
    )


def params():
    return pltpu.CompilerParams(vmem_limit_bytes=VMEM_LIMIT)


def cross_forward(query, pairs, bias, width, groups):
    heads = width // HEAD_DIM
    length = query.shape[1]
    tokens = length // groups
    parts = len(pairs)
    rows = [p.shape[2] for p in pairs]
    starts = [sum(rows[:i]) for i in range(parts)]
    total = sum(rows)
    stat_rows = 16 * ((heads + 15) // 16)

    def kernel(*refs):
        q_ref = refs[0]
        k_refs = refs[1 : 1 + parts]
        v_refs = refs[1 + parts : 1 + 2 * parts]
        b_refs = refs[1 + 2 * parts : 1 + 3 * parts]
        o_ref, p_ref, m_ref, lse_ref = refs[1 + 3 * parts :]
        head = pl.program_id(0)
        query = q_ref[...]
        aug_query = jnp.concatenate([query, jnp.ones((16, length), BF16)], axis=0)
        q_norm = jnp.max(jnp.sum(jnp.square(query.astype(F32)), axis=0, keepdims=True))
        k_norm = jnp.float32(0)
        for k_ref in k_refs:
            k_norm = jnp.maximum(
                k_norm, jnp.max(jnp.sum(jnp.square(k_ref[0].astype(F32)), axis=0, keepdims=True))
            )
        small = q_norm * k_norm < safe_score * safe_score

        def score(i):
            return dot(jnp.concatenate([k_refs[i][0], b_refs[i][...]], axis=0), aug_query, 0, 0)

        def finish(probs, top):
            mixed = None
            for i in range(parts):
                aug_value = jnp.concatenate([v_refs[i][0], jnp.ones((16, rows[i]), BF16)], axis=0)
                term = dot(aug_value, probs[i], 1, 0)
                mixed = term if mixed is None else mixed + term
            norm = mixed[HEAD_DIM : HEAD_DIM + 1]
            out = (mixed[:HEAD_DIM] / norm).astype(BF16)
            where = pl.ds(pl.multiple_of(head * HEAD_DIM, HEAD_DIM), HEAD_DIM)
            for g in range(groups):
                o_ref[g, where, :] = out[:, g * tokens : (g + 1) * tokens]
            lse_ref[pl.ds(head, 1), :] = top + jnp.log(norm)
            m_ref[0] = top

        @pl.when(small)
        def plain():
            probs = []
            for i in range(parts):
                prob = jnp.exp(score(i)).astype(BF16)
                p_ref[0, starts[i] : starts[i] + rows[i], :] = prob
                probs.append(prob)
            finish(probs, jnp.zeros((1, length), F32))

        @pl.when(jnp.logical_not(small))
        def shifted():
            raw = [score(i) for i in range(parts)]
            top = jnp.max(raw[0], axis=0, keepdims=True)
            for i in range(1, parts):
                top = jnp.maximum(top, jnp.max(raw[i], axis=0, keepdims=True))
            probs = []
            for i in range(parts):
                prob = jnp.exp(raw[i] - top).astype(BF16)
                p_ref[0, starts[i] : starts[i] + rows[i], :] = prob
                probs.append(prob)
            finish(probs, top)

        @pl.when(head == heads - 1)
        def stats():
            high, low = split_low(lse_ref[...])
            for g in range(groups):
                o_ref[g, width : width + stat_rows, :] = high[:, g * tokens : (g + 1) * tokens]
                o_ref[g, width + stat_rows :, :] = low[:, g * tokens : (g + 1) * tokens]

    payload = width + 2 * stat_rows
    key_specs = [pl.BlockSpec((1, HEAD_DIM, r), lambda h: (0, h, 0)) for r in rows]
    value_specs = [pl.BlockSpec((1, HEAD_DIM, r), lambda h: (1, h, 0)) for r in rows]
    return pl.pallas_call(
        kernel,
        grid=(heads,),
        in_specs=[pl.BlockSpec((HEAD_DIM, length), lambda h: (h, 0))]
        + key_specs
        + value_specs
        + [pl.BlockSpec((16, r), lambda h: (0, 0)) for r in rows],
        out_specs=[
            pl.BlockSpec((groups, payload, tokens), lambda h: (0, 0, 0)),
            pl.BlockSpec((1, total, length), lambda h: (h, 0, 0)),
            pl.BlockSpec((1, 1, length), lambda h: (h, 0, 0)),
        ],
        out_shape=[
            jax.ShapeDtypeStruct((groups, payload, tokens), BF16),
            jax.ShapeDtypeStruct((heads, total, length), BF16),
            jax.ShapeDtypeStruct((heads, 1, length), F32),
        ],
        scratch_shapes=[pltpu.VMEM((stat_rows, length), F32)],
        compiler_params=params(),
        cost_estimate=estimate(
            flops=16 * heads * total * length * HEAD_DIM,
            bytes_accessed=2 * heads * total * length,
            transcendentals=heads * total * length,
        ),
        name="cross_forward",
    )(query, *pairs, *pairs, *bias)


def cross_backward(query, pairs, prob, grads, weight, delta, width, groups):
    heads = width // HEAD_DIM
    length = query.shape[1]
    tokens = length // groups
    parts = len(pairs)
    rows = [p.shape[2] for p in pairs]
    starts = [sum(rows[:i]) for i in range(parts)]
    total = sum(rows)
    pair = 2
    sources = [rows[0], total - rows[0]]
    where = [(0, 0)] + [(1, start - rows[0]) for start in starts[1:]]

    def kernel(*refs):
        q_ref = refs[0]
        k_refs = refs[1 : 1 + parts]
        v_refs = refs[1 + parts : 1 + 2 * parts]
        p_ref, g_ref, w_ref, d_ref = refs[1 + 2 * parts : 5 + 2 * parts]
        dq_ref = refs[5 + 2 * parts]
        dk_refs = refs[6 + 2 * parts : 8 + 2 * parts]
        dv_refs = refs[8 + 2 * parts :]
        key_out = [[] for _ in range(parts)]
        value_out = [[] for _ in range(parts)]
        for j in range(pair):
            at = slice(j * HEAD_DIM, (j + 1) * HEAD_DIM)
            grad = jnp.concatenate([g_ref[g, at, :] for g in range(groups)], axis=1).astype(F32)
            scaled = grad * w_ref[j]
            high, low = split_low(-d_ref[j])
            scaled_low = scaled.astype(BF16)
            pad = jnp.zeros((14, length), BF16)
            aug = jnp.concatenate([scaled_low, high, low, pad], axis=0)
            scaled_rows = scaled.T.astype(BF16)
            query_rows = q_ref[at, :].astype(F32).T.astype(BF16)
            query_grad = None
            for i in range(parts):
                aug_value = jnp.concatenate(
                    [v_refs[i][0, at, :], jnp.ones((16, rows[i]), BF16)], axis=0
                )
                prob = p_ref[j, starts[i] : starts[i] + rows[i], :]
                score = (prob.astype(F32) * dot(aug_value, aug, 0, 0)).astype(BF16)
                value_out[i].append(dot(prob, scaled_rows, 1, 0).astype(BF16))
                key_out[i].append(dot(score, query_rows, 1, 0).astype(BF16))
                term = dot(k_refs[i][0, at, :], score, 1, 0)
                query_grad = term if query_grad is None else query_grad + term
            query_low = (query_grad * 0.125).astype(BF16)
            for g in range(groups):
                dq_ref[g, at, :] = query_low[:, g * tokens : (g + 1) * tokens]
        for i in range(parts):
            source, start = where[i]
            at = slice(start, start + rows[i])
            dk_refs[source][at, :] = jnp.concatenate(key_out[i], axis=1)
            dv_refs[source][at, :] = jnp.concatenate(value_out[i], axis=1)

    size = pair * HEAD_DIM
    key_specs = [pl.BlockSpec((1, size, r), lambda h: (0, h, 0)) for r in rows]
    value_specs = [pl.BlockSpec((1, size, r), lambda h: (1, h, 0)) for r in rows]
    kv_grads = [pl.BlockSpec((r, size), lambda h: (0, h)) for r in sources]
    outs = pl.pallas_call(
        kernel,
        grid=(heads // pair,),
        in_specs=[pl.BlockSpec((size, length), lambda h: (h, 0))]
        + key_specs
        + value_specs
        + [
            pl.BlockSpec((pair, total, length), lambda h: (h, 0, 0)),
            pl.BlockSpec((groups, size, tokens), lambda h: (0, h, 0)),
            pl.BlockSpec((pair, 1, length), lambda h: (h, 0, 0)),
            pl.BlockSpec((pair, 1, length), lambda h: (h, 0, 0)),
        ],
        out_specs=[pl.BlockSpec((groups, size, tokens), lambda h: (0, h, 0))] + kv_grads + kv_grads,
        out_shape=[jax.ShapeDtypeStruct((groups, width, tokens), BF16)]
        + [jax.ShapeDtypeStruct((r, width), BF16) for r in sources] * 2,
        compiler_params=params(),
        cost_estimate=estimate(
            flops=32 * heads * total * length * HEAD_DIM,
            bytes_accessed=2 * heads * total * length,
            transcendentals=0,
        ),
        name="cross_backward",
    )(query, *pairs, *pairs, prob, grads, weight, delta)
    return outs[0], list(outs[1:3]), list(outs[3:5])


def self_forward(inputs, gain, weights, key_pos, query_pos, groups):
    length, width = inputs.shape
    own = weights.shape[1]
    heads = own // HEAD_DIM

    def kernel(x_ref, g_ref, w_ref, kp_ref, qp_ref, a_ref, pr_ref, o_ref, p_ref, n_ref):
        head = pl.program_id(0)

        @pl.when(head == 0)
        def project():
            low = normed(x_ref[...].astype(F32), g_ref[...]).astype(BF16)
            a_ref[...] = low
            for c in range(3):
                pr_ref[c] = dot(w_ref[c], low, 1, 1).astype(BF16)

        at = pl.ds(pl.multiple_of(head * HEAD_DIM, HEAD_DIM), HEAD_DIM)
        raw = dot(pr_ref[1, at, :], pr_ref[0, at, :], 0, 0) * 0.125
        raw = jnp.where(kp_ref[...] <= qp_ref[...], raw, negative_fill)
        top = jnp.max(raw, axis=0, keepdims=True)
        prob = jnp.exp(raw - top).astype(BF16)
        p_ref[0] = prob
        aug_value = jnp.concatenate([pr_ref[2, at, :], jnp.ones((16, length), BF16)], axis=0)
        mixed = dot(aug_value, prob, 1, 0)
        inverse = 1.0 / mixed[HEAD_DIM : HEAD_DIM + 1]
        out = (mixed[:HEAD_DIM] * inverse).astype(BF16)
        for g in range(groups):
            o_ref[g] = out
        n_ref[0] = inverse

    whole = lambda *shape: pl.BlockSpec(shape, lambda h: (0,) * len(shape))
    return pl.pallas_call(
        kernel,
        grid=(heads,),
        in_specs=[
            whole(length, width),
            whole(1, width),
            whole(3, own, width),
            whole(length, 1),
            whole(1, length),
        ],
        out_specs=[
            whole(length, width),
            whole(3, own, length),
            pl.BlockSpec((groups, HEAD_DIM, length), lambda h: (0, h, 0)),
            pl.BlockSpec((1, length, length), lambda h: (h, 0, 0)),
            pl.BlockSpec((1, 1, length), lambda h: (h, 0, 0)),
        ],
        out_shape=[
            jax.ShapeDtypeStruct((length, width), BF16),
            jax.ShapeDtypeStruct((3, own, length), BF16),
            jax.ShapeDtypeStruct((groups, own, length), BF16),
            jax.ShapeDtypeStruct((heads, length, length), BF16),
            jax.ShapeDtypeStruct((heads, 1, length), F32),
        ],
        compiler_params=params(),
        cost_estimate=estimate(
            flops=16 * heads * length * length * HEAD_DIM,
            bytes_accessed=2 * heads * length * length,
            transcendentals=heads * length * length,
        ),
        name="self_forward",
    )(inputs, gain, weights, key_pos, query_pos)


def project_rows(pieces, weights):
    counts = [p.shape[0] for p in pieces]
    total, width = sum(counts), pieces[0].shape[1]

    def kernel(*refs):
        w_ref, out_ref = refs[len(counts) :]
        start = 0
        for e_ref, count in zip(refs, counts):
            out_ref[0, :, start : start + count] = dot(w_ref[0], e_ref[...], 1, 1).astype(BF16)
            start += count

    return pl.pallas_call(
        kernel,
        grid=(2,),
        in_specs=[pl.BlockSpec((count, width), lambda c: (0, 0)) for count in counts]
        + [pl.BlockSpec((1, width, width), lambda c: (c, 0, 0))],
        out_specs=pl.BlockSpec((1, width, total), lambda c: (c, 0, 0)),
        out_shape=jax.ShapeDtypeStruct((2, width, total), BF16),
        compiler_params=params(),
        cost_estimate=estimate(
            flops=4 * total * width * width, bytes_accessed=8 * total * width, transcendentals=0
        ),
        name="project_rows",
    )(*pieces, weights)


def query_stage(inputs, mixed, out_weight, gain, query_weight, slot, groups):
    length, width = inputs.shape
    tokens = length // groups
    rows = mixed.shape[0]

    def kernel(s_ref, x_ref, o_ref, w_ref, g_ref, q_ref, qc_ref, h_ref, a_ref):
        after = x_ref[...].astype(F32) + dot(o_ref[...], w_ref[...], 0, 0)
        low = normed(after, g_ref[...]).astype(BF16)
        scaled = dot(q_ref[...], low, 1, 1).astype(BF16)
        qc_ref[...] = (scaled.astype(F32) * 0.125).astype(BF16)

        @pl.when(pl.program_id(0) == s_ref[0])
        def keep():
            h_ref[...] = after
            a_ref[...] = low

    whole = lambda *shape: pl.BlockSpec(shape, lambda i, s: (0,) * len(shape))
    return pl.pallas_call(
        kernel,
        grid_spec=pltpu.PrefetchScalarGridSpec(
            num_scalar_prefetch=1,
            grid=(groups,),
            in_specs=[
                pl.BlockSpec((tokens, width), lambda i, s: (i, 0)),
                pl.BlockSpec((rows, tokens), lambda i, s: (0, i)),
                whole(rows, width),
                whole(1, width),
                whole(width, width),
            ],
            out_specs=[
                pl.BlockSpec((width, tokens), lambda i, s: (0, i)),
                whole(tokens, width),
                whole(tokens, width),
            ],
        ),
        out_shape=[
            jax.ShapeDtypeStruct((width, length), BF16),
            jax.ShapeDtypeStruct((tokens, width), F32),
            jax.ShapeDtypeStruct((tokens, width), BF16),
        ],
        compiler_params=params(),
        cost_estimate=estimate(
            flops=8 * length * width * width, bytes_accessed=8 * width * width, transcendentals=0
        ),
        name="query_stage",
    )(slot, inputs, mixed, out_weight, gain, query_weight)


def gelu_parts(value):
    root = 0.7978845608028654
    cubic = 0.044715
    square = value * value
    bent = jnp.tanh(root * value * (1.0 + cubic * square))
    half = 0.5 * (1.0 + bent)
    slope = half + 0.5 * value * (1.0 - bent * bent) * root * (1.0 + 3.0 * cubic * square)
    return value * half, slope


def pulled_norm(values, gain, grad):
    inverse = lax.rsqrt(jnp.mean(values * values, axis=-1, keepdims=True) + epsilon)
    scaled = values * inverse
    gain_grad = jnp.sum(grad * scaled, axis=0, keepdims=True)
    weighted = grad * gain
    back = inverse * (weighted - scaled * jnp.mean(weighted * scaled, axis=-1, keepdims=True))
    return back, gain_grad


def token_stage(parts, after_self, cross_out, gain, ffn_in, ffn_out, cotangent, groups):
    tokens, width = after_self.shape
    heads = width // HEAD_DIM
    stat_rows = (parts.shape[1] - width) // 2
    hidden = ffn_in.shape[1]
    piece = 384
    steps = hidden // piece
    payload = width + 4 * stat_rows

    def kernel(
        r_ref, h_ref, co_ref, g_ref, w1_ref, w2_ref, c_ref,
        out_ref, dh_ref, g2_ref, a_ref, z_ref, du_ref, o_ref, pay_ref, gain_ref,
        after_ref, acc_ref, back_ref, lse_ref,
    ):
        step = pl.program_id(0)

        @pl.when(step == 0)
        def join():
            lse = [
                r_ref[g, width : width + stat_rows, :].astype(F32)
                + r_ref[g, width + stat_rows :, :].astype(F32)
                for g in range(groups)
            ]
            top = functools.reduce(jnp.maximum, lse)
            share = [jnp.exp(l - top) for l in lse]
            total = functools.reduce(jnp.add, share)
            lse_ref[...] = top + jnp.log(total)
            share = [s / total for s in share]
            for h in range(heads):
                at = slice(h * HEAD_DIM, (h + 1) * HEAD_DIM)
                mixed = None
                for g in range(groups):
                    term = r_ref[g, at, :].astype(F32) * share[g][h : h + 1]
                    mixed = term if mixed is None else mixed + term
                o_ref[at, :] = mixed.astype(BF16)
            after = h_ref[...] + dot(o_ref[...], co_ref[...], 0, 0)
            after_ref[...] = after
            a_ref[...] = normed(after, g_ref[...]).astype(BF16)
            acc_ref[...] = jnp.zeros_like(acc_ref)
            back_ref[...] = jnp.zeros_like(back_ref)

        pre = dot(a_ref[...], w1_ref[...], 1, 0)
        act, slope = gelu_parts(pre)
        act = act.astype(BF16)
        z_ref[...] = act
        acc_ref[...] += dot(act, w2_ref[...], 1, 0)
        pre_grad = (dot(c_ref[...], w2_ref[...], 1, 1) * slope).astype(BF16)
        du_ref[...] = pre_grad
        back_ref[...] += dot(pre_grad, w1_ref[...], 1, 1)

        @pl.when(step == steps - 1)
        def finish():
            after = after_ref[...]
            out_ref[...] = (after + acc_ref[...]).astype(BF16)
            back, gain_grad = pulled_norm(after, g_ref[...], back_ref[...])
            gain_ref[...] = gain_grad
            grad = c_ref[...].astype(F32) + back
            dh_ref[...] = grad
            low = grad.astype(BF16)
            g2_ref[...] = low
            mix_grad = dot(co_ref[...], low, 1, 1).astype(BF16)
            both = mix_grad.astype(F32) * o_ref[...].astype(F32)
            rows = [
                jnp.sum(both[h * HEAD_DIM : (h + 1) * HEAD_DIM], axis=0, keepdims=True)
                for h in range(heads)
            ]
            rows.append(jnp.zeros((stat_rows - heads, tokens), F32))
            stats = [*split_low(lse_ref[...]), *split_low(jnp.concatenate(rows, axis=0))]
            for g in range(groups):
                pay_ref[g, :width, :] = mix_grad
                for i in range(4):
                    start = width + i * stat_rows
                    pay_ref[g, start : start + stat_rows, :] = stats[i]

    whole = lambda *shape: pl.BlockSpec(shape, lambda i: (0,) * len(shape))
    flat = lambda rows, kind: jax.ShapeDtypeStruct((rows, width), kind)
    return pl.pallas_call(
        kernel,
        grid=(steps,),
        in_specs=[
            whole(*parts.shape),
            whole(tokens, width),
            whole(width, width),
            whole(1, width),
            pl.BlockSpec((width, piece), lambda i: (0, i)),
            pl.BlockSpec((piece, width), lambda i: (i, 0)),
            whole(tokens, width),
        ],
        out_specs=[
            whole(tokens, width),
            whole(tokens, width),
            whole(tokens, width),
            whole(tokens, width),
            pl.BlockSpec((tokens, piece), lambda i: (0, i)),
            pl.BlockSpec((tokens, piece), lambda i: (0, i)),
            whole(width, tokens),
            whole(groups, payload, tokens),
            whole(1, width),
        ],
        out_shape=[
            flat(tokens, BF16),
            flat(tokens, F32),
            flat(tokens, BF16),
            flat(tokens, BF16),
            jax.ShapeDtypeStruct((tokens, hidden), BF16),
            jax.ShapeDtypeStruct((tokens, hidden), BF16),
            jax.ShapeDtypeStruct((width, tokens), BF16),
            jax.ShapeDtypeStruct((groups, payload, tokens), BF16),
            flat(1, F32),
        ],
        scratch_shapes=[pltpu.VMEM((tokens, width), F32)] * 3
        + [pltpu.VMEM((stat_rows, tokens), F32)],
        compiler_params=params(),
        cost_estimate=estimate(
            flops=8 * tokens * width * hidden,
            bytes_accessed=4 * width * hidden,
            transcendentals=tokens * hidden,
        ),
        name="token_stage",
    )(parts, after_self, cross_out, gain, ffn_in, ffn_out, cotangent)


def hidden_weight_grads(low, pre_grad, act, cotangent, columns, blocks):
    tokens, width = low.shape
    hidden = act.shape[1]
    step_size = hidden // blocks
    size, piece = width // blocks, width // columns
    half = step_size // 2

    def kernel(a_ref, du_ref, z_ref, c_ref, out_ref):
        step = pl.program_id(0)
        first = dot(a_ref[...], du_ref[...], 0, 0).astype(BF16)
        for p in range(2):

            @pl.when(lax.rem(step, 2) == p)
            def put():
                for b in range(blocks):
                    out_ref[step // 2, b, p * size : (p + 1) * size, :] = first[
                        b * size : (b + 1) * size
                    ]

        second = dot(z_ref[...], c_ref[...], 0, 0).astype(BF16)
        for d in range(columns):
            at = slice(d * piece, (d + 1) * piece)
            out_ref[d, step, 2 * size :, :] = jnp.concatenate(
                [second[:half, at], second[half:, at]], axis=1
            )

    shape = (columns, blocks, 2 * size + half, 2 * piece)
    whole = lambda *shape: pl.BlockSpec(shape, lambda i: (0,) * len(shape))
    return pl.pallas_call(
        kernel,
        grid=(blocks,),
        in_specs=[
            whole(tokens, width),
            pl.BlockSpec((tokens, step_size), lambda i: (0, i)),
            pl.BlockSpec((tokens, step_size), lambda i: (0, i)),
            whole(tokens, width),
        ],
        out_specs=whole(*shape),
        out_shape=jax.ShapeDtypeStruct(shape, BF16),
        compiler_params=params(),
        cost_estimate=estimate(
            flops=4 * tokens * width * hidden,
            bytes_accessed=4 * width * hidden,
            transcendentals=0,
        ),
        name="hidden_weight_grads",
    )(low, pre_grad, act, cotangent)


def mixed_stage(parts, cross_q, after_self, gain, cross_grad, self_out, groups, own):
    tokens, width = after_self.shape
    rows = self_out.shape[0]

    def kernel(r_ref, q_ref, h_ref, g_ref, dh_ref, w_ref, dq_ref, out_ref, g1_ref, do_ref, gain_ref):
        total = r_ref[0].astype(F32)
        for g in range(1, groups):
            total = total + r_ref[g].astype(F32)
        query_grad = total.astype(BF16)
        dq_ref[...] = query_grad
        back, gain_grad = pulled_norm(h_ref[...], g_ref[...], dot(query_grad, q_ref[...], 0, 1))
        gain_ref[...] = gain_grad
        grad = dh_ref[...] + back
        out_ref[...] = grad
        low = grad.astype(BF16)
        g1_ref[...] = low
        mixed = dot(w_ref[...], low, 1, 1).astype(BF16)
        for g in range(groups):
            do_ref[g] = mixed[g * own : (g + 1) * own]

    return pl.pallas_call(
        kernel,
        out_shape=[
            jax.ShapeDtypeStruct((width, tokens), BF16),
            jax.ShapeDtypeStruct((tokens, width), F32),
            jax.ShapeDtypeStruct((tokens, width), BF16),
            jax.ShapeDtypeStruct((groups, own, tokens), BF16),
            jax.ShapeDtypeStruct((1, width), F32),
        ],
        compiler_params=params(),
        cost_estimate=estimate(
            flops=4 * tokens * width * width, bytes_accessed=8 * width * width, transcendentals=0
        ),
        name="mixed_stage",
    )(parts, cross_q, after_self, gain, cross_grad, self_out)


def input_stage(back, weights, inputs, gain, self_grad, slot, groups):
    own, tokens = back.shape[2:]
    width = inputs.shape[1]
    padded = groups * own

    def kernel(s_ref, b_ref, w_ref, x_ref, g_ref, h_ref, out_ref, acc_ref):
        step = pl.program_id(0)
        grads = jnp.concatenate([b_ref[g, 0] for g in range(groups)], axis=0)
        term = dot(grads, w_ref[0], 0, 1)

        @pl.when(step == 0)
        def first():
            acc_ref[...] = term

        @pl.when(step > 0)
        def more():
            acc_ref[...] += term

        @pl.when(step == 2)
        def last():
            back, unused = pulled_norm(x_ref[...].astype(F32), g_ref[...], acc_ref[...])
            out_ref[...] = (h_ref[...] + back).astype(BF16)

    whole = lambda *shape: pl.BlockSpec(shape, lambda i, s: (0,) * len(shape))
    return pl.pallas_call(
        kernel,
        grid_spec=pltpu.PrefetchScalarGridSpec(
            num_scalar_prefetch=1,
            grid=(3,),
            in_specs=[
                pl.BlockSpec((groups, 1, own, tokens), lambda i, s: (0, i, 0, 0)),
                pl.BlockSpec((1, width, padded), lambda i, s: (i, 0, 0)),
                pl.BlockSpec((tokens, width), lambda i, s: (s[0], 0)),
                whole(1, width),
                whole(tokens, width),
            ],
            out_specs=whole(tokens, width),
            scratch_shapes=[pltpu.VMEM((tokens, width), F32)],
        ),
        out_shape=jax.ShapeDtypeStruct((tokens, width), BF16),
        compiler_params=params(),
        cost_estimate=estimate(
            flops=6 * tokens * width * width, bytes_accessed=6 * width * width, transcendentals=0
        ),
        name="input_stage",
    )(slot, back, weights, inputs, gain, self_grad)


def both_queries(own, pieces, mine):
    rows, width = own.shape

    def kernel(s_ref, own_ref, *refs):
        out_ref = refs[-1]

        @pl.when(pl.program_id(0) == s_ref[0])
        def here():
            out_ref[0] = own_ref[...]

        @pl.when(pl.program_id(0) != s_ref[0])
        def there():
            start = 0
            for ref in refs[:-1]:
                out_ref[0, start : start + ref.shape[0], :] = ref[...]
                start += ref.shape[0]

    whole = lambda *shape: pl.BlockSpec(shape, lambda i, s: (0,) * len(shape))
    return pl.pallas_call(
        kernel,
        grid_spec=pltpu.PrefetchScalarGridSpec(
            num_scalar_prefetch=1,
            grid=(2,),
            in_specs=[whole(*own.shape)] + [whole(*p.shape) for p in pieces],
            out_specs=pl.BlockSpec((1, rows, width), lambda i, s: (i, 0, 0)),
        ),
        out_shape=jax.ShapeDtypeStruct((2, rows, width), own.dtype),
        compiler_params=params(),
        cost_estimate=estimate(flops=0, bytes_accessed=8 * rows * width, transcendentals=0),
        name="both_queries",
    )(mine, own, *pieces)


def own_weight_grads(low, gain, grads, weights, core, columns, blocks):
    length, width = low.shape
    groups, _, own, tokens = grads.shape
    rows = width // blocks
    per = blocks // columns

    def kernel(c_ref, a_ref, g_ref, d_ref, w_ref, kept_ref, sent_ref, gain_ref):
        step = pl.program_id(0)
        grads = jnp.concatenate([d_ref[g, 0] for g in range(groups)], axis=1)
        turned = dot(grads, a_ref[...], 1, 0)
        weight = turned.T.astype(BF16)
        for bit in range(2):

            @pl.when(c_ref[0] == bit)
            def put():
                for b in range(blocks):
                    column = b // per
                    ref = kept_ref if column % 2 == bit else sent_ref
                    ref[column // 2, b % per, 0] = weight[b * rows : (b + 1) * rows]

        term = jnp.sum(turned * w_ref[0].astype(F32), axis=0, keepdims=True) / g_ref[...]

        @pl.when(step == 0)
        def first():
            gain_ref[...] = term

        @pl.when(step > 0)
        def more():
            gain_ref[...] += term

    shape = (columns // 2, per, 3, rows, own)
    whole = lambda *shape: pl.BlockSpec(shape, lambda i, c: (0,) * len(shape))
    part = pl.BlockSpec((columns // 2, per, 1, rows, own), lambda i, c: (0, 0, i, 0, 0))
    return pl.pallas_call(
        kernel,
        grid_spec=pltpu.PrefetchScalarGridSpec(
            num_scalar_prefetch=1,
            grid=(3,),
            in_specs=[
                whole(length, width),
                whole(1, width),
                pl.BlockSpec((groups, 1, own, tokens), lambda i, c: (0, i, 0, 0)),
                pl.BlockSpec((1, own, width), lambda i, c: (i, 0, 0)),
            ],
            out_specs=[part, part, whole(1, width)],
        ),
        out_shape=[jax.ShapeDtypeStruct(shape, BF16)] * 2 + [jax.ShapeDtypeStruct((1, width), F32)],
        compiler_params=params(),
        cost_estimate=estimate(
            flops=12 * length * width * own, bytes_accessed=4 * length * width, transcendentals=0
        ),
        name="own_weight_grads",
    )(core, low, gain, grads, weights)


def self_backward(projected, mixed, grads, prob, weight, groups):
    own, length = projected.shape[1:]
    heads = own // HEAD_DIM
    tokens = length // groups

    def kernel(q_ref, k_ref, v_ref, o_ref, g_ref, p_ref, w_ref, out_ref):
        grad = jnp.concatenate([g_ref[g] for g in range(groups)], axis=1).astype(F32)
        scaled = grad * w_ref[0]
        high, low = split_low(-jnp.sum(scaled * o_ref[0].astype(F32), axis=0, keepdims=True))
        scaled_low = scaled.astype(BF16)
        aug = jnp.concatenate([scaled_low, high, low, jnp.zeros((14, length), BF16)], axis=0)
        aug_value = jnp.concatenate([v_ref[0], jnp.ones((16, length), BF16)], axis=0)
        prob = p_ref[0]
        score = (prob.astype(F32) * dot(aug_value, aug, 0, 0)).astype(BF16)
        results = (
            dot(k_ref[0], score, 1, 0) * 0.125,
            dot(q_ref[0], score, 1, 1) * 0.125,
            dot(scaled_low, prob, 1, 1),
        )
        for c in range(3):
            result = results[c].astype(BF16)
            for g in range(groups):
                out_ref[g, c] = result[:, g * tokens : (g + 1) * tokens]

    spec = lambda c: pl.BlockSpec((1, HEAD_DIM, length), lambda h: (c, h, 0))
    return pl.pallas_call(
        kernel,
        grid=(heads,),
        in_specs=[
            spec(0),
            spec(1),
            spec(2),
            pl.BlockSpec((1, HEAD_DIM, length), lambda h: (0, h, 0)),
            pl.BlockSpec((groups, HEAD_DIM, tokens), lambda h: (0, h, 0)),
            pl.BlockSpec((1, length, length), lambda h: (h, 0, 0)),
            pl.BlockSpec((1, 1, length), lambda h: (h, 0, 0)),
        ],
        out_specs=pl.BlockSpec((groups, 3, HEAD_DIM, tokens), lambda h: (0, 0, h, 0)),
        out_shape=jax.ShapeDtypeStruct((groups, 3, own, tokens), BF16),
        compiler_params=params(),
        cost_estimate=estimate(
            flops=32 * heads * length * length * HEAD_DIM,
            bytes_accessed=2 * heads * length * length,
            transcendentals=0,
        ),
        name="self_backward",
    )(projected, projected, projected, mixed, grads, prob, weight)


def body(
    dec_input,
    enc_output,
    lengths,
    gains,
    self_qkv,
    self_out,
    cross_q,
    cross_kv,
    cross_out,
    ffn_in,
    ffn_out,
    cotangent,
):
    seg, seqs, width = dec_input.shape
    heads = width // HEAD_DIM
    blocks = lax.axis_size("blk")
    place = lax.axis_index("blk")
    groups = blocks // seqs
    mine = place // groups
    slot_of = lax.rem(place, groups)
    members = [[s * groups + g for g in range(groups)] for s in range(seqs)]
    own_heads = -(-heads // groups)
    own = own_heads * HEAD_DIM
    padded = own * groups
    tokens = seqs * seg
    length = groups * tokens
    enc_rows = enc_output.shape[1]
    columns = lax.axis_size("dp")
    gain_rows = gains.astype(F32)[:, None, :]

    def shifted(step):
        return [(b, (b + step * groups) % blocks) for b in range(blocks)]

    def exchange(pieces):
        parts = [pieces(mine)]
        for step in range(1, seqs):
            parts.append(lax.ppermute(pieces(lax.rem(mine + step, seqs)), "blk", shifted(step)))
        return parts

    def in_order(parts):
        ordered = []
        for s in range(seqs):
            choice = parts[0]
            for step in range(1, seqs):
                from_there = lax.rem(mine - step + seqs, seqs) == s
                choice = jnp.where(from_there, parts[step], choice)
            ordered.append(choice)
        return ordered

    def spread(array):
        return lax.all_to_all(
            jnp.broadcast_to(array[None], (groups,) + array.shape),
            "blk",
            0,
            0,
            axis_index_groups=members,
        )

    def traded(array):
        return lax.all_to_all(array, "blk", 0, 0, axis_index_groups=members)

    def gathered(array):
        by_query = lax.optimization_barrier(array.swapaxes(0, 1))
        take = lambda s: lax.dynamic_index_in_dim(by_query, s, 0, False)
        return jnp.concatenate(in_order(exchange(take)), axis=0)

    def leaving(array):
        split = array.reshape(seqs, seg, width)
        return exchange(lambda s: lax.dynamic_index_in_dim(split, s, 0, False))

    def returned(parts):
        return jnp.stack(in_order(parts), axis=1)

    own_inputs = gathered(dec_input)
    all_inputs = spread(own_inputs).reshape(length, width)

    pick = lambda s: lax.dynamic_index_in_dim(enc_output, s, 0, False)
    cuts = [max(enc_rows * 3 // 7 // 128 * 128, 128)]
    cuts.append(cuts[0] + 128)
    spans = [(0, 0, enc_rows)]
    arrived = []
    for step in range(1, seqs):
        sent = pick(lax.rem(mine + step, seqs))
        arrived.append([lax.ppermute(sent[: cuts[0]], "blk", shifted(step))])
        spans += [(step, 0, cuts[0]), (step, cuts[0], enc_rows)]
        for start, stop in ((cuts[0], cuts[1]), (cuts[1], enc_rows)):
            piece, unused = lax.optimization_barrier((sent[start:stop], arrived[-1][-1]))
            arrived[-1].append(lax.ppermute(piece, "blk", shifted(step)))
    own_rows_low = pick(mine)
    turned_kv = cross_kv.swapaxes(1, 2)
    first_pair = project_rows([own_rows_low], turned_kv)
    all_inputs, first_pair, firsts = lax.optimization_barrier(
        (all_inputs, first_pair, [a[0] for a in arrived])
    )

    row_lengths = lax.dynamic_index_in_dim(lengths, mine, 0, False)
    bias = []
    for step, start, stop in spans:
        source = lax.rem(place - step * groups + blocks, blocks)
        slot = source * enc_rows + jnp.arange(start, stop)
        match = (slot // SLOTS)[:, None] == jnp.arange(lengths.shape[1])[None, :]
        filled = jnp.sum(jnp.where(match, row_lengths[None, :], 0), axis=-1)
        row = jnp.where((slot % SLOTS) < filled, 0.0, negative_fill).astype(BF16)
        bias.append(jnp.concatenate([row[None], jnp.zeros((15, stop - start), BF16)], axis=0))

    extra = [(0, 0), (0, 0), (0, padded - width)]
    padded_qkv = jnp.pad(self_qkv, extra)
    own_qkv = lax.dynamic_slice_in_dim(padded_qkv, slot_of * own, own, 2).swapaxes(1, 2)
    padded_out = jnp.pad(self_out, [(0, padded - width), (0, 0)])
    index = jnp.arange(length)
    block = index // seg
    position = ((block % seqs) * groups + block // seqs) * seg + index % seg
    position = position.astype(jnp.int32)
    first_low, projected, sent_mix, self_prob, self_weight = self_forward(
        all_inputs,
        gain_rows[0],
        own_qkv,
        position[:, None],
        position[None, :],
        groups,
    )
    sent_mix, seconds = lax.optimization_barrier((sent_mix, [a[1] for a in arrived]))
    self_mix = traded(sent_mix).reshape(padded, length)
    slot = jnp.full((1,), slot_of, jnp.int32)
    cross_query, after_self, second_low = query_stage(
        all_inputs, self_mix, padded_out, gain_rows[1], cross_q.T, slot, groups
    )

    cross_query, thirds = lax.optimization_barrier((cross_query, [a[2] for a in arrived]))
    pairs = [first_pair]
    came = []
    for first, second, third in zip(firsts, seconds, thirds):
        pairs.append(project_rows([first], turned_kv))
        pairs.append(project_rows([second, third], turned_kv))
        came += [first, second, third]

    part_mix, cross_prob, local_top = cross_forward(cross_query, pairs, bias, width, groups)
    stat_rows = (part_mix.shape[1] - width) // 2

    own_cotangent = gathered(cotangent)
    (
        own_output,
        cross_grad,
        cross_grad_low,
        third_low,
        hidden_low,
        pre_low,
        cross_mix,
        payload,
        gain_three,
    ) = token_stage(
        traded(part_mix),
        after_self,
        cross_out,
        gain_rows[2],
        ffn_in,
        ffn_out,
        own_cotangent,
        groups,
    )
    packed = traded(payload)

    def by_rows(grad):
        return grad.astype(BF16).reshape(blocks, columns, -1, grad.shape[-1]).swapaxes(0, 1)

    def placed(rows, counts):
        count, full = rows.shape
        split = rows.reshape(count, columns, full // columns).swapaxes(0, 1)
        moved = lax.all_to_all(split, "dp", 0, 0).astype(F32)
        ends = [sum(counts[: i + 1]) for i in range(len(counts) - 1)]
        return [p.reshape(-1, full // columns) for p in jnp.split(moved, ends, axis=1)]

    unit = width // blocks // columns
    staged = (
        padded == width
        and columns * own == width
        and columns * seqs == blocks
        and columns % 2 == 0
        and ffn_in.shape[1] == columns * width
        and ffn_in.shape[1] // blocks * columns == 2 * width
        and blocks == 8
    )
    if staged:
        chunks = hidden_weight_grads(
            third_low, pre_low, hidden_low, own_cotangent, columns, blocks
        )
        packed, chunks, own_output = lax.optimization_barrier((packed, chunks, own_output))
        inner = chunks.shape[2:]
        hidden = lax.psum_scatter(
            chunks.reshape(-1, inner[1]), "dp", scatter_dimension=0, tiled=True
        )
    else:
        in_chunks = dot(third_low, pre_low, 0, 0).astype(BF16)
        in_chunks = in_chunks.reshape(blocks, width // blocks, columns, -1).transpose(2, 0, 1, 3)
        out_chunks = by_rows(dot(hidden_low, own_cotangent, 0, 0))
    output_parts = leaving(own_output)

    def whole_rows(start):
        rows = packed[:, start : start + 2 * stat_rows].astype(F32)
        rows = (rows[:, :stat_rows] + rows[:, stat_rows:])[:, :heads]
        return rows.transpose(1, 0, 2).reshape(heads, 1, length)

    scale = jnp.exp(local_top - whole_rows(width))
    query_parts, key_low, value_low = cross_backward(
        cross_query,
        pairs,
        cross_prob,
        packed,
        scale,
        whole_rows(width + 2 * stat_rows) * scale,
        width,
        groups,
    )
    query_parts, output_parts = lax.optimization_barrier((query_parts, output_parts))
    joined = traded(query_parts)
    shares = [0, 7, 11, 15, 22, 28]
    marks = [enc_rows * share // 28 for share in shares]
    pieces = row_grads(key_low[1], value_low[1], cross_kv, marks)
    here = jnp.full((1,), mine, jnp.int32)
    together = lambda *values: lax.optimization_barrier(values)

    def sent_back(piece):
        return lax.ppermute(piece, "blk", shifted(1))

    def moved(array, axis, step):
        size = lax.axis_size(axis)
        return lax.ppermute(array, axis, [(i, i ^ step) for i in range(size)])

    def bit_of(axis, step):
        return jnp.full((1,), lax.rem(lax.axis_index(axis) // step, 2), jnp.int32)

    def chunks_of(kernel_dots, operands, specs):
        return weight_chunks(
            kernel_dots, operands, specs, bit_of("dp", 1), slot, columns, blocks, width
        )

    back_1 = sent_back(pieces[0])
    output = returned(output_parts)
    if staged:
        cuts = [0]
        for piece in came:
            cuts.append(cuts[-1] + piece.shape[0])

        def rows_dot(grad):
            def one(refs):
                total = dot(refs[0][...], refs[grad][...], 0, 0)
                for i, (start, stop) in enumerate(zip(cuts, cuts[1:])):
                    total += dot(refs[1 + i][...], refs[grad + 1][start:stop, :], 0, 0)
                return total

            return one

        count = 1 + len(came)
        operands = [own_rows_low, *came, *key_low, *value_low, cross_mix, cross_grad_low]
        kept_1, sent_1 = chunks_of(
            [
                rows_dot(count),
                rows_dot(count + 2),
                lambda refs: dot(refs[count + 4][...], refs[count + 5][...], 1, 0),
            ],
            operands,
            [None] * len(operands),
        )
        joined, pieces, back_1, output, hidden, kept_1, sent_1 = together(
            joined, pieces, back_1, output, hidden, kept_1, sent_1
        )
        got_1 = moved(sent_1, "dp", 1)
    query_grad, self_grad, self_grad_low, mixed_grad, gain_two = mixed_stage(
        joined, cross_q, after_self, gain_rows[1], cross_grad, padded_out, groups, own
    )
    if staged:
        (
            query_grad, self_grad, self_grad_low, mixed_grad, gain_two, kept_1, got_1, pieces, hidden,
        ) = together(
            query_grad, self_grad, self_grad_low, mixed_grad, gain_two, kept_1, got_1, pieces, hidden,
        )
    own_mixed = traded(mixed_grad)
    if staged:
        back_2 = sent_back(pieces[1])
        shares = [inner[0] // 3, inner[0] * 5 // 12, inner[0] // 4]
        (kept_i, sent_i), (kept_o, sent_o), (kept_u, sent_u) = evens(
            hidden.reshape((blocks,) + inner), bit_of("blk", 1), shares
        )
        got_i = moved(sent_i, "blk", 1)
        kept_1, sent_1 = fold([(kept_1, got_1)], bit_of("dp", 2), blocks)
        operands = [second_low, query_grad, self_mix, self_grad_low]
        specs = [None] * 2
        specs += [pl.BlockSpec((width, tokens), lambda i, c, n: (0, n[0])), None]
        kept_2, sent_2 = chunks_of(
            [
                lambda refs: dot(refs[0][...], refs[1][...], 0, 1),
                lambda refs: dot(refs[2][...], refs[3][...], 1, 0),
            ],
            operands,
            specs,
        )
        (
            own_mixed, back_2, kept_i, got_i, kept_o, sent_o, kept_1, sent_1, kept_2, sent_2, pieces,
            kept_u, sent_u,
        ) = together(
            own_mixed, back_2, kept_i, got_i, kept_o, sent_o, kept_1, sent_1, kept_2, sent_2, pieces,
            kept_u, sent_u,
        )
        got_o = moved(sent_o, "blk", 1)
        got_1 = moved(sent_1, "dp", 2)
        got_2 = moved(sent_2, "dp", 1)
        back_3 = sent_back(pieces[2])
    own_grads = self_backward(projected, sent_mix, own_mixed, self_prob, self_weight, groups)
    if staged:
        own_grads, kept_o, got_o, kept_2, got_2, pieces, back_3, sent_u = together(
            own_grads, kept_o, got_o, kept_2, got_2, pieces, back_3, sent_u
        )
    back = traded(own_grads)
    if staged:
        back_4 = sent_back(pieces[3])
        kept_2, sent_2 = fold([(kept_2, got_2)], bit_of("dp", 2), blocks)
        got_2 = moved(sent_2, "dp", 2)
        got_u = moved(sent_u, "blk", 1)
        kept_w, sent_w, gain_one = own_weight_grads(
            first_low, gain_rows[0], own_grads, own_qkv, bit_of("dp", 1), columns, blocks
        )
        gains = jnp.concatenate([gain_one, gain_two, gain_three], axis=0)
        (
            back, back_4, kept_1, got_1, kept_2, got_2, kept_u, got_u, kept_w, sent_w, gains, pieces,
        ) = together(
            back, back_4, kept_1, got_1, kept_2, got_2, kept_u, got_u, kept_w, sent_w, gains, pieces,
        )
    own_grad = input_stage(back, padded_qkv, all_inputs, gain_rows[0], self_grad, slot, groups)
    if staged:
        back_5 = sent_back(pieces[4])
        got_w = moved(sent_w, "dp", 1)
        kept_j, sent_j = fold([(kept_1, got_1), (kept_2, got_2)], bit_of("blk", 1), 1)
        got_j = moved(sent_j, "blk", 1)
        kept_h, sent_h = fold(
            [(kept_i, got_i), (kept_o, got_o), (kept_u, got_u)], bit_of("blk", 2), 1
        )
        got_h = moved(sent_h, "blk", 2)
        gains = gains + moved(gains, "dp", 1)
        own_grad, back_5, kept_w, got_w, kept_j, got_j, kept_h, got_h, gains, pieces, key_low = (
            together(
                own_grad, back_5, kept_w, got_w, kept_j, got_j, kept_h, got_h, gains, pieces, key_low
            )
        )
    dec_parts = leaving(own_grad)
    if staged:
        kept_h, sent_h = fold([(kept_h, got_h)], bit_of("blk", 4), 1)
        got_h = moved(sent_h, "blk", 4)
        flat = (columns // 2, -1, own)
        kept_w, sent_w = fold([(kept_w.reshape(flat), got_w.reshape(flat))], bit_of("dp", 2), 1)
        got_w = moved(sent_w, "dp", 2)
        kept_j, sent_j = fold([(kept_j, got_j)], bit_of("blk", 2), 1)
        got_j = moved(sent_j, "blk", 2)
        gains = gains + moved(gains, "dp", 2)
        dec_parts, kept_w, got_w, kept_j, got_j, gains, key_low, kept_h, got_h = together(
            dec_parts, kept_w, got_w, kept_j, got_j, gains, key_low, kept_h, got_h
        )
        (enc_own,) = row_grads(key_low[0], value_low[0], cross_kv, [0, enc_rows])
        flat = (seqs, -1, own)
        halves = fold([(kept_w.reshape(flat), got_w.reshape(flat))], here, 1)
        got_w = []
        for step, piece in enumerate(halves):
            pairs = []
            for b in range(blocks):
                row = (b // groups + step) % seqs
                for d in range(columns):
                    pairs.append((b * columns + d, (d * seqs + row) * columns + b % groups))
            piece = piece.reshape(3, width // blocks, own)
            got_w.append(lax.ppermute(piece, ("blk", "dp"), pairs))
        kept_j, sent_j = fold([(kept_j, got_j)], bit_of("blk", 4), 1)
        got_j = moved(sent_j, "blk", 4)
        dec_grad = returned(dec_parts)
        gains = gains + moved(gains, "blk", 1)
        kept_j, got_j, dec_grad, gains, enc_own = together(
            kept_j, got_j, dec_grad, gains, enc_own
        )
        enc_grad = both_queries(enc_own, [back_1, back_2, back_3, back_4, back_5], here)
        qkv = sum(piece.astype(F32) for piece in got_w)
        gains = gains + moved(gains, "blk", 2)
        gain_grads = gains + moved(gains, "blk", 4)
        ffn_in_own, ffn_out_own, kv_own, cross_out_own, cross_q_own, self_out_own = unpacked(
            (kept_h[0], got_h[0]), (kept_j[0], got_j[0]), width // blocks, width // columns
        )
    else:
        rest = sent_back(jnp.concatenate(pieces[1:], axis=0))
        (enc_own,) = row_grads(key_low[0], value_low[0], cross_kv, [0, enc_rows])
        enc_grad = both_queries(enc_own, [back_1, rest], here)
        own_rows = lambda array: lax.dynamic_slice_in_dim(array, slot_of * tokens, tokens, 0)
        full = back.transpose(1, 0, 2, 3).reshape(3, padded, tokens)[:, :width]
        first_back = sum(dot(full[c], self_qkv[c], 0, 1) for c in range(3))
        unused, gain_one = pulled_norm(
            own_rows(all_inputs).astype(F32), gain_rows[0], first_back
        )
        gains = jnp.concatenate([gain_one, gain_two, gain_three], axis=0)
        gain_grads = total_of(total_of(gains, "dp"), "blk")
        dec_grad = returned(dec_parts)
        reduced = lambda array: halved(halved(array, "dp", 0), "blk", 0)
        own_first = own_rows(first_low)
        own_self_mix = lax.dynamic_slice_in_dim(self_mix, slot_of * tokens, tokens, 1)
        encoded = [own_rows_low, jnp.concatenate(came, axis=0)]
        late = [
            sum(dot(e, g, 0, 0) for e, g in zip(encoded, key_low)),
            sum(dot(e, g, 0, 0) for e, g in zip(encoded, value_low)),
            dot(cross_mix, cross_grad_low, 1, 0),
            dot(second_low, query_grad, 0, 1),
            dot(own_self_mix[:width], self_grad_low, 1, 0),
        ] + [dot(own_first, full[c], 0, 1) for c in range(3)]
        chunks = [out_chunks] + [by_rows(grad) for grad in late]
        counts = [out_chunks.shape[2]] + [unit] * 8
        rows = placed(reduced(jnp.concatenate(chunks, axis=2)), counts)
        ffn_out_own, key_own, value_own, cross_out_own, cross_q_own, self_out_own = rows[:6]
        kv_own = jnp.stack([key_own, value_own])
        qkv = jnp.stack(rows[6:])
        ffn_in_own = reduced(in_chunks).astype(F32)

    return (
        output,
        dec_grad,
        enc_grad,
        gain_grads,
        qkv,
        self_out_own,
        cross_q_own,
        kv_own,
        cross_out_own,
        ffn_in_own,
        ffn_out_own,
    )


def solution(mesh):
    placed = (
        P("blk", "dp", None),
        P("dp", "blk", None),
        P("dp", None),
        P(),
        P(),
        P(),
        P(),
        P(),
        P(),
        P(),
        P(),
        P("blk", "dp", None),
    )
    return jax.shard_map(
        body,
        mesh=mesh,
        in_specs=placed,
        out_specs=(
            P("blk", "dp", None),
            P("blk", "dp", None),
            P("dp", "blk", None),
            P(),
            P(None, "blk", "dp"),
            P("blk", "dp"),
            P("blk", "dp"),
            P(None, "blk", "dp"),
            P("blk", "dp"),
            P("blk", "dp"),
            P("blk", "dp"),
        ),
        check_vma=False,
    )
```

```python
import functools

import jax
import jax.numpy as jnp
from jax import lax
from jax.experimental import pallas as pl
from jax.experimental.pallas import tpu as pltpu
from jax.sharding import PartitionSpec as P

HEAD_DIM = 64
SLOTS = 448
F32 = jnp.float32
BF16 = jnp.bfloat16
epsilon = 1e-06
negative_fill = -1e30
safe_score = 60.0
VMEM_LIMIT = 60 * 1024 * 1024


def dot(left, right, left_dim, right_dim):
    return lax.dot_general(
        left, right, (((left_dim,), (right_dim,)), ((), ())), preferred_element_type=F32
    )


def split_low(value):
    high = value.astype(BF16)
    return high, (value - high.astype(F32)).astype(BF16)


def normed(values, gain):
    return values * lax.rsqrt(jnp.mean(values * values, axis=-1, keepdims=True) + epsilon) * gain


def parted(array, axis, dim):
    size = lax.axis_size(axis)
    shape = array.shape
    above = size // shape[dim]
    split = array.reshape(shape[:dim] + (shape[dim] // 2, 2) + shape[dim + 1 :])
    bit = lax.rem(lax.axis_index(axis) // above, 2)
    kept = lax.dynamic_index_in_dim(split, bit, dim + 1, False)
    sent = lax.dynamic_index_in_dim(split, 1 - bit, dim + 1, False)
    return kept, sent, [(i, i ^ above) for i in range(size)]


def added(kept, got):
    return (kept.astype(F32) + got.astype(F32)).astype(BF16)


def fold(pairs, bit, low):
    count, _, width = pairs[0][0].shape
    rows = [k.shape[1] for k, _ in pairs]
    high, total = count // 2 // low, sum(rows)

    def kernel(s_ref, *refs):
        start = 0
        for i, size in enumerate(rows):
            for side in range(2):
                kept, got = refs[4 * i + 2 * side], refs[4 * i + 2 * side + 1]
                both = kept[...].astype(F32) + got[...].astype(F32)
                refs[4 * len(rows) + side][:, start : start + size, :] = both.reshape(
                    high * low, size, width
                ).astype(BF16)
            start += size

    def spec(size, side):
        return pl.BlockSpec(
            (high, 1, low, size, width), lambda j, s: (0, (s[0] + side) % 2, 0, 0, 0)
        )

    split = lambda array: array.reshape(high, 2, low, array.shape[1], width)
    out = pl.BlockSpec((high * low, total, width), lambda j, s: (0, 0, 0))
    return pl.pallas_call(
        kernel,
        grid_spec=pltpu.PrefetchScalarGridSpec(
            num_scalar_prefetch=1,
            grid=(1,),
            in_specs=[spec(size, side) for size in rows for side in range(2) for _ in range(2)],
            out_specs=[out] * 2,
        ),
        out_shape=[jax.ShapeDtypeStruct((high * low, total, width), BF16)] * 2,
        compiler_params=params(),
        cost_estimate=estimate(flops=0, bytes_accessed=0, transcendentals=0),
        name="fold",
    )(bit, *[split(array) for k, g in pairs for array in (k, g, k, g)])


def weight_chunks(kernel_dots, operands, specs, core, slot, columns, blocks, width):
    number = len(kernel_dots)
    size, piece = width // blocks, width // columns
    rows = number // 2 * size + number % 2 * size // 2
    shape = (columns // 2 * blocks, rows, 2 * piece)

    def kernel(c_ref, n_ref, *refs):
        kept_ref, sent_ref = refs[-2:]
        grads = [one(refs[:-2]).astype(BF16) for one in kernel_dots]

        def chunk(b, d):
            cut = lambda g, start, stop: g[
                b * size + start : b * size + stop, d * piece : (d + 1) * piece
            ]
            sides = [
                jnp.concatenate([cut(g, 0, size), cut(h, 0, size)], axis=1)
                for g, h in zip(grads[::2], grads[1::2])
            ]
            if number % 2:
                g = grads[-1]
                sides.append(
                    jnp.concatenate([cut(g, 0, size // 2), cut(g, size // 2, size)], axis=1)
                )
            return sides[0] if len(sides) == 1 else jnp.concatenate(sides, axis=0)

        for bit in range(2):

            @pl.when(c_ref[0] == bit)
            def put():
                for b in range(blocks):
                    for d in range(columns):
                        ref = kept_ref if d % 2 == bit else sent_ref
                        ref[d // 2 * blocks + b] = chunk(b, d)

    whole = lambda *shape: pl.BlockSpec(shape, lambda i, c, n: (0,) * len(shape))
    in_specs = [spec or whole(*array.shape) for array, spec in zip(operands, specs)]
    return pl.pallas_call(
        kernel,
        grid_spec=pltpu.PrefetchScalarGridSpec(
            num_scalar_prefetch=2,
            grid=(1,),
            in_specs=in_specs,
            out_specs=[whole(*shape)] * 2,
        ),
        out_shape=[jax.ShapeDtypeStruct(shape, BF16)] * 2,
        compiler_params=params(),
        cost_estimate=estimate(flops=0, bytes_accessed=0, transcendentals=0),
        name="weight_chunks",
    )(core, slot, *operands)


def row_grads(keys, values, weights, marks):
    rows, width = keys.shape
    sizes = [b - a for a, b in zip(marks, marks[1:])]

    def kernel(k_ref, v_ref, w_ref, *out_refs):
        total = dot(k_ref[...], w_ref[0], 1, 1) + dot(v_ref[...], w_ref[1], 1, 1)
        for ref, start, size in zip(out_refs, marks, sizes):
            ref[...] = total[start : start + size].astype(BF16)

    return pl.pallas_call(
        kernel,
        out_shape=[jax.ShapeDtypeStruct((size, width), BF16) for size in sizes],
        compiler_params=params(),
        cost_estimate=estimate(flops=0, bytes_accessed=0, transcendentals=0),
        name="row_grads",
    )(keys, values, weights)


def unpacked(early, late, size, piece):
    half = size // 2

    def kernel(e_ref, lk_ref, lg_ref, in_ref, out_ref, kv_ref, co_ref, cq_ref, so_ref):
        first = e_ref[...].astype(F32)
        in_ref[...] = jnp.concatenate([first[:size], first[size : 2 * size]], axis=1)
        turned = first[2 * size : 4 * size].T
        out_ref[...] = jnp.concatenate([turned[:piece], turned[piece:]], axis=1)
        co_ref[:half, :] = first[4 * size :, :piece]
        co_ref[half:, :] = first[4 * size :, piece:]
        second = lk_ref[...].astype(F32) + lg_ref[...].astype(F32)
        kv_ref[0] = second[:size, :piece]
        kv_ref[1] = second[:size, piece:]
        cq_ref[...] = second[size:, :piece]
        so_ref[...] = second[size:, piece:]

    flat = lambda *shape: jax.ShapeDtypeStruct(shape, F32)
    outs = pl.pallas_call(
        kernel,
        out_shape=[
            flat(size, 4 * piece),
            flat(piece, 4 * size),
            flat(2, size, piece),
            flat(size, piece),
            flat(size, piece),
            flat(size, piece),
        ],
        compiler_params=params(),
        cost_estimate=estimate(flops=0, bytes_accessed=0, transcendentals=0),
        name="unpacked",
    )(early, *late)
    return (outs[0], outs[1].T) + tuple(outs[2:])


def halved(array, axis, dim):
    while array.shape[dim] > 1:
        kept, sent, pairs = parted(array, axis, dim)
        array = added(kept, lax.ppermute(sent, axis, pairs))
    return jnp.squeeze(array, dim)


def total_of(array, axis):
    size = lax.axis_size(axis)
    copies = jnp.broadcast_to(array[None], (size,) + array.shape)
    return jnp.sum(lax.all_to_all(copies, axis, 0, 0), axis=0)


def estimate(flops, bytes_accessed, transcendentals):
    scale = 10**9
    return pl.CostEstimate(
        flops=max(flops // scale, 1),
        bytes_accessed=max(bytes_accessed // scale, 1),
        transcendentals=transcendentals // scale,
    )


def params():
    return pltpu.CompilerParams(vmem_limit_bytes=VMEM_LIMIT)


def cross_forward(query, pairs, bias, width, groups):
    heads = width // HEAD_DIM
    length = query.shape[1]
    tokens = length // groups
    parts = len(pairs)
    rows = [p.shape[2] for p in pairs]
    starts = [sum(rows[:i]) for i in range(parts)]
    total = sum(rows)
    stat_rows = 16 * ((heads + 15) // 16)

    def kernel(*refs):
        q_ref = refs[0]
        k_refs = refs[1 : 1 + parts]
        v_refs = refs[1 + parts : 1 + 2 * parts]
        b_refs = refs[1 + 2 * parts : 1 + 3 * parts]
        o_ref, p_ref, m_ref, lse_ref = refs[1 + 3 * parts :]
        head = pl.program_id(0)
        query = q_ref[...]
        aug_query = jnp.concatenate([query, jnp.ones((16, length), BF16)], axis=0)
        q_norm = jnp.max(jnp.sum(jnp.square(query.astype(F32)), axis=0, keepdims=True))
        k_norm = jnp.float32(0)
        for k_ref in k_refs:
            k_norm = jnp.maximum(
                k_norm, jnp.max(jnp.sum(jnp.square(k_ref[0].astype(F32)), axis=0, keepdims=True))
            )
        small = q_norm * k_norm < safe_score * safe_score

        def score(i):
            return dot(jnp.concatenate([k_refs[i][0], b_refs[i][...]], axis=0), aug_query, 0, 0)

        def finish(probs, top):
            mixed = None
            for i in range(parts):
                aug_value = jnp.concatenate([v_refs[i][0], jnp.ones((16, rows[i]), BF16)], axis=0)
                term = dot(aug_value, probs[i], 1, 0)
                mixed = term if mixed is None else mixed + term
            norm = mixed[HEAD_DIM : HEAD_DIM + 1]
            out = (mixed[:HEAD_DIM] / norm).astype(BF16)
            where = pl.ds(pl.multiple_of(head * HEAD_DIM, HEAD_DIM), HEAD_DIM)
            for g in range(groups):
                o_ref[g, where, :] = out[:, g * tokens : (g + 1) * tokens]
            lse_ref[pl.ds(head, 1), :] = top + jnp.log(norm)
            m_ref[0] = top

        @pl.when(small)
        def plain():
            probs = []
            for i in range(parts):
                prob = jnp.exp(score(i)).astype(BF16)
                p_ref[0, starts[i] : starts[i] + rows[i], :] = prob
                probs.append(prob)
            finish(probs, jnp.zeros((1, length), F32))

        @pl.when(jnp.logical_not(small))
        def shifted():
            raw = [score(i) for i in range(parts)]
            top = jnp.max(raw[0], axis=0, keepdims=True)
            for i in range(1, parts):
                top = jnp.maximum(top, jnp.max(raw[i], axis=0, keepdims=True))
            probs = []
            for i in range(parts):
                prob = jnp.exp(raw[i] - top).astype(BF16)
                p_ref[0, starts[i] : starts[i] + rows[i], :] = prob
                probs.append(prob)
            finish(probs, top)

        @pl.when(head == heads - 1)
        def stats():
            high, low = split_low(lse_ref[...])
            for g in range(groups):
                o_ref[g, width : width + stat_rows, :] = high[:, g * tokens : (g + 1) * tokens]
                o_ref[g, width + stat_rows :, :] = low[:, g * tokens : (g + 1) * tokens]

    payload = width + 2 * stat_rows
    key_specs = [pl.BlockSpec((1, HEAD_DIM, r), lambda h: (0, h, 0)) for r in rows]
    value_specs = [pl.BlockSpec((1, HEAD_DIM, r), lambda h: (1, h, 0)) for r in rows]
    return pl.pallas_call(
        kernel,
        grid=(heads,),
        in_specs=[pl.BlockSpec((HEAD_DIM, length), lambda h: (h, 0))]
        + key_specs
        + value_specs
        + [pl.BlockSpec((16, r), lambda h: (0, 0)) for r in rows],
        out_specs=[
            pl.BlockSpec((groups, payload, tokens), lambda h: (0, 0, 0)),
            pl.BlockSpec((1, total, length), lambda h: (h, 0, 0)),
            pl.BlockSpec((1, 1, length), lambda h: (h, 0, 0)),
        ],
        out_shape=[
            jax.ShapeDtypeStruct((groups, payload, tokens), BF16),
            jax.ShapeDtypeStruct((heads, total, length), BF16),
            jax.ShapeDtypeStruct((heads, 1, length), F32),
        ],
        scratch_shapes=[pltpu.VMEM((stat_rows, length), F32)],
        compiler_params=params(),
        cost_estimate=estimate(
            flops=16 * heads * total * length * HEAD_DIM,
            bytes_accessed=2 * heads * total * length,
            transcendentals=heads * total * length,
        ),
        name="cross_forward",
    )(query, *pairs, *pairs, *bias)


def cross_backward(query, pairs, prob, place, grads, tops, earlier, width, groups):
    heads = width // HEAD_DIM
    length = query.shape[1]
    tokens = length // groups
    parts = len(pairs)
    rows = [p.shape[2] for p in pairs]
    starts = [sum(rows[:i]) for i in range(parts)]
    total = sum(rows)
    pair = 2
    stat_rows = grads.shape[1] - width
    each = stat_rows // 4

    def kernel(*refs):
        q_ref = refs[0]
        k_refs = refs[1 : 1 + parts]
        v_refs = refs[1 + parts : 1 + 2 * parts]
        p_ref, g_ref, s_ref, t_ref = refs[1 + 2 * parts : 5 + 2 * parts]
        dq_ref, dk_ref, dv_ref = refs[-3:]
        step = pl.program_id(0)
        stats = jnp.concatenate([s_ref[g] for g in range(groups)], axis=1).astype(F32)
        lse = stats[:each] + stats[each : 2 * each]
        delta = stats[2 * each : 3 * each] + stats[3 * each :]
        row = lax.broadcasted_iota(jnp.int32, (each, length), 0)
        key_out = [[] for _ in range(parts)]
        value_out = [[] for _ in range(parts)]
        for j in range(pair):
            at = slice(j * HEAD_DIM, (j + 1) * HEAD_DIM)
            grad = jnp.concatenate([g_ref[g, at, :] for g in range(groups)], axis=1).astype(F32)
            pick = lambda x: jnp.sum(
                jnp.where(row == step * pair + j, x, 0.0), axis=0, keepdims=True
            )
            scale = jnp.exp(t_ref[j] - pick(lse))
            scaled = grad * scale
            high, low = split_low(-pick(delta) * scale)
            scaled_low = scaled.astype(BF16)
            pad = jnp.zeros((14, length), BF16)
            aug = jnp.concatenate([scaled_low, high, low, pad], axis=0)
            scaled_rows = scaled.T.astype(BF16)
            query_rows = q_ref[at, :].astype(F32).T.astype(BF16)
            query_grad = None
            for i in range(parts):
                aug_value = jnp.concatenate(
                    [v_refs[i][0, at, :], jnp.ones((16, rows[i]), BF16)], axis=0
                )
                prob = p_ref[j, starts[i] : starts[i] + rows[i], :]
                score = (prob.astype(F32) * dot(aug_value, aug, 0, 0)).astype(BF16)
                value_out[i].append(dot(prob, scaled_rows, 1, 0).astype(BF16))
                key_out[i].append(dot(score, query_rows, 1, 0).astype(BF16))
                term = dot(k_refs[i][0, at, :], score, 1, 0)
                query_grad = term if query_grad is None else query_grad + term
            query_grad = query_grad * 0.125
            if earlier is not None:
                before = refs[5 + 2 * parts]
                query_grad += jnp.concatenate(
                    [before[g, at, :] for g in range(groups)], axis=1
                ).astype(F32)
            query_low = query_grad.astype(BF16)
            for g in range(groups):
                dq_ref[g, at, :] = query_low[:, g * tokens : (g + 1) * tokens]
        for i in range(parts):
            at = slice(starts[i], starts[i] + rows[i])
            dk_ref[at, :] = jnp.concatenate(key_out[i], axis=1)
            dv_ref[at, :] = jnp.concatenate(value_out[i], axis=1)

    size = pair * HEAD_DIM
    key_specs = [pl.BlockSpec((1, size, r), lambda h: (0, h, 0)) for r in rows]
    value_specs = [pl.BlockSpec((1, size, r), lambda h: (1, h, 0)) for r in rows]
    token_spec = pl.BlockSpec((groups, size, tokens), lambda h: (0, h, 0))
    row_spec = pl.BlockSpec((total, size), lambda h: (0, h))
    more = [] if earlier is None else [earlier]
    return pl.pallas_call(
        kernel,
        grid=(heads // pair,),
        in_specs=[pl.BlockSpec((size, length), lambda h: (h, 0))]
        + key_specs
        + value_specs
        + [
            pl.BlockSpec((pair, total, length), lambda h: (h, place, 0)),
            token_spec,
            pl.BlockSpec((groups, stat_rows, tokens), lambda h: (0, width // stat_rows, 0)),
            pl.BlockSpec((pair, 1, length), lambda h: (h, 0, 0)),
        ]
        + [token_spec for _ in more],
        out_specs=[token_spec, row_spec, row_spec],
        out_shape=[jax.ShapeDtypeStruct((groups, width, tokens), BF16)]
        + [jax.ShapeDtypeStruct((total, width), BF16)] * 2,
        compiler_params=params(),
        cost_estimate=estimate(
            flops=32 * heads * total * length * HEAD_DIM,
            bytes_accessed=2 * heads * total * length,
            transcendentals=0,
        ),
        name="cross_backward",
    )(query, *pairs, *pairs, prob, grads, grads, tops, *more)


def self_forward(inputs, gain, weights, key_pos, query_pos, groups):
    length, width = inputs.shape
    own = weights.shape[1]
    heads = own // HEAD_DIM

    def kernel(x_ref, g_ref, w_ref, kp_ref, qp_ref, a_ref, pr_ref, o_ref, p_ref, n_ref):
        head = pl.program_id(0)

        @pl.when(head == 0)
        def project():
            low = normed(x_ref[...].astype(F32), g_ref[...]).astype(BF16)
            a_ref[...] = low
            for c in range(3):
                pr_ref[c] = dot(w_ref[c], low, 1, 1).astype(BF16)

        at = pl.ds(pl.multiple_of(head * HEAD_DIM, HEAD_DIM), HEAD_DIM)
        raw = dot(pr_ref[1, at, :], pr_ref[0, at, :], 0, 0) * 0.125
        raw = jnp.where(kp_ref[...] <= qp_ref[...], raw, negative_fill)
        top = jnp.max(raw, axis=0, keepdims=True)
        prob = jnp.exp(raw - top).astype(BF16)
        p_ref[0] = prob
        aug_value = jnp.concatenate([pr_ref[2, at, :], jnp.ones((16, length), BF16)], axis=0)
        mixed = dot(aug_value, prob, 1, 0)
        inverse = 1.0 / mixed[HEAD_DIM : HEAD_DIM + 1]
        out = (mixed[:HEAD_DIM] * inverse).astype(BF16)
        for g in range(groups):
            o_ref[g] = out
        n_ref[0] = inverse

    whole = lambda *shape: pl.BlockSpec(shape, lambda h: (0,) * len(shape))
    return pl.pallas_call(
        kernel,
        grid=(heads,),
        in_specs=[
            whole(length, width),
            whole(1, width),
            whole(3, own, width),
            whole(length, 1),
            whole(1, length),
        ],
        out_specs=[
            whole(length, width),
            whole(3, own, length),
            pl.BlockSpec((groups, HEAD_DIM, length), lambda h: (0, h, 0)),
            pl.BlockSpec((1, length, length), lambda h: (h, 0, 0)),
            pl.BlockSpec((1, 1, length), lambda h: (h, 0, 0)),
        ],
        out_shape=[
            jax.ShapeDtypeStruct((length, width), BF16),
            jax.ShapeDtypeStruct((3, own, length), BF16),
            jax.ShapeDtypeStruct((groups, own, length), BF16),
            jax.ShapeDtypeStruct((heads, length, length), BF16),
            jax.ShapeDtypeStruct((heads, 1, length), F32),
        ],
        compiler_params=params(),
        cost_estimate=estimate(
            flops=16 * heads * length * length * HEAD_DIM,
            bytes_accessed=2 * heads * length * length,
            transcendentals=heads * length * length,
        ),
        name="self_forward",
    )(inputs, gain, weights, key_pos, query_pos)


def project_rows(pieces, weights):
    counts = [p.shape[0] for p in pieces]
    total, width = sum(counts), pieces[0].shape[1]

    def kernel(*refs):
        w_ref, out_ref = refs[len(counts) :]
        start = 0
        for e_ref, count in zip(refs, counts):
            out_ref[0, :, start : start + count] = dot(w_ref[0], e_ref[...], 1, 1).astype(BF16)
            start += count

    return pl.pallas_call(
        kernel,
        grid=(2,),
        in_specs=[pl.BlockSpec((count, width), lambda c: (0, 0)) for count in counts]
        + [pl.BlockSpec((1, width, width), lambda c: (c, 0, 0))],
        out_specs=pl.BlockSpec((1, width, total), lambda c: (c, 0, 0)),
        out_shape=jax.ShapeDtypeStruct((2, width, total), BF16),
        compiler_params=params(),
        cost_estimate=estimate(
            flops=4 * total * width * width, bytes_accessed=8 * total * width, transcendentals=0
        ),
        name="project_rows",
    )(*pieces, weights)


def query_stage(inputs, mixed, out_weight, gain, query_weight, slot, groups):
    length, width = inputs.shape
    tokens = length // groups
    rows = mixed.shape[0]

    def kernel(s_ref, x_ref, o_ref, w_ref, g_ref, q_ref, qc_ref, h_ref, a_ref):
        after = x_ref[...].astype(F32) + dot(o_ref[...], w_ref[...], 0, 0)
        low = normed(after, g_ref[...]).astype(BF16)
        scaled = dot(q_ref[...], low, 1, 1).astype(BF16)
        qc_ref[...] = (scaled.astype(F32) * 0.125).astype(BF16)

        @pl.when(pl.program_id(0) == s_ref[0])
        def keep():
            h_ref[...] = after
            a_ref[...] = low

    whole = lambda *shape: pl.BlockSpec(shape, lambda i, s: (0,) * len(shape))
    return pl.pallas_call(
        kernel,
        grid_spec=pltpu.PrefetchScalarGridSpec(
            num_scalar_prefetch=1,
            grid=(groups,),
            in_specs=[
                pl.BlockSpec((tokens, width), lambda i, s: (i, 0)),
                pl.BlockSpec((rows, tokens), lambda i, s: (0, i)),
                whole(rows, width),
                whole(1, width),
                whole(width, width),
            ],
            out_specs=[
                pl.BlockSpec((width, tokens), lambda i, s: (0, i)),
                whole(tokens, width),
                whole(tokens, width),
            ],
        ),
        out_shape=[
            jax.ShapeDtypeStruct((width, length), BF16),
            jax.ShapeDtypeStruct((tokens, width), F32),
            jax.ShapeDtypeStruct((tokens, width), BF16),
        ],
        compiler_params=params(),
        cost_estimate=estimate(
            flops=8 * length * width * width, bytes_accessed=8 * width * width, transcendentals=0
        ),
        name="query_stage",
    )(slot, inputs, mixed, out_weight, gain, query_weight)


def gelu_parts(value):
    root = 0.7978845608028654
    cubic = 0.044715
    square = value * value
    bent = jnp.tanh(root * value * (1.0 + cubic * square))
    half = 0.5 * (1.0 + bent)
    slope = half + 0.5 * value * (1.0 - bent * bent) * root * (1.0 + 3.0 * cubic * square)
    return value * half, slope


def pulled_norm(values, gain, grad):
    inverse = lax.rsqrt(jnp.mean(values * values, axis=-1, keepdims=True) + epsilon)
    scaled = values * inverse
    gain_grad = jnp.sum(grad * scaled, axis=0, keepdims=True)
    weighted = grad * gain
    back = inverse * (weighted - scaled * jnp.mean(weighted * scaled, axis=-1, keepdims=True))
    return back, gain_grad


def token_stage(parts, after_self, cross_out, gain, ffn_in, ffn_out, cotangent, groups):
    tokens, width = after_self.shape
    heads = width // HEAD_DIM
    stat_rows = (parts.shape[1] - width) // 2
    hidden = ffn_in.shape[1]
    piece = 384
    steps = hidden // piece
    payload = width + 4 * stat_rows

    def kernel(
        r_ref, h_ref, co_ref, g_ref, w1_ref, w2_ref, c_ref,
        out_ref, dh_ref, g2_ref, a_ref, z_ref, du_ref, o_ref, pay_ref, gain_ref,
        after_ref, acc_ref, back_ref, lse_ref,
    ):
        step = pl.program_id(0)

        @pl.when(step == 0)
        def join():
            lse = [
                r_ref[g, width : width + stat_rows, :].astype(F32)
                + r_ref[g, width + stat_rows :, :].astype(F32)
                for g in range(groups)
            ]
            top = functools.reduce(jnp.maximum, lse)
            share = [jnp.exp(l - top) for l in lse]
            total = functools.reduce(jnp.add, share)
            lse_ref[...] = top + jnp.log(total)
            share = [s / total for s in share]
            for h in range(heads):
                at = slice(h * HEAD_DIM, (h + 1) * HEAD_DIM)
                mixed = None
                for g in range(groups):
                    term = r_ref[g, at, :].astype(F32) * share[g][h : h + 1]
                    mixed = term if mixed is None else mixed + term
                o_ref[at, :] = mixed.astype(BF16)
            after = h_ref[...] + dot(o_ref[...], co_ref[...], 0, 0)
            after_ref[...] = after
            a_ref[...] = normed(after, g_ref[...]).astype(BF16)
            acc_ref[...] = jnp.zeros_like(acc_ref)
            back_ref[...] = jnp.zeros_like(back_ref)

        pre = dot(a_ref[...], w1_ref[...], 1, 0)
        act, slope = gelu_parts(pre)
        act = act.astype(BF16)
        z_ref[...] = act
        acc_ref[...] += dot(act, w2_ref[...], 1, 0)
        pre_grad = (dot(c_ref[...], w2_ref[...], 1, 1) * slope).astype(BF16)
        du_ref[...] = pre_grad
        back_ref[...] += dot(pre_grad, w1_ref[...], 1, 1)

        @pl.when(step == steps - 1)
        def finish():
            after = after_ref[...]
            out_ref[...] = (after + acc_ref[...]).astype(BF16)
            back, gain_grad = pulled_norm(after, g_ref[...], back_ref[...])
            gain_ref[...] = gain_grad
            grad = c_ref[...].astype(F32) + back
            dh_ref[...] = grad
            low = grad.astype(BF16)
            g2_ref[...] = low
            mix_grad = dot(co_ref[...], low, 1, 1).astype(BF16)
            both = mix_grad.astype(F32) * o_ref[...].astype(F32)
            rows = [
                jnp.sum(both[h * HEAD_DIM : (h + 1) * HEAD_DIM], axis=0, keepdims=True)
                for h in range(heads)
            ]
            rows.append(jnp.zeros((stat_rows - heads, tokens), F32))
            stats = [*split_low(lse_ref[...]), *split_low(jnp.concatenate(rows, axis=0))]
            for g in range(groups):
                pay_ref[g, :width, :] = mix_grad
                for i in range(4):
                    start = width + i * stat_rows
                    pay_ref[g, start : start + stat_rows, :] = stats[i]

    whole = lambda *shape: pl.BlockSpec(shape, lambda i: (0,) * len(shape))
    flat = lambda rows, kind: jax.ShapeDtypeStruct((rows, width), kind)
    return pl.pallas_call(
        kernel,
        grid=(steps,),
        in_specs=[
            whole(*parts.shape),
            whole(tokens, width),
            whole(width, width),
            whole(1, width),
            pl.BlockSpec((width, piece), lambda i: (0, i)),
            pl.BlockSpec((piece, width), lambda i: (i, 0)),
            whole(tokens, width),
        ],
        out_specs=[
            whole(tokens, width),
            whole(tokens, width),
            whole(tokens, width),
            whole(tokens, width),
            pl.BlockSpec((tokens, piece), lambda i: (0, i)),
            pl.BlockSpec((tokens, piece), lambda i: (0, i)),
            whole(width, tokens),
            whole(groups, payload, tokens),
            whole(1, width),
        ],
        out_shape=[
            flat(tokens, BF16),
            flat(tokens, F32),
            flat(tokens, BF16),
            flat(tokens, BF16),
            jax.ShapeDtypeStruct((tokens, hidden), BF16),
            jax.ShapeDtypeStruct((tokens, hidden), BF16),
            jax.ShapeDtypeStruct((width, tokens), BF16),
            jax.ShapeDtypeStruct((groups, payload, tokens), BF16),
            flat(1, F32),
        ],
        scratch_shapes=[pltpu.VMEM((tokens, width), F32)] * 3
        + [pltpu.VMEM((stat_rows, tokens), F32)],
        compiler_params=params(),
        cost_estimate=estimate(
            flops=8 * tokens * width * hidden,
            bytes_accessed=4 * width * hidden,
            transcendentals=tokens * hidden,
        ),
        name="token_stage",
    )(parts, after_self, cross_out, gain, ffn_in, ffn_out, cotangent)


def early_weight_grads(low, pre_grad, act, cotangent, mixed, mixed_grad, columns, blocks):
    tokens, width = low.shape
    hidden = act.shape[1]
    step_size = hidden // blocks
    size, piece = width // blocks, width // columns
    half = step_size // 2

    def kernel(a_ref, du_ref, z_ref, c_ref, m_ref, g_ref, out_ref):
        step = pl.program_id(0)
        first = dot(a_ref[...], du_ref[...], 0, 0).astype(BF16)
        for p in range(2):

            @pl.when(lax.rem(step, 2) == p)
            def put():
                for b in range(blocks):
                    out_ref[step // 2, b, p * size : (p + 1) * size, :] = first[
                        b * size : (b + 1) * size
                    ]

        second = dot(z_ref[...], c_ref[...], 0, 0).astype(BF16)
        for d in range(columns):
            at = slice(d * piece, (d + 1) * piece)
            out_ref[d, step, 2 * size : 2 * size + half, :] = jnp.concatenate(
                [second[:half, at], second[half:, at]], axis=1
            )
        third = dot(m_ref[...], g_ref[...], 1, 0).astype(BF16)
        for d in range(columns):
            at = slice(d * piece, (d + 1) * piece)
            out_ref[d, step, 2 * size + half :, :] = jnp.concatenate(
                [third[: size // 2, at], third[size // 2 :, at]], axis=1
            )

    shape = (columns, blocks, 2 * size + half + size // 2, 2 * piece)
    whole = lambda *shape: pl.BlockSpec(shape, lambda i: (0,) * len(shape))
    return pl.pallas_call(
        kernel,
        grid=(blocks,),
        in_specs=[
            whole(tokens, width),
            pl.BlockSpec((tokens, step_size), lambda i: (0, i)),
            pl.BlockSpec((tokens, step_size), lambda i: (0, i)),
            whole(tokens, width),
            pl.BlockSpec((size, tokens), lambda i: (i, 0)),
            whole(tokens, width),
        ],
        out_specs=whole(*shape),
        out_shape=jax.ShapeDtypeStruct(shape, BF16),
        compiler_params=params(),
        cost_estimate=estimate(
            flops=4 * tokens * width * hidden,
            bytes_accessed=4 * width * hidden,
            transcendentals=0,
        ),
        name="early_weight_grads",
    )(low, pre_grad, act, cotangent, mixed, mixed_grad)


def mixed_stage(parts, cross_q, after_self, gain, cross_grad, self_out, groups, own):
    tokens, width = after_self.shape
    rows = self_out.shape[0]

    def kernel(r_ref, q_ref, h_ref, g_ref, dh_ref, w_ref, dq_ref, out_ref, g1_ref, do_ref, gain_ref):
        total = r_ref[0].astype(F32)
        for g in range(1, groups):
            total = total + r_ref[g].astype(F32)
        query_grad = total.astype(BF16)
        dq_ref[...] = query_grad
        back, gain_grad = pulled_norm(h_ref[...], g_ref[...], dot(query_grad, q_ref[...], 0, 1))
        gain_ref[...] = gain_grad
        grad = dh_ref[...] + back
        out_ref[...] = grad
        low = grad.astype(BF16)
        g1_ref[...] = low
        mixed = dot(w_ref[...], low, 1, 1).astype(BF16)
        for g in range(groups):
            do_ref[g] = mixed[g * own : (g + 1) * own]

    return pl.pallas_call(
        kernel,
        out_shape=[
            jax.ShapeDtypeStruct((width, tokens), BF16),
            jax.ShapeDtypeStruct((tokens, width), F32),
            jax.ShapeDtypeStruct((tokens, width), BF16),
            jax.ShapeDtypeStruct((groups, own, tokens), BF16),
            jax.ShapeDtypeStruct((1, width), F32),
        ],
        compiler_params=params(),
        cost_estimate=estimate(
            flops=4 * tokens * width * width, bytes_accessed=8 * width * width, transcendentals=0
        ),
        name="mixed_stage",
    )(parts, cross_q, after_self, gain, cross_grad, self_out)


def input_stage(back, weights, inputs, gain, self_grad, slot, groups):
    own, tokens = back.shape[2:]
    width = inputs.shape[1]
    padded = groups * own

    def kernel(s_ref, b_ref, w_ref, x_ref, g_ref, h_ref, out_ref, acc_ref):
        step = pl.program_id(0)
        grads = jnp.concatenate([b_ref[g, 0] for g in range(groups)], axis=0)
        term = dot(grads, w_ref[0], 0, 1)

        @pl.when(step == 0)
        def first():
            acc_ref[...] = term

        @pl.when(step > 0)
        def more():
            acc_ref[...] += term

        @pl.when(step == 2)
        def last():
            back, unused = pulled_norm(x_ref[...].astype(F32), g_ref[...], acc_ref[...])
            out_ref[...] = (h_ref[...] + back).astype(BF16)

    whole = lambda *shape: pl.BlockSpec(shape, lambda i, s: (0,) * len(shape))
    return pl.pallas_call(
        kernel,
        grid_spec=pltpu.PrefetchScalarGridSpec(
            num_scalar_prefetch=1,
            grid=(3,),
            in_specs=[
                pl.BlockSpec((groups, 1, own, tokens), lambda i, s: (0, i, 0, 0)),
                pl.BlockSpec((1, width, padded), lambda i, s: (i, 0, 0)),
                pl.BlockSpec((tokens, width), lambda i, s: (s[0], 0)),
                whole(1, width),
                whole(tokens, width),
            ],
            out_specs=whole(tokens, width),
            scratch_shapes=[pltpu.VMEM((tokens, width), F32)],
        ),
        out_shape=jax.ShapeDtypeStruct((tokens, width), BF16),
        compiler_params=params(),
        cost_estimate=estimate(
            flops=6 * tokens * width * width, bytes_accessed=6 * width * width, transcendentals=0
        ),
        name="input_stage",
    )(slot, back, weights, inputs, gain, self_grad)


def both_queries(own, pieces, mine):
    rows, width = own.shape

    def kernel(s_ref, own_ref, *refs):
        out_ref = refs[-1]

        @pl.when(pl.program_id(0) == s_ref[0])
        def here():
            out_ref[0] = own_ref[...]

        @pl.when(pl.program_id(0) != s_ref[0])
        def there():
            start = 0
            for ref in refs[:-1]:
                out_ref[0, start : start + ref.shape[0], :] = ref[...]
                start += ref.shape[0]

    whole = lambda *shape: pl.BlockSpec(shape, lambda i, s: (0,) * len(shape))
    return pl.pallas_call(
        kernel,
        grid_spec=pltpu.PrefetchScalarGridSpec(
            num_scalar_prefetch=1,
            grid=(2,),
            in_specs=[whole(*own.shape)] + [whole(*p.shape) for p in pieces],
            out_specs=pl.BlockSpec((1, rows, width), lambda i, s: (i, 0, 0)),
        ),
        out_shape=jax.ShapeDtypeStruct((2, rows, width), own.dtype),
        compiler_params=params(),
        cost_estimate=estimate(flops=0, bytes_accessed=8 * rows * width, transcendentals=0),
        name="both_queries",
    )(mine, own, *pieces)


def own_weight_grads(low, gain, grads, weights, column, columns, blocks):
    length, width = low.shape
    groups, _, own, tokens = grads.shape
    rows = width // blocks
    per = blocks // columns

    def kernel(c_ref, a_ref, g_ref, d_ref, w_ref, *refs):
        gain_ref = refs[-1]
        step = pl.program_id(0)
        grads = jnp.concatenate([d_ref[g, 0] for g in range(groups)], axis=1)
        turned = dot(grads, a_ref[...], 1, 0)
        weight = turned.T.astype(BF16)
        for d in range(columns):

            @pl.when(c_ref[0] == d)
            def put():
                for b in range(blocks):
                    refs[b // per ^ d][b % per, 0] = weight[b * rows : (b + 1) * rows]

        term = jnp.sum(turned * w_ref[0].astype(F32), axis=0, keepdims=True) / g_ref[...]

        @pl.when(step == 0)
        def first():
            gain_ref[...] = term

        @pl.when(step > 0)
        def more():
            gain_ref[...] += term

    shape = (per, 3, rows, own)
    whole = lambda *shape: pl.BlockSpec(shape, lambda i, c: (0,) * len(shape))
    part = pl.BlockSpec((per, 1, rows, own), lambda i, c: (0, i, 0, 0))
    return pl.pallas_call(
        kernel,
        grid_spec=pltpu.PrefetchScalarGridSpec(
            num_scalar_prefetch=1,
            grid=(3,),
            in_specs=[
                whole(length, width),
                whole(1, width),
                pl.BlockSpec((groups, 1, own, tokens), lambda i, c: (0, i, 0, 0)),
                pl.BlockSpec((1, own, width), lambda i, c: (i, 0, 0)),
            ],
            out_specs=[part] * columns + [whole(1, width)],
        ),
        out_shape=[jax.ShapeDtypeStruct(shape, BF16)] * columns
        + [jax.ShapeDtypeStruct((1, width), F32)],
        compiler_params=params(),
        cost_estimate=estimate(
            flops=12 * length * width * own, bytes_accessed=4 * length * width, transcendentals=0
        ),
        name="own_weight_grads",
    )(column, low, gain, grads, weights)


def sums_for(pairs, groups):
    blocks, _, width = pairs[0][0].shape
    rows = [k.shape[1] for k, _ in pairs]
    high = blocks // groups

    def kernel(*refs):
        out_ref = refs[-1]
        start = 0
        for i, size in enumerate(rows):
            both = refs[2 * i][...].astype(F32) + refs[2 * i + 1][...].astype(F32)
            both = both.astype(BF16)
            for b in range(blocks):
                out_ref[b % groups, b // groups, start : start + size, :] = both[b]
            start += size

    return pl.pallas_call(
        kernel,
        out_shape=jax.ShapeDtypeStruct((groups, high, sum(rows), width), BF16),
        compiler_params=params(),
        cost_estimate=estimate(flops=0, bytes_accessed=0, transcendentals=0),
        name="sums_for",
    )(*[array for pair in pairs for array in pair])


def sums_of(arrays, bit):
    _, rows, width = arrays[0].shape

    def kernel(s_ref, *refs):
        for side in range(2):
            terms = [refs[2 * i + side][0].astype(F32) for i in range(len(arrays))]
            refs[2 * len(arrays) + side][...] = functools.reduce(jnp.add, terms).astype(BF16)

    spec = lambda side: pl.BlockSpec((1, rows, width), lambda j, s: ((s[0] + side) % 2, 0, 0))
    out = pl.BlockSpec((rows, width), lambda j, s: (0, 0))
    return pl.pallas_call(
        kernel,
        grid_spec=pltpu.PrefetchScalarGridSpec(
            num_scalar_prefetch=1,
            grid=(1,),
            in_specs=[spec(side) for _ in arrays for side in range(2)],
            out_specs=[out] * 2,
        ),
        out_shape=[jax.ShapeDtypeStruct((rows, width), BF16)] * 2,
        compiler_params=params(),
        cost_estimate=estimate(flops=0, bytes_accessed=0, transcendentals=0),
        name="sums_of",
    )(bit, *[array for array in arrays for _ in range(2)])


def self_backward(projected, mixed, grads, prob, weight, groups):
    own, length = projected.shape[1:]
    heads = own // HEAD_DIM
    tokens = length // groups

    def kernel(q_ref, k_ref, v_ref, o_ref, g_ref, p_ref, w_ref, out_ref):
        grad = jnp.concatenate([g_ref[g] for g in range(groups)], axis=1).astype(F32)
        scaled = grad * w_ref[0]
        high, low = split_low(-jnp.sum(scaled * o_ref[0].astype(F32), axis=0, keepdims=True))
        scaled_low = scaled.astype(BF16)
        aug = jnp.concatenate([scaled_low, high, low, jnp.zeros((14, length), BF16)], axis=0)
        aug_value = jnp.concatenate([v_ref[0], jnp.ones((16, length), BF16)], axis=0)
        prob = p_ref[0]
        score = (prob.astype(F32) * dot(aug_value, aug, 0, 0)).astype(BF16)
        results = (
            dot(k_ref[0], score, 1, 0) * 0.125,
            dot(q_ref[0], score, 1, 1) * 0.125,
            dot(scaled_low, prob, 1, 1),
        )
        for c in range(3):
            result = results[c].astype(BF16)
            for g in range(groups):
                out_ref[g, c] = result[:, g * tokens : (g + 1) * tokens]

    spec = lambda c: pl.BlockSpec((1, HEAD_DIM, length), lambda h: (c, h, 0))
    return pl.pallas_call(
        kernel,
        grid=(heads,),
        in_specs=[
            spec(0),
            spec(1),
            spec(2),
            pl.BlockSpec((1, HEAD_DIM, length), lambda h: (0, h, 0)),
            pl.BlockSpec((groups, HEAD_DIM, tokens), lambda h: (0, h, 0)),
            pl.BlockSpec((1, length, length), lambda h: (h, 0, 0)),
            pl.BlockSpec((1, 1, length), lambda h: (h, 0, 0)),
        ],
        out_specs=pl.BlockSpec((groups, 3, HEAD_DIM, tokens), lambda h: (0, 0, h, 0)),
        out_shape=jax.ShapeDtypeStruct((groups, 3, own, tokens), BF16),
        compiler_params=params(),
        cost_estimate=estimate(
            flops=32 * heads * length * length * HEAD_DIM,
            bytes_accessed=2 * heads * length * length,
            transcendentals=0,
        ),
        name="self_backward",
    )(projected, projected, projected, mixed, grads, prob, weight)


def body(
    dec_input,
    enc_output,
    lengths,
    gains,
    self_qkv,
    self_out,
    cross_q,
    cross_kv,
    cross_out,
    ffn_in,
    ffn_out,
    cotangent,
):
    seg, seqs, width = dec_input.shape
    heads = width // HEAD_DIM
    blocks = lax.axis_size("blk")
    place = lax.axis_index("blk")
    groups = blocks // seqs
    mine = place // groups
    slot_of = lax.rem(place, groups)
    members = [[s * groups + g for g in range(groups)] for s in range(seqs)]
    own_heads = -(-heads // groups)
    own = own_heads * HEAD_DIM
    padded = own * groups
    tokens = seqs * seg
    length = groups * tokens
    enc_rows = enc_output.shape[1]
    columns = lax.axis_size("dp")
    gain_rows = gains.astype(F32)[:, None, :]

    def shifted(step):
        return [(b, (b + step * groups) % blocks) for b in range(blocks)]

    def exchange(pieces):
        parts = [pieces(mine)]
        for step in range(1, seqs):
            parts.append(lax.ppermute(pieces(lax.rem(mine + step, seqs)), "blk", shifted(step)))
        return parts

    def in_order(parts):
        ordered = []
        for s in range(seqs):
            choice = parts[0]
            for step in range(1, seqs):
                from_there = lax.rem(mine - step + seqs, seqs) == s
                choice = jnp.where(from_there, parts[step], choice)
            ordered.append(choice)
        return ordered

    def spread(array):
        return lax.all_to_all(
            jnp.broadcast_to(array[None], (groups,) + array.shape),
            "blk",
            0,
            0,
            axis_index_groups=members,
        )

    def traded(array):
        return lax.all_to_all(array, "blk", 0, 0, axis_index_groups=members)

    def gathered(array):
        by_query = lax.optimization_barrier(array.swapaxes(0, 1))
        take = lambda s: lax.dynamic_index_in_dim(by_query, s, 0, False)
        return jnp.concatenate(in_order(exchange(take)), axis=0)

    def leaving(array):
        split = array.reshape(seqs, seg, width)
        return exchange(lambda s: lax.dynamic_index_in_dim(split, s, 0, False))

    def returned(parts):
        return jnp.stack(in_order(parts), axis=1)

    own_inputs = gathered(dec_input)
    all_inputs = spread(own_inputs).reshape(length, width)

    pick = lambda s: lax.dynamic_index_in_dim(enc_output, s, 0, False)
    cuts = [max(enc_rows * 3 // 7 // 128 * 128, 128)]
    cuts.append(cuts[0] + 128)
    spans = [(0, 0, enc_rows)]
    arrived = []
    for step in range(1, seqs):
        sent = pick(lax.rem(mine + step, seqs))
        arrived.append([lax.ppermute(sent[: cuts[0]], "blk", shifted(step))])
        spans += [(step, 0, cuts[0]), (step, cuts[0], enc_rows)]
        for start, stop in ((cuts[0], cuts[1]), (cuts[1], enc_rows)):
            piece, unused = lax.optimization_barrier((sent[start:stop], arrived[-1][-1]))
            arrived[-1].append(lax.ppermute(piece, "blk", shifted(step)))
    own_rows_low = pick(mine)
    turned_kv = cross_kv.swapaxes(1, 2)
    first_pair = project_rows([own_rows_low], turned_kv)
    all_inputs, first_pair, firsts = lax.optimization_barrier(
        (all_inputs, first_pair, [a[0] for a in arrived])
    )

    row_lengths = lax.dynamic_index_in_dim(lengths, mine, 0, False)
    bias = []
    for step, start, stop in spans:
        source = lax.rem(place - step * groups + blocks, blocks)
        slot = source * enc_rows + jnp.arange(start, stop)
        match = (slot // SLOTS)[:, None] == jnp.arange(lengths.shape[1])[None, :]
        filled = jnp.sum(jnp.where(match, row_lengths[None, :], 0), axis=-1)
        row = jnp.where((slot % SLOTS) < filled, 0.0, negative_fill).astype(BF16)
        bias.append(jnp.concatenate([row[None], jnp.zeros((15, stop - start), BF16)], axis=0))

    extra = [(0, 0), (0, 0), (0, padded - width)]
    padded_qkv = jnp.pad(self_qkv, extra)
    own_qkv = lax.dynamic_slice_in_dim(padded_qkv, slot_of * own, own, 2).swapaxes(1, 2)
    padded_out = jnp.pad(self_out, [(0, padded - width), (0, 0)])
    index = jnp.arange(length)
    block = index // seg
    position = ((block % seqs) * groups + block // seqs) * seg + index % seg
    position = position.astype(jnp.int32)
    first_low, projected, sent_mix, self_prob, self_weight = self_forward(
        all_inputs,
        gain_rows[0],
        own_qkv,
        position[:, None],
        position[None, :],
        groups,
    )
    sent_mix, seconds = lax.optimization_barrier((sent_mix, [a[1] for a in arrived]))
    self_mix = traded(sent_mix).reshape(padded, length)
    slot = jnp.full((1,), slot_of, jnp.int32)
    cross_query, after_self, second_low = query_stage(
        all_inputs, self_mix, padded_out, gain_rows[1], cross_q.T, slot, groups
    )

    cross_query, thirds = lax.optimization_barrier((cross_query, [a[2] for a in arrived]))
    pairs = [first_pair]
    came = []
    for first, second, third in zip(firsts, seconds, thirds):
        pairs.append(project_rows([first], turned_kv))
        pairs.append(project_rows([second, third], turned_kv))
        came += [first, second, third]

    part_mix, cross_prob, local_top = cross_forward(cross_query, pairs, bias, width, groups)

    own_cotangent = gathered(cotangent)
    (
        own_output,
        cross_grad,
        cross_grad_low,
        third_low,
        hidden_low,
        pre_low,
        cross_mix,
        payload,
        gain_three,
    ) = token_stage(
        traded(part_mix),
        after_self,
        cross_out,
        gain_rows[2],
        ffn_in,
        ffn_out,
        own_cotangent,
        groups,
    )
    packed = traded(payload)

    def by_rows(grad):
        return grad.astype(BF16).reshape(blocks, columns, -1, grad.shape[-1]).swapaxes(0, 1)

    def placed(rows, counts):
        count, full = rows.shape
        split = rows.reshape(count, columns, full // columns).swapaxes(0, 1)
        moved = lax.all_to_all(split, "dp", 0, 0).astype(F32)
        ends = [sum(counts[: i + 1]) for i in range(len(counts) - 1)]
        return [p.reshape(-1, full // columns) for p in jnp.split(moved, ends, axis=1)]

    unit = width // blocks // columns
    staged = (
        padded == width
        and columns * own == width
        and columns * seqs == blocks
        and columns % 2 == 0
        and ffn_in.shape[1] == columns * width
        and ffn_in.shape[1] // blocks * columns == 2 * width
        and blocks == 8
    )
    if staged:
        chunks = early_weight_grads(
            third_low,
            pre_low,
            hidden_low,
            own_cotangent,
            cross_mix,
            cross_grad_low,
            columns,
            blocks,
        )
        packed, chunks, own_output = lax.optimization_barrier((packed, chunks, own_output))
        inner = chunks.shape[2:]
        hidden = lax.psum_scatter(
            chunks.reshape(-1, inner[1]), "dp", scatter_dimension=0, tiled=True
        )
    else:
        in_chunks = dot(third_low, pre_low, 0, 0).astype(BF16)
        in_chunks = in_chunks.reshape(blocks, width // blocks, columns, -1).transpose(2, 0, 1, 3)
        out_chunks = by_rows(dot(hidden_low, own_cotangent, 0, 0))
    together = lambda *values: lax.optimization_barrier(values)

    output_parts = leaving(own_output)

    def rows_backward(place, subset, earlier):
        return cross_backward(
            cross_query, subset, cross_prob, place, packed, local_top, earlier, width, groups
        )

    shares = [0, 11, 19, 23, 28]
    marks = [enc_rows * share // 28 for share in shares]
    part_grads, came_key, came_value = rows_backward(1, pairs[1:], None)
    pieces = row_grads(came_key, came_value, cross_kv, marks)

    def sent_back(piece):
        return lax.ppermute(piece, "blk", shifted(1))

    part_grads, pieces, output_parts = together(part_grads, pieces, output_parts)
    back_1 = sent_back(pieces[0])
    query_parts, own_key, own_value = rows_backward(0, pairs[:1], part_grads)
    key_low, value_low = [own_key, came_key], [own_value, came_value]
    query_parts, key_low, value_low, back_1, pieces = together(
        query_parts, key_low, value_low, back_1, pieces
    )
    joined = traded(query_parts)
    here = jnp.full((1,), mine, jnp.int32)

    def moved(array, axis, step):
        size = lax.axis_size(axis)
        return lax.ppermute(array, axis, [(i, i ^ step) for i in range(size)])

    def bit_of(axis, step):
        return jnp.full((1,), lax.rem(lax.axis_index(axis) // step, 2), jnp.int32)

    def chunks_of(kernel_dots, operands, specs):
        return weight_chunks(
            kernel_dots, operands, specs, bit_of("dp", 1), slot, columns, blocks, width
        )

    back_2 = sent_back(pieces[1])
    output = returned(output_parts)
    if staged:
        cuts = [0]
        for piece in came:
            cuts.append(cuts[-1] + piece.shape[0])

        def rows_dot(grad):
            def one(refs):
                total = dot(refs[0][...], refs[grad][...], 0, 0)
                for i, (start, stop) in enumerate(zip(cuts, cuts[1:])):
                    total += dot(refs[1 + i][...], refs[grad + 1][start:stop, :], 0, 0)
                return total

            return one

        count = 1 + len(came)
        operands = [own_rows_low, *came, *key_low, *value_low]
        kept_1, sent_1 = chunks_of(
            [
                rows_dot(count),
                rows_dot(count + 2),
            ],
            operands,
            [None] * len(operands),
        )
        joined, pieces, back_2, output, hidden, kept_1, sent_1 = together(
            joined, pieces, back_2, output, hidden, kept_1, sent_1
        )
        hidden = lax.psum_scatter(hidden, "blk", scatter_dimension=0, tiled=True)
        got_1 = moved(sent_1, "dp", 1)
    query_grad, self_grad, self_grad_low, mixed_grad, gain_two = mixed_stage(
        joined, cross_q, after_self, gain_rows[1], cross_grad, padded_out, groups, own
    )
    if staged:
        query_grad, self_grad, self_grad_low, mixed_grad, gain_two, kept_1, got_1, pieces = (
            together(
                query_grad, self_grad, self_grad_low, mixed_grad, gain_two, kept_1, got_1, pieces
            )
        )
    own_mixed = traded(mixed_grad)
    if staged:
        back_3 = sent_back(pieces[2])
        kept_1, sent_1 = fold([(kept_1, got_1)], bit_of("dp", 2), blocks)
        operands = [second_low, query_grad, self_mix, self_grad_low]
        specs = [None] * 2
        specs += [pl.BlockSpec((width, tokens), lambda i, c, n: (0, n[0])), None]
        kept_2, sent_2 = chunks_of(
            [
                lambda refs: dot(refs[0][...], refs[1][...], 0, 1),
                lambda refs: dot(refs[2][...], refs[3][...], 1, 0),
            ],
            operands,
            specs,
        )
        own_mixed, back_3, kept_1, sent_1, kept_2, sent_2, pieces = together(
            own_mixed, back_3, kept_1, sent_1, kept_2, sent_2, pieces
        )
        got_1 = moved(sent_1, "dp", 2)
        got_2 = moved(sent_2, "dp", 1)
    own_grads = self_backward(projected, sent_mix, own_mixed, self_prob, self_weight, groups)
    if staged:
        own_grads, kept_1, got_1, kept_2, got_2, pieces = together(
            own_grads, kept_1, got_1, kept_2, got_2, pieces
        )
    back = traded(own_grads)
    if staged:
        back_4 = sent_back(pieces[3])
        kept_2, sent_2 = fold([(kept_2, got_2)], bit_of("dp", 2), blocks)
        got_2 = moved(sent_2, "dp", 2)
        *parts_w, gain_one = own_weight_grads(
            first_low,
            gain_rows[0],
            own_grads,
            own_qkv,
            jnp.full((1,), lax.axis_index("dp"), jnp.int32),
            columns,
            blocks,
        )
        gains = jnp.concatenate([gain_one, gain_two, gain_three], axis=0)
        back, back_4, kept_1, got_1, kept_2, got_2, parts_w, gains, key_low = together(
            back, back_4, kept_1, got_1, kept_2, got_2, parts_w, gains, key_low
        )
    own_grad = input_stage(back, padded_qkv, all_inputs, gain_rows[0], self_grad, slot, groups)
    if staged:
        late = traded(sums_for([(kept_1, got_1), (kept_2, got_2)], groups))
        parts_w = [parts_w[0]] + [moved(p, "dp", r) for r, p in enumerate(parts_w) if r]
        gains = gains + moved(gains, "dp", 1)
        gains = gains + moved(gains, "dp", 2)
        (enc_own,) = row_grads(key_low[0], value_low[0], cross_kv, [0, enc_rows])
        enc_grad = both_queries(enc_own, [back_1, back_2, back_3, back_4], here)
        own_grad, late, parts_w, gains, enc_grad = together(
            own_grad, late, parts_w, gains, enc_grad
        )
    dec_parts = leaving(own_grad)
    if staged:
        kept_j, sent_j = sums_of([late[g] for g in range(groups)], here)
        got_j = moved(sent_j, "blk", groups)
        halves = sums_of([p.reshape(seqs, -1, own) for p in parts_w], here)
        got_w = []
        for step, piece in enumerate(halves):
            pairs = []
            for b in range(blocks):
                row = (b // groups + step) % seqs
                for d in range(columns):
                    pairs.append((b * columns + d, (d * seqs + row) * columns + b % groups))
            piece = piece.reshape(3, width // blocks, own)
            got_w.append(lax.ppermute(piece, ("blk", "dp"), pairs))
        gains = gains + moved(gains, "blk", 1)
        gains = gains + moved(gains, "blk", 2)
        dec_parts, kept_j, got_j, got_w, gains = together(
            dec_parts, kept_j, got_j, got_w, gains
        )
        gain_grads = gains + moved(gains, "blk", 4)
        dec_grad = returned(dec_parts)
        qkv = sum(piece.astype(F32) for piece in got_w)
        ffn_in_own, ffn_out_own, kv_own, cross_out_own, cross_q_own, self_out_own = unpacked(
            hidden, (kept_j, got_j), width // blocks, width // columns
        )
    else:
        rest = sent_back(jnp.concatenate(pieces[2:], axis=0))
        (enc_own,) = row_grads(key_low[0], value_low[0], cross_kv, [0, enc_rows])
        enc_grad = both_queries(enc_own, [back_1, back_2, rest], here)
        own_rows = lambda array: lax.dynamic_slice_in_dim(array, slot_of * tokens, tokens, 0)
        full = back.transpose(1, 0, 2, 3).reshape(3, padded, tokens)[:, :width]
        first_back = sum(dot(full[c], self_qkv[c], 0, 1) for c in range(3))
        unused, gain_one = pulled_norm(
            own_rows(all_inputs).astype(F32), gain_rows[0], first_back
        )
        gains = jnp.concatenate([gain_one, gain_two, gain_three], axis=0)
        gain_grads = total_of(total_of(gains, "dp"), "blk")
        dec_grad = returned(dec_parts)
        reduced = lambda array: halved(halved(array, "dp", 0), "blk", 0)
        own_first = own_rows(first_low)
        own_self_mix = lax.dynamic_slice_in_dim(self_mix, slot_of * tokens, tokens, 1)
        encoded = [own_rows_low, jnp.concatenate(came, axis=0)]
        late = [
            sum(dot(e, g, 0, 0) for e, g in zip(encoded, key_low)),
            sum(dot(e, g, 0, 0) for e, g in zip(encoded, value_low)),
            dot(cross_mix, cross_grad_low, 1, 0),
            dot(second_low, query_grad, 0, 1),
            dot(own_self_mix[:width], self_grad_low, 1, 0),
        ] + [dot(own_first, full[c], 0, 1) for c in range(3)]
        chunks = [out_chunks] + [by_rows(grad) for grad in late]
        counts = [out_chunks.shape[2]] + [unit] * 8
        rows = placed(reduced(jnp.concatenate(chunks, axis=2)), counts)
        ffn_out_own, key_own, value_own, cross_out_own, cross_q_own, self_out_own = rows[:6]
        kv_own = jnp.stack([key_own, value_own])
        qkv = jnp.stack(rows[6:])
        ffn_in_own = reduced(in_chunks).astype(F32)

    return (
        output,
        dec_grad,
        enc_grad,
        gain_grads,
        qkv,
        self_out_own,
        cross_q_own,
        kv_own,
        cross_out_own,
        ffn_in_own,
        ffn_out_own,
    )


def solution(mesh):
    placed = (
        P("blk", "dp", None),
        P("dp", "blk", None),
        P("dp", None),
        P(),
        P(),
        P(),
        P(),
        P(),
        P(),
        P(),
        P(),
        P("blk", "dp", None),
    )
    return jax.shard_map(
        body,
        mesh=mesh,
        in_specs=placed,
        out_specs=(
            P("blk", "dp", None),
            P("blk", "dp", None),
            P("dp", "blk", None),
            P(),
            P(None, "blk", "dp"),
            P("blk", "dp"),
            P("blk", "dp"),
            P(None, "blk", "dp"),
            P("blk", "dp"),
            P("blk", "dp"),
            P("blk", "dp"),
        ),
        check_vma=False,
    )
```

```python
import functools

import jax
import jax.numpy as jnp
from jax import lax
from jax.experimental import pallas as pl
from jax.experimental.pallas import tpu as pltpu
from jax.sharding import PartitionSpec as P

HEAD_DIM = 64
SLOTS = 448
F32 = jnp.float32
BF16 = jnp.bfloat16
epsilon = 1e-06
negative_fill = -1e30
safe_score = 60.0
VMEM_LIMIT = 60 * 1024 * 1024


def dot(left, right, left_dim, right_dim):
    return lax.dot_general(
        left, right, (((left_dim,), (right_dim,)), ((), ())), preferred_element_type=F32
    )


def split_low(value):
    high = value.astype(BF16)
    return high, (value - high.astype(F32)).astype(BF16)


def normed(values, gain):
    return values * lax.rsqrt(jnp.mean(values * values, axis=-1, keepdims=True) + epsilon) * gain


def parted(array, axis, dim):
    size = lax.axis_size(axis)
    shape = array.shape
    above = size // shape[dim]
    split = array.reshape(shape[:dim] + (shape[dim] // 2, 2) + shape[dim + 1 :])
    bit = lax.rem(lax.axis_index(axis) // above, 2)
    kept = lax.dynamic_index_in_dim(split, bit, dim + 1, False)
    sent = lax.dynamic_index_in_dim(split, 1 - bit, dim + 1, False)
    return kept, sent, [(i, i ^ above) for i in range(size)]


def added(kept, got):
    return (kept.astype(F32) + got.astype(F32)).astype(BF16)


def fold(pairs, bit, low):
    count, _, width = pairs[0][0].shape
    rows = [k.shape[1] for k, _ in pairs]
    high, total = count // 2 // low, sum(rows)

    def kernel(s_ref, *refs):
        start = 0
        for i, size in enumerate(rows):
            for side in range(2):
                kept, got = refs[4 * i + 2 * side], refs[4 * i + 2 * side + 1]
                both = kept[...].astype(F32) + got[...].astype(F32)
                refs[4 * len(rows) + side][:, start : start + size, :] = both.reshape(
                    high * low, size, width
                ).astype(BF16)
            start += size

    def spec(size, side):
        return pl.BlockSpec(
            (high, 1, low, size, width), lambda j, s: (0, (s[0] + side) % 2, 0, 0, 0)
        )

    split = lambda array: array.reshape(high, 2, low, array.shape[1], width)
    out = pl.BlockSpec((high * low, total, width), lambda j, s: (0, 0, 0))
    return pl.pallas_call(
        kernel,
        grid_spec=pltpu.PrefetchScalarGridSpec(
            num_scalar_prefetch=1,
            grid=(1,),
            in_specs=[spec(size, side) for size in rows for side in range(2) for _ in range(2)],
            out_specs=[out] * 2,
        ),
        out_shape=[jax.ShapeDtypeStruct((high * low, total, width), BF16)] * 2,
        compiler_params=params(),
        cost_estimate=estimate(flops=0, bytes_accessed=0, transcendentals=0),
        name="fold",
    )(bit, *[split(array) for k, g in pairs for array in (k, g, k, g)])


def weight_chunks(kernel_dots, operands, specs, core, slot, columns, blocks, width):
    number = len(kernel_dots)
    size, piece = width // blocks, width // columns
    rows = number // 2 * size + number % 2 * size // 2
    shape = (columns // 2 * blocks, rows, 2 * piece)

    def kernel(c_ref, n_ref, *refs):
        kept_ref, sent_ref = refs[-2:]
        grads = [one(refs[:-2]).astype(BF16) for one in kernel_dots]

        def chunk(b, d):
            cut = lambda g, start, stop: g[
                b * size + start : b * size + stop, d * piece : (d + 1) * piece
            ]
            sides = [
                jnp.concatenate([cut(g, 0, size), cut(h, 0, size)], axis=1)
                for g, h in zip(grads[::2], grads[1::2])
            ]
            if number % 2:
                g = grads[-1]
                sides.append(
                    jnp.concatenate([cut(g, 0, size // 2), cut(g, size // 2, size)], axis=1)
                )
            return sides[0] if len(sides) == 1 else jnp.concatenate(sides, axis=0)

        for bit in range(2):

            @pl.when(c_ref[0] == bit)
            def put():
                for b in range(blocks):
                    for d in range(columns):
                        ref = kept_ref if d % 2 == bit else sent_ref
                        ref[d // 2 * blocks + b] = chunk(b, d)

    whole = lambda *shape: pl.BlockSpec(shape, lambda i, c, n: (0,) * len(shape))
    in_specs = [spec or whole(*array.shape) for array, spec in zip(operands, specs)]
    return pl.pallas_call(
        kernel,
        grid_spec=pltpu.PrefetchScalarGridSpec(
            num_scalar_prefetch=2,
            grid=(1,),
            in_specs=in_specs,
            out_specs=[whole(*shape)] * 2,
        ),
        out_shape=[jax.ShapeDtypeStruct(shape, BF16)] * 2,
        compiler_params=params(),
        cost_estimate=estimate(flops=0, bytes_accessed=0, transcendentals=0),
        name="weight_chunks",
    )(core, slot, *operands)


def row_grads(keys, values, weights, marks):
    rows, width = keys.shape
    sizes = [b - a for a, b in zip(marks, marks[1:])]

    def kernel(k_ref, v_ref, w_ref, *out_refs):
        total = dot(k_ref[...], w_ref[0], 1, 1) + dot(v_ref[...], w_ref[1], 1, 1)
        for ref, start, size in zip(out_refs, marks, sizes):
            ref[...] = total[start : start + size].astype(BF16)

    return pl.pallas_call(
        kernel,
        out_shape=[jax.ShapeDtypeStruct((size, width), BF16) for size in sizes],
        compiler_params=params(),
        cost_estimate=estimate(flops=0, bytes_accessed=0, transcendentals=0),
        name="row_grads",
    )(keys, values, weights)


def unpacked(early, late, size, piece):
    half = size // 2

    def kernel(e_ref, lk_ref, lg_ref, in_ref, out_ref, kv_ref, co_ref, cq_ref, so_ref):
        first = e_ref[...].astype(F32)
        in_ref[...] = jnp.concatenate([first[:size], first[size : 2 * size]], axis=1)
        turned = first[2 * size : 4 * size].T
        out_ref[...] = jnp.concatenate([turned[:piece], turned[piece:]], axis=1)
        co_ref[:half, :] = first[4 * size :, :piece]
        co_ref[half:, :] = first[4 * size :, piece:]
        second = lk_ref[...].astype(F32) + lg_ref[...].astype(F32)
        kv_ref[0] = second[:size, :piece]
        kv_ref[1] = second[:size, piece:]
        cq_ref[...] = second[size:, :piece]
        so_ref[...] = second[size:, piece:]

    flat = lambda *shape: jax.ShapeDtypeStruct(shape, F32)
    outs = pl.pallas_call(
        kernel,
        out_shape=[
            flat(size, 4 * piece),
            flat(piece, 4 * size),
            flat(2, size, piece),
            flat(size, piece),
            flat(size, piece),
            flat(size, piece),
        ],
        compiler_params=params(),
        cost_estimate=estimate(flops=0, bytes_accessed=0, transcendentals=0),
        name="unpacked",
    )(early, *late)
    return (outs[0], outs[1].T) + tuple(outs[2:])


def halved(array, axis, dim):
    while array.shape[dim] > 1:
        kept, sent, pairs = parted(array, axis, dim)
        array = added(kept, lax.ppermute(sent, axis, pairs))
    return jnp.squeeze(array, dim)


def total_of(array, axis):
    size = lax.axis_size(axis)
    copies = jnp.broadcast_to(array[None], (size,) + array.shape)
    return jnp.sum(lax.all_to_all(copies, axis, 0, 0), axis=0)


def estimate(flops, bytes_accessed, transcendentals):
    scale = 10**9
    return pl.CostEstimate(
        flops=max(flops // scale, 1),
        bytes_accessed=max(bytes_accessed // scale, 1),
        transcendentals=transcendentals // scale,
    )


def params():
    return pltpu.CompilerParams(vmem_limit_bytes=VMEM_LIMIT)


def cross_forward(query, pairs, bias, width, groups):
    heads = width // HEAD_DIM
    length = query.shape[1]
    tokens = length // groups
    parts = len(pairs)
    rows = [p.shape[2] for p in pairs]
    starts = [sum(rows[:i]) for i in range(parts)]
    total = sum(rows)
    stat_rows = 16 * ((heads + 15) // 16)

    def kernel(*refs):
        q_ref = refs[0]
        k_refs = refs[1 : 1 + parts]
        v_refs = refs[1 + parts : 1 + 2 * parts]
        b_refs = refs[1 + 2 * parts : 1 + 3 * parts]
        o_ref, p_ref, m_ref, lse_ref = refs[1 + 3 * parts :]
        head = pl.program_id(0)
        query = q_ref[...]
        aug_query = jnp.concatenate([query, jnp.ones((16, length), BF16)], axis=0)
        q_norm = jnp.max(jnp.sum(jnp.square(query.astype(F32)), axis=0, keepdims=True))
        k_norm = jnp.float32(0)
        for k_ref in k_refs:
            k_norm = jnp.maximum(
                k_norm, jnp.max(jnp.sum(jnp.square(k_ref[0].astype(F32)), axis=0, keepdims=True))
            )
        small = q_norm * k_norm < safe_score * safe_score

        def score(i):
            return dot(jnp.concatenate([k_refs[i][0], b_refs[i][...]], axis=0), aug_query, 0, 0)

        def finish(probs, top):
            mixed = None
            for i in range(parts):
                aug_value = jnp.concatenate([v_refs[i][0], jnp.ones((16, rows[i]), BF16)], axis=0)
                term = dot(aug_value, probs[i], 1, 0)
                mixed = term if mixed is None else mixed + term
            norm = mixed[HEAD_DIM : HEAD_DIM + 1]
            out = (mixed[:HEAD_DIM] / norm).astype(BF16)
            where = pl.ds(pl.multiple_of(head * HEAD_DIM, HEAD_DIM), HEAD_DIM)
            for g in range(groups):
                o_ref[g, where, :] = out[:, g * tokens : (g + 1) * tokens]
            lse_ref[pl.ds(head, 1), :] = top + jnp.log(norm)
            m_ref[0] = top

        @pl.when(small)
        def plain():
            probs = []
            for i in range(parts):
                prob = jnp.exp(score(i)).astype(BF16)
                p_ref[0, starts[i] : starts[i] + rows[i], :] = prob
                probs.append(prob)
            finish(probs, jnp.zeros((1, length), F32))

        @pl.when(jnp.logical_not(small))
        def shifted():
            raw = [score(i) for i in range(parts)]
            top = jnp.max(raw[0], axis=0, keepdims=True)
            for i in range(1, parts):
                top = jnp.maximum(top, jnp.max(raw[i], axis=0, keepdims=True))
            probs = []
            for i in range(parts):
                prob = jnp.exp(raw[i] - top).astype(BF16)
                p_ref[0, starts[i] : starts[i] + rows[i], :] = prob
                probs.append(prob)
            finish(probs, top)

        @pl.when(head == heads - 1)
        def stats():
            high, low = split_low(lse_ref[...])
            for g in range(groups):
                o_ref[g, width : width + stat_rows, :] = high[:, g * tokens : (g + 1) * tokens]
                o_ref[g, width + stat_rows :, :] = low[:, g * tokens : (g + 1) * tokens]

    payload = width + 2 * stat_rows
    key_specs = [pl.BlockSpec((1, HEAD_DIM, r), lambda h: (0, h, 0)) for r in rows]
    value_specs = [pl.BlockSpec((1, HEAD_DIM, r), lambda h: (1, h, 0)) for r in rows]
    return pl.pallas_call(
        kernel,
        grid=(heads,),
        in_specs=[pl.BlockSpec((HEAD_DIM, length), lambda h: (h, 0))]
        + key_specs
        + value_specs
        + [pl.BlockSpec((16, r), lambda h: (0, 0)) for r in rows],
        out_specs=[
            pl.BlockSpec((groups, payload, tokens), lambda h: (0, 0, 0)),
            pl.BlockSpec((1, total, length), lambda h: (h, 0, 0)),
            pl.BlockSpec((1, 1, length), lambda h: (h, 0, 0)),
        ],
        out_shape=[
            jax.ShapeDtypeStruct((groups, payload, tokens), BF16),
            jax.ShapeDtypeStruct((heads, total, length), BF16),
            jax.ShapeDtypeStruct((heads, 1, length), F32),
        ],
        scratch_shapes=[pltpu.VMEM((stat_rows, length), F32)],
        compiler_params=params(),
        cost_estimate=estimate(
            flops=16 * heads * total * length * HEAD_DIM,
            bytes_accessed=2 * heads * total * length,
            transcendentals=heads * total * length,
        ),
        name="cross_forward",
    )(query, *pairs, *pairs, *bias)


def cross_backward(query, pairs, prob, place, grads, tops, earlier, width, groups):
    heads = width // HEAD_DIM
    length = query.shape[1]
    tokens = length // groups
    parts = len(pairs)
    rows = [p.shape[2] for p in pairs]
    starts = [sum(rows[:i]) for i in range(parts)]
    total = sum(rows)
    pair = 2
    stat_rows = grads.shape[1] - width
    each = stat_rows // 4

    def kernel(*refs):
        q_ref = refs[0]
        k_refs = refs[1 : 1 + parts]
        v_refs = refs[1 + parts : 1 + 2 * parts]
        p_ref, g_ref, s_ref, t_ref = refs[1 + 2 * parts : 5 + 2 * parts]
        dq_ref, dk_ref, dv_ref = refs[-3:]
        step = pl.program_id(0)
        stats = jnp.concatenate([s_ref[g] for g in range(groups)], axis=1).astype(F32)
        lse = stats[:each] + stats[each : 2 * each]
        delta = stats[2 * each : 3 * each] + stats[3 * each :]
        row = lax.broadcasted_iota(jnp.int32, (each, length), 0)
        key_out = [[] for _ in range(parts)]
        value_out = [[] for _ in range(parts)]
        for j in range(pair):
            at = slice(j * HEAD_DIM, (j + 1) * HEAD_DIM)
            grad = jnp.concatenate([g_ref[g, at, :] for g in range(groups)], axis=1).astype(F32)
            pick = lambda x: jnp.sum(
                jnp.where(row == step * pair + j, x, 0.0), axis=0, keepdims=True
            )
            scale = jnp.exp(t_ref[j] - pick(lse))
            scaled = grad * scale
            high, low = split_low(-pick(delta) * scale)
            scaled_low = scaled.astype(BF16)
            pad = jnp.zeros((14, length), BF16)
            aug = jnp.concatenate([scaled_low, high, low, pad], axis=0)
            scaled_rows = scaled.T.astype(BF16)
            query_rows = q_ref[at, :].astype(F32).T.astype(BF16)
            query_grad = None
            for i in range(parts):
                aug_value = jnp.concatenate(
                    [v_refs[i][0, at, :], jnp.ones((16, rows[i]), BF16)], axis=0
                )
                prob = p_ref[j, starts[i] : starts[i] + rows[i], :]
                score = (prob.astype(F32) * dot(aug_value, aug, 0, 0)).astype(BF16)
                value_out[i].append(dot(prob, scaled_rows, 1, 0).astype(BF16))
                key_out[i].append(dot(score, query_rows, 1, 0).astype(BF16))
                term = dot(k_refs[i][0, at, :], score, 1, 0)
                query_grad = term if query_grad is None else query_grad + term
            query_grad = query_grad * 0.125
            if earlier is not None:
                before = refs[5 + 2 * parts]
                query_grad += jnp.concatenate(
                    [before[g, at, :] for g in range(groups)], axis=1
                ).astype(F32)
            query_low = query_grad.astype(BF16)
            for g in range(groups):
                dq_ref[g, at, :] = query_low[:, g * tokens : (g + 1) * tokens]
        for i in range(parts):
            at = slice(starts[i], starts[i] + rows[i])
            dk_ref[at, :] = jnp.concatenate(key_out[i], axis=1)
            dv_ref[at, :] = jnp.concatenate(value_out[i], axis=1)

    size = pair * HEAD_DIM
    key_specs = [pl.BlockSpec((1, size, r), lambda h: (0, h, 0)) for r in rows]
    value_specs = [pl.BlockSpec((1, size, r), lambda h: (1, h, 0)) for r in rows]
    token_spec = pl.BlockSpec((groups, size, tokens), lambda h: (0, h, 0))
    row_spec = pl.BlockSpec((total, size), lambda h: (0, h))
    more = [] if earlier is None else [earlier]
    return pl.pallas_call(
        kernel,
        grid=(heads // pair,),
        in_specs=[pl.BlockSpec((size, length), lambda h: (h, 0))]
        + key_specs
        + value_specs
        + [
            pl.BlockSpec((pair, total, length), lambda h: (h, place, 0)),
            token_spec,
            pl.BlockSpec((groups, stat_rows, tokens), lambda h: (0, width // stat_rows, 0)),
            pl.BlockSpec((pair, 1, length), lambda h: (h, 0, 0)),
        ]
        + [token_spec for _ in more],
        out_specs=[token_spec, row_spec, row_spec],
        out_shape=[jax.ShapeDtypeStruct((groups, width, tokens), BF16)]
        + [jax.ShapeDtypeStruct((total, width), BF16)] * 2,
        compiler_params=params(),
        cost_estimate=estimate(
            flops=32 * heads * total * length * HEAD_DIM,
            bytes_accessed=2 * heads * total * length,
            transcendentals=0,
        ),
        name="cross_backward",
    )(query, *pairs, *pairs, prob, grads, grads, tops, *more)


def self_forward(inputs, gain, weights, key_pos, query_pos, groups):
    length, width = inputs.shape
    own = weights.shape[1]
    heads = own // HEAD_DIM

    def kernel(x_ref, g_ref, w_ref, kp_ref, qp_ref, a_ref, pr_ref, o_ref, p_ref, n_ref):
        head = pl.program_id(0)

        @pl.when(head == 0)
        def project():
            low = normed(x_ref[...].astype(F32), g_ref[...]).astype(BF16)
            a_ref[...] = low
            for c in range(3):
                pr_ref[c] = dot(w_ref[c], low, 1, 1).astype(BF16)

        at = pl.ds(pl.multiple_of(head * HEAD_DIM, HEAD_DIM), HEAD_DIM)
        raw = dot(pr_ref[1, at, :], pr_ref[0, at, :], 0, 0) * 0.125
        raw = jnp.where(kp_ref[...] <= qp_ref[...], raw, negative_fill)
        top = jnp.max(raw, axis=0, keepdims=True)
        prob = jnp.exp(raw - top).astype(BF16)
        p_ref[0] = prob
        aug_value = jnp.concatenate([pr_ref[2, at, :], jnp.ones((16, length), BF16)], axis=0)
        mixed = dot(aug_value, prob, 1, 0)
        inverse = 1.0 / mixed[HEAD_DIM : HEAD_DIM + 1]
        out = (mixed[:HEAD_DIM] * inverse).astype(BF16)
        for g in range(groups):
            o_ref[g] = out
        n_ref[0] = inverse

    whole = lambda *shape: pl.BlockSpec(shape, lambda h: (0,) * len(shape))
    return pl.pallas_call(
        kernel,
        grid=(heads,),
        in_specs=[
            whole(length, width),
            whole(1, width),
            whole(3, own, width),
            whole(length, 1),
            whole(1, length),
        ],
        out_specs=[
            whole(length, width),
            whole(3, own, length),
            pl.BlockSpec((groups, HEAD_DIM, length), lambda h: (0, h, 0)),
            pl.BlockSpec((1, length, length), lambda h: (h, 0, 0)),
            pl.BlockSpec((1, 1, length), lambda h: (h, 0, 0)),
        ],
        out_shape=[
            jax.ShapeDtypeStruct((length, width), BF16),
            jax.ShapeDtypeStruct((3, own, length), BF16),
            jax.ShapeDtypeStruct((groups, own, length), BF16),
            jax.ShapeDtypeStruct((heads, length, length), BF16),
            jax.ShapeDtypeStruct((heads, 1, length), F32),
        ],
        compiler_params=params(),
        cost_estimate=estimate(
            flops=16 * heads * length * length * HEAD_DIM,
            bytes_accessed=2 * heads * length * length,
            transcendentals=heads * length * length,
        ),
        name="self_forward",
    )(inputs, gain, weights, key_pos, query_pos)


def project_rows(pieces, weights):
    counts = [p.shape[0] for p in pieces]
    total, width = sum(counts), pieces[0].shape[1]

    def kernel(*refs):
        w_ref, out_ref = refs[len(counts) :]
        start = 0
        for e_ref, count in zip(refs, counts):
            out_ref[0, :, start : start + count] = dot(w_ref[0], e_ref[...], 1, 1).astype(BF16)
            start += count

    return pl.pallas_call(
        kernel,
        grid=(2,),
        in_specs=[pl.BlockSpec((count, width), lambda c: (0, 0)) for count in counts]
        + [pl.BlockSpec((1, width, width), lambda c: (c, 0, 0))],
        out_specs=pl.BlockSpec((1, width, total), lambda c: (c, 0, 0)),
        out_shape=jax.ShapeDtypeStruct((2, width, total), BF16),
        compiler_params=params(),
        cost_estimate=estimate(
            flops=4 * total * width * width, bytes_accessed=8 * total * width, transcendentals=0
        ),
        name="project_rows",
    )(*pieces, weights)


def query_stage(inputs, mixed, out_weight, gain, query_weight, slot, groups):
    length, width = inputs.shape
    tokens = length // groups
    rows = mixed.shape[0]

    def kernel(s_ref, x_ref, o_ref, w_ref, g_ref, q_ref, qc_ref, h_ref, a_ref):
        after = x_ref[...].astype(F32) + dot(o_ref[...], w_ref[...], 0, 0)
        low = normed(after, g_ref[...]).astype(BF16)
        scaled = dot(q_ref[...], low, 1, 1).astype(BF16)
        qc_ref[...] = (scaled.astype(F32) * 0.125).astype(BF16)

        @pl.when(pl.program_id(0) == s_ref[0])
        def keep():
            h_ref[...] = after
            a_ref[...] = low

    whole = lambda *shape: pl.BlockSpec(shape, lambda i, s: (0,) * len(shape))
    return pl.pallas_call(
        kernel,
        grid_spec=pltpu.PrefetchScalarGridSpec(
            num_scalar_prefetch=1,
            grid=(groups,),
            in_specs=[
                pl.BlockSpec((tokens, width), lambda i, s: (i, 0)),
                pl.BlockSpec((rows, tokens), lambda i, s: (0, i)),
                whole(rows, width),
                whole(1, width),
                whole(width, width),
            ],
            out_specs=[
                pl.BlockSpec((width, tokens), lambda i, s: (0, i)),
                whole(tokens, width),
                whole(tokens, width),
            ],
        ),
        out_shape=[
            jax.ShapeDtypeStruct((width, length), BF16),
            jax.ShapeDtypeStruct((tokens, width), F32),
            jax.ShapeDtypeStruct((tokens, width), BF16),
        ],
        compiler_params=params(),
        cost_estimate=estimate(
            flops=8 * length * width * width, bytes_accessed=8 * width * width, transcendentals=0
        ),
        name="query_stage",
    )(slot, inputs, mixed, out_weight, gain, query_weight)


def gelu_parts(value):
    root = 0.7978845608028654
    cubic = 0.044715
    square = value * value
    bent = jnp.tanh(root * value * (1.0 + cubic * square))
    half = 0.5 * (1.0 + bent)
    slope = half + 0.5 * value * (1.0 - bent * bent) * root * (1.0 + 3.0 * cubic * square)
    return value * half, slope


def pulled_norm(values, gain, grad):
    inverse = lax.rsqrt(jnp.mean(values * values, axis=-1, keepdims=True) + epsilon)
    scaled = values * inverse
    gain_grad = jnp.sum(grad * scaled, axis=0, keepdims=True)
    weighted = grad * gain
    back = inverse * (weighted - scaled * jnp.mean(weighted * scaled, axis=-1, keepdims=True))
    return back, gain_grad


def token_stage(parts, after_self, cross_out, gain, ffn_in, ffn_out, cotangent, groups):
    tokens, width = after_self.shape
    heads = width // HEAD_DIM
    stat_rows = (parts.shape[1] - width) // 2
    hidden = ffn_in.shape[1]
    piece = 768
    steps = hidden // piece
    payload = width + 4 * stat_rows

    def kernel(
        r_ref, h_ref, co_ref, g_ref, w1_ref, w2_ref, c_ref,
        out_ref, dh_ref, g2_ref, a_ref, z_ref, du_ref, o_ref, pay_ref, gain_ref,
        after_ref, acc_ref, back_ref, lse_ref,
    ):
        step = pl.program_id(0)

        @pl.when(step == 0)
        def join():
            lse = [
                r_ref[g, width : width + stat_rows, :].astype(F32)
                + r_ref[g, width + stat_rows :, :].astype(F32)
                for g in range(groups)
            ]
            top = functools.reduce(jnp.maximum, lse)
            share = [jnp.exp(l - top) for l in lse]
            total = functools.reduce(jnp.add, share)
            lse_ref[...] = top + jnp.log(total)
            share = [s / total for s in share]
            for h in range(heads):
                at = slice(h * HEAD_DIM, (h + 1) * HEAD_DIM)
                mixed = None
                for g in range(groups):
                    term = r_ref[g, at, :].astype(F32) * share[g][h : h + 1]
                    mixed = term if mixed is None else mixed + term
                o_ref[at, :] = mixed.astype(BF16)
            after = h_ref[...] + dot(o_ref[...], co_ref[...], 0, 0)
            after_ref[...] = after
            a_ref[...] = normed(after, g_ref[...]).astype(BF16)
            acc_ref[...] = jnp.zeros_like(acc_ref)
            back_ref[...] = jnp.zeros_like(back_ref)

        pre = dot(a_ref[...], w1_ref[...], 1, 0)
        act, slope = gelu_parts(pre)
        act = act.astype(BF16)
        z_ref[...] = act
        acc_ref[...] += dot(act, w2_ref[...], 1, 0)
        pre_grad = (dot(c_ref[...], w2_ref[...], 1, 1) * slope).astype(BF16)
        du_ref[...] = pre_grad
        back_ref[...] += dot(pre_grad, w1_ref[...], 1, 1)

        @pl.when(step == steps - 1)
        def finish():
            after = after_ref[...]
            out_ref[...] = (after + acc_ref[...]).astype(BF16)
            back, gain_grad = pulled_norm(after, g_ref[...], back_ref[...])
            gain_ref[...] = gain_grad
            grad = c_ref[...].astype(F32) + back
            dh_ref[...] = grad
            low = grad.astype(BF16)
            g2_ref[...] = low
            mix_grad = dot(co_ref[...], low, 1, 1).astype(BF16)
            both = mix_grad.astype(F32) * o_ref[...].astype(F32)
            rows = [
                jnp.sum(both[h * HEAD_DIM : (h + 1) * HEAD_DIM], axis=0, keepdims=True)
                for h in range(heads)
            ]
            rows.append(jnp.zeros((stat_rows - heads, tokens), F32))
            stats = [*split_low(lse_ref[...]), *split_low(jnp.concatenate(rows, axis=0))]
            for g in range(groups):
                pay_ref[g, :width, :] = mix_grad
                for i in range(4):
                    start = width + i * stat_rows
                    pay_ref[g, start : start + stat_rows, :] = stats[i]

    whole = lambda *shape: pl.BlockSpec(shape, lambda i: (0,) * len(shape))
    flat = lambda rows, kind: jax.ShapeDtypeStruct((rows, width), kind)
    return pl.pallas_call(
        kernel,
        grid=(steps,),
        in_specs=[
            whole(*parts.shape),
            whole(tokens, width),
            whole(width, width),
            whole(1, width),
            pl.BlockSpec((width, piece), lambda i: (0, i)),
            pl.BlockSpec((piece, width), lambda i: (i, 0)),
            whole(tokens, width),
        ],
        out_specs=[
            whole(tokens, width),
            whole(tokens, width),
            whole(tokens, width),
            whole(tokens, width),
            pl.BlockSpec((tokens, piece), lambda i: (0, i)),
            pl.BlockSpec((tokens, piece), lambda i: (0, i)),
            whole(width, tokens),
            whole(groups, payload, tokens),
            whole(1, width),
        ],
        out_shape=[
            flat(tokens, BF16),
            flat(tokens, F32),
            flat(tokens, BF16),
            flat(tokens, BF16),
            jax.ShapeDtypeStruct((tokens, hidden), BF16),
            jax.ShapeDtypeStruct((tokens, hidden), BF16),
            jax.ShapeDtypeStruct((width, tokens), BF16),
            jax.ShapeDtypeStruct((groups, payload, tokens), BF16),
            flat(1, F32),
        ],
        scratch_shapes=[pltpu.VMEM((tokens, width), F32)] * 3
        + [pltpu.VMEM((stat_rows, tokens), F32)],
        compiler_params=params(),
        cost_estimate=estimate(
            flops=8 * tokens * width * hidden,
            bytes_accessed=4 * width * hidden,
            transcendentals=tokens * hidden,
        ),
        name="token_stage",
    )(parts, after_self, cross_out, gain, ffn_in, ffn_out, cotangent)


def early_weight_grads(low, pre_grad, act, cotangent, mixed, mixed_grad, columns, blocks):
    tokens, width = low.shape
    hidden = act.shape[1]
    step_size = hidden // blocks
    size, piece = width // blocks, width // columns
    half = step_size // 2

    def kernel(a_ref, du_ref, z_ref, c_ref, m_ref, g_ref, out_ref):
        step = pl.program_id(0)
        first = dot(a_ref[...], du_ref[...], 0, 0).astype(BF16)
        for p in range(2):

            @pl.when(lax.rem(step, 2) == p)
            def put():
                for b in range(blocks):
                    out_ref[step // 2, b, p * size : (p + 1) * size, :] = first[
                        b * size : (b + 1) * size
                    ]

        second = dot(z_ref[...], c_ref[...], 0, 0).astype(BF16)
        for d in range(columns):
            at = slice(d * piece, (d + 1) * piece)
            out_ref[d, step, 2 * size : 2 * size + half, :] = jnp.concatenate(
                [second[:half, at], second[half:, at]], axis=1
            )
        third = dot(m_ref[...], g_ref[...], 1, 0).astype(BF16)
        for d in range(columns):
            at = slice(d * piece, (d + 1) * piece)
            out_ref[d, step, 2 * size + half :, :] = jnp.concatenate(
                [third[: size // 2, at], third[size // 2 :, at]], axis=1
            )

    shape = (columns, blocks, 2 * size + half + size // 2, 2 * piece)
    whole = lambda *shape: pl.BlockSpec(shape, lambda i: (0,) * len(shape))
    return pl.pallas_call(
        kernel,
        grid=(blocks,),
        in_specs=[
            whole(tokens, width),
            pl.BlockSpec((tokens, step_size), lambda i: (0, i)),
            pl.BlockSpec((tokens, step_size), lambda i: (0, i)),
            whole(tokens, width),
            pl.BlockSpec((size, tokens), lambda i: (i, 0)),
            whole(tokens, width),
        ],
        out_specs=whole(*shape),
        out_shape=jax.ShapeDtypeStruct(shape, BF16),
        compiler_params=params(),
        cost_estimate=estimate(
            flops=4 * tokens * width * hidden,
            bytes_accessed=4 * width * hidden,
            transcendentals=0,
        ),
        name="early_weight_grads",
    )(low, pre_grad, act, cotangent, mixed, mixed_grad)


def mixed_stage(parts, cross_q, after_self, gain, cross_grad, self_out, groups, own):
    tokens, width = after_self.shape
    rows = self_out.shape[0]

    def kernel(r_ref, q_ref, h_ref, g_ref, dh_ref, w_ref, dq_ref, out_ref, g1_ref, do_ref, gain_ref):
        total = r_ref[0].astype(F32)
        for g in range(1, groups):
            total = total + r_ref[g].astype(F32)
        query_grad = total.astype(BF16)
        dq_ref[...] = query_grad
        back, gain_grad = pulled_norm(h_ref[...], g_ref[...], dot(query_grad, q_ref[...], 0, 1))
        gain_ref[...] = gain_grad
        grad = dh_ref[...] + back
        out_ref[...] = grad
        low = grad.astype(BF16)
        g1_ref[...] = low
        mixed = dot(w_ref[...], low, 1, 1).astype(BF16)
        for g in range(groups):
            do_ref[g] = mixed[g * own : (g + 1) * own]

    return pl.pallas_call(
        kernel,
        out_shape=[
            jax.ShapeDtypeStruct((width, tokens), BF16),
            jax.ShapeDtypeStruct((tokens, width), F32),
            jax.ShapeDtypeStruct((tokens, width), BF16),
            jax.ShapeDtypeStruct((groups, own, tokens), BF16),
            jax.ShapeDtypeStruct((1, width), F32),
        ],
        compiler_params=params(),
        cost_estimate=estimate(
            flops=4 * tokens * width * width, bytes_accessed=8 * width * width, transcendentals=0
        ),
        name="mixed_stage",
    )(parts, cross_q, after_self, gain, cross_grad, self_out)


def input_stage(back, weights, inputs, gain, self_grad, slot, groups):
    own, tokens = back.shape[2:]
    width = inputs.shape[1]
    padded = groups * own

    def kernel(s_ref, b_ref, w_ref, x_ref, g_ref, h_ref, out_ref, acc_ref):
        step = pl.program_id(0)
        grads = jnp.concatenate([b_ref[g, 0] for g in range(groups)], axis=0)
        term = dot(grads, w_ref[0], 0, 1)

        @pl.when(step == 0)
        def first():
            acc_ref[...] = term

        @pl.when(step > 0)
        def more():
            acc_ref[...] += term

        @pl.when(step == 2)
        def last():
            back, unused = pulled_norm(x_ref[...].astype(F32), g_ref[...], acc_ref[...])
            out_ref[...] = (h_ref[...] + back).astype(BF16)

    whole = lambda *shape: pl.BlockSpec(shape, lambda i, s: (0,) * len(shape))
    return pl.pallas_call(
        kernel,
        grid_spec=pltpu.PrefetchScalarGridSpec(
            num_scalar_prefetch=1,
            grid=(3,),
            in_specs=[
                pl.BlockSpec((groups, 1, own, tokens), lambda i, s: (0, i, 0, 0)),
                pl.BlockSpec((1, width, padded), lambda i, s: (i, 0, 0)),
                pl.BlockSpec((tokens, width), lambda i, s: (s[0], 0)),
                whole(1, width),
                whole(tokens, width),
            ],
            out_specs=whole(tokens, width),
            scratch_shapes=[pltpu.VMEM((tokens, width), F32)],
        ),
        out_shape=jax.ShapeDtypeStruct((tokens, width), BF16),
        compiler_params=params(),
        cost_estimate=estimate(
            flops=6 * tokens * width * width, bytes_accessed=6 * width * width, transcendentals=0
        ),
        name="input_stage",
    )(slot, back, weights, inputs, gain, self_grad)


def both_queries(own, pieces, mine):
    rows, width = own.shape

    def kernel(s_ref, own_ref, *refs):
        out_ref = refs[-1]

        @pl.when(pl.program_id(0) == s_ref[0])
        def here():
            out_ref[0] = own_ref[...]

        @pl.when(pl.program_id(0) != s_ref[0])
        def there():
            start = 0
            for ref in refs[:-1]:
                out_ref[0, start : start + ref.shape[0], :] = ref[...]
                start += ref.shape[0]

    whole = lambda *shape: pl.BlockSpec(shape, lambda i, s: (0,) * len(shape))
    return pl.pallas_call(
        kernel,
        grid_spec=pltpu.PrefetchScalarGridSpec(
            num_scalar_prefetch=1,
            grid=(2,),
            in_specs=[whole(*own.shape)] + [whole(*p.shape) for p in pieces],
            out_specs=pl.BlockSpec((1, rows, width), lambda i, s: (i, 0, 0)),
        ),
        out_shape=jax.ShapeDtypeStruct((2, rows, width), own.dtype),
        compiler_params=params(),
        cost_estimate=estimate(flops=0, bytes_accessed=8 * rows * width, transcendentals=0),
        name="both_queries",
    )(mine, own, *pieces)


def own_weight_grads(low, gain, grads, weights, column, columns, blocks):
    length, width = low.shape
    groups, _, own, tokens = grads.shape
    rows = width // blocks
    per = blocks // columns

    def kernel(c_ref, a_ref, g_ref, d_ref, w_ref, *refs):
        gain_ref = refs[-1]
        step = pl.program_id(0)
        grads = jnp.concatenate([d_ref[g, 0] for g in range(groups)], axis=1)
        turned = dot(grads, a_ref[...], 1, 0)
        weight = turned.T.astype(BF16)
        for d in range(columns):

            @pl.when(c_ref[0] == d)
            def put():
                for b in range(blocks):
                    refs[b // per ^ d][b % per, 0] = weight[b * rows : (b + 1) * rows]

        term = jnp.sum(turned * w_ref[0].astype(F32), axis=0, keepdims=True) / g_ref[...]

        @pl.when(step == 0)
        def first():
            gain_ref[...] = term

        @pl.when(step > 0)
        def more():
            gain_ref[...] += term

    shape = (per, 3, rows, own)
    whole = lambda *shape: pl.BlockSpec(shape, lambda i, c: (0,) * len(shape))
    part = pl.BlockSpec((per, 1, rows, own), lambda i, c: (0, i, 0, 0))
    return pl.pallas_call(
        kernel,
        grid_spec=pltpu.PrefetchScalarGridSpec(
            num_scalar_prefetch=1,
            grid=(3,),
            in_specs=[
                whole(length, width),
                whole(1, width),
                pl.BlockSpec((groups, 1, own, tokens), lambda i, c: (0, i, 0, 0)),
                pl.BlockSpec((1, own, width), lambda i, c: (i, 0, 0)),
            ],
            out_specs=[part] * columns + [whole(1, width)],
        ),
        out_shape=[jax.ShapeDtypeStruct(shape, BF16)] * columns
        + [jax.ShapeDtypeStruct((1, width), F32)],
        compiler_params=params(),
        cost_estimate=estimate(
            flops=12 * length * width * own, bytes_accessed=4 * length * width, transcendentals=0
        ),
        name="own_weight_grads",
    )(column, low, gain, grads, weights)


def sums_for(pairs, groups):
    blocks, _, width = pairs[0][0].shape
    rows = [k.shape[1] for k, _ in pairs]
    high = blocks // groups

    def kernel(*refs):
        out_ref = refs[-1]
        start = 0
        for i, size in enumerate(rows):
            both = refs[2 * i][...].astype(F32) + refs[2 * i + 1][...].astype(F32)
            both = both.astype(BF16)
            for b in range(blocks):
                out_ref[b % groups, b // groups, start : start + size, :] = both[b]
            start += size

    return pl.pallas_call(
        kernel,
        out_shape=jax.ShapeDtypeStruct((groups, high, sum(rows), width), BF16),
        compiler_params=params(),
        cost_estimate=estimate(flops=0, bytes_accessed=0, transcendentals=0),
        name="sums_for",
    )(*[array for pair in pairs for array in pair])


def sums_of(lists, bit):
    arrays = [array for one in lists for array in one]

    def kernel(s_ref, *refs):
        start = 0
        for i, one in enumerate(lists):
            for side in range(2):
                terms = [refs[2 * (start + n) + side][0].astype(F32) for n in range(len(one))]
                total = functools.reduce(jnp.add, terms)
                refs[2 * (len(arrays) + i) + side][...] = total.astype(BF16)
            start += len(one)

    def spec(array, side):
        return pl.BlockSpec((1,) + array.shape[1:], lambda j, s: ((s[0] + side) % 2, 0, 0))

    outs = pl.pallas_call(
        kernel,
        grid_spec=pltpu.PrefetchScalarGridSpec(
            num_scalar_prefetch=1,
            grid=(1,),
            in_specs=[spec(array, side) for array in arrays for side in range(2)],
            out_specs=[
                pl.BlockSpec(one[0].shape[1:], lambda j, s: (0, 0)) for one in lists for _ in range(2)
            ],
        ),
        out_shape=[
            jax.ShapeDtypeStruct(one[0].shape[1:], BF16) for one in lists for _ in range(2)
        ],
        compiler_params=params(),
        cost_estimate=estimate(flops=0, bytes_accessed=0, transcendentals=0),
        name="sums_of",
    )(bit, *[array for array in arrays for _ in range(2)])
    return list(zip(outs[::2], outs[1::2]))


def self_backward(projected, mixed, grads, prob, weight, groups):
    own, length = projected.shape[1:]
    heads = own // HEAD_DIM
    tokens = length // groups

    def kernel(q_ref, k_ref, v_ref, o_ref, g_ref, p_ref, w_ref, out_ref):
        grad = jnp.concatenate([g_ref[g] for g in range(groups)], axis=1).astype(F32)
        scaled = grad * w_ref[0]
        high, low = split_low(-jnp.sum(scaled * o_ref[0].astype(F32), axis=0, keepdims=True))
        scaled_low = scaled.astype(BF16)
        aug = jnp.concatenate([scaled_low, high, low, jnp.zeros((14, length), BF16)], axis=0)
        aug_value = jnp.concatenate([v_ref[0], jnp.ones((16, length), BF16)], axis=0)
        prob = p_ref[0]
        score = (prob.astype(F32) * dot(aug_value, aug, 0, 0)).astype(BF16)
        results = (
            dot(k_ref[0], score, 1, 0) * 0.125,
            dot(q_ref[0], score, 1, 1) * 0.125,
            dot(scaled_low, prob, 1, 1),
        )
        for c in range(3):
            result = results[c].astype(BF16)
            for g in range(groups):
                out_ref[g, c] = result[:, g * tokens : (g + 1) * tokens]

    spec = lambda c: pl.BlockSpec((1, HEAD_DIM, length), lambda h: (c, h, 0))
    return pl.pallas_call(
        kernel,
        grid=(heads,),
        in_specs=[
            spec(0),
            spec(1),
            spec(2),
            pl.BlockSpec((1, HEAD_DIM, length), lambda h: (0, h, 0)),
            pl.BlockSpec((groups, HEAD_DIM, tokens), lambda h: (0, h, 0)),
            pl.BlockSpec((1, length, length), lambda h: (h, 0, 0)),
            pl.BlockSpec((1, 1, length), lambda h: (h, 0, 0)),
        ],
        out_specs=pl.BlockSpec((groups, 3, HEAD_DIM, tokens), lambda h: (0, 0, h, 0)),
        out_shape=jax.ShapeDtypeStruct((groups, 3, own, tokens), BF16),
        compiler_params=params(),
        cost_estimate=estimate(
            flops=32 * heads * length * length * HEAD_DIM,
            bytes_accessed=2 * heads * length * length,
            transcendentals=0,
        ),
        name="self_backward",
    )(projected, projected, projected, mixed, grads, prob, weight)


def body(
    dec_input,
    enc_output,
    lengths,
    gains,
    self_qkv,
    self_out,
    cross_q,
    cross_kv,
    cross_out,
    ffn_in,
    ffn_out,
    cotangent,
):
    seg, seqs, width = dec_input.shape
    heads = width // HEAD_DIM
    blocks = lax.axis_size("blk")
    place = lax.axis_index("blk")
    groups = blocks // seqs
    mine = place // groups
    slot_of = lax.rem(place, groups)
    members = [[s * groups + g for g in range(groups)] for s in range(seqs)]
    own_heads = -(-heads // groups)
    own = own_heads * HEAD_DIM
    padded = own * groups
    tokens = seqs * seg
    length = groups * tokens
    enc_rows = enc_output.shape[1]
    columns = lax.axis_size("dp")
    gain_rows = gains.astype(F32)[:, None, :]

    def shifted(step):
        return [(b, (b + step * groups) % blocks) for b in range(blocks)]

    def exchange(pieces):
        parts = [pieces(mine)]
        for step in range(1, seqs):
            parts.append(lax.ppermute(pieces(lax.rem(mine + step, seqs)), "blk", shifted(step)))
        return parts

    def in_order(parts):
        ordered = []
        for s in range(seqs):
            choice = parts[0]
            for step in range(1, seqs):
                from_there = lax.rem(mine - step + seqs, seqs) == s
                choice = jnp.where(from_there, parts[step], choice)
            ordered.append(choice)
        return ordered

    def spread(array):
        return lax.all_to_all(
            jnp.broadcast_to(array[None], (groups,) + array.shape),
            "blk",
            0,
            0,
            axis_index_groups=members,
        )

    def traded(array):
        return lax.all_to_all(array, "blk", 0, 0, axis_index_groups=members)

    def gathered(array):
        by_query = lax.optimization_barrier(array.swapaxes(0, 1))
        take = lambda s: lax.dynamic_index_in_dim(by_query, s, 0, False)
        return jnp.concatenate(in_order(exchange(take)), axis=0)

    def leaving(array):
        split = array.reshape(seqs, seg, width)
        return exchange(lambda s: lax.dynamic_index_in_dim(split, s, 0, False))

    def returned(parts):
        return jnp.stack(in_order(parts), axis=1)

    own_inputs = gathered(dec_input)
    all_inputs = spread(own_inputs).reshape(length, width)

    pick = lambda s: lax.dynamic_index_in_dim(enc_output, s, 0, False)
    cuts = [max(enc_rows * 3 // 7 // 128 * 128, 128)]
    cuts.append(cuts[0] + 128)
    spans = [(0, 0, enc_rows)]
    arrived = []
    for step in range(1, seqs):
        sent = pick(lax.rem(mine + step, seqs))
        arrived.append([lax.ppermute(sent[: cuts[0]], "blk", shifted(step))])
        spans += [(step, 0, cuts[0]), (step, cuts[0], enc_rows)]
        for start, stop in ((cuts[0], cuts[1]), (cuts[1], enc_rows)):
            piece, unused = lax.optimization_barrier((sent[start:stop], arrived[-1][-1]))
            arrived[-1].append(lax.ppermute(piece, "blk", shifted(step)))
    own_rows_low = pick(mine)
    turned_kv = cross_kv.swapaxes(1, 2)
    first_pair = project_rows([own_rows_low], turned_kv)
    all_inputs, first_pair, firsts = lax.optimization_barrier(
        (all_inputs, first_pair, [a[0] for a in arrived])
    )

    row_lengths = lax.dynamic_index_in_dim(lengths, mine, 0, False)
    bias = []
    for step, start, stop in spans:
        source = lax.rem(place - step * groups + blocks, blocks)
        slot = source * enc_rows + jnp.arange(start, stop)
        match = (slot // SLOTS)[:, None] == jnp.arange(lengths.shape[1])[None, :]
        filled = jnp.sum(jnp.where(match, row_lengths[None, :], 0), axis=-1)
        row = jnp.where((slot % SLOTS) < filled, 0.0, negative_fill).astype(BF16)
        bias.append(jnp.concatenate([row[None], jnp.zeros((15, stop - start), BF16)], axis=0))

    extra = [(0, 0), (0, 0), (0, padded - width)]
    padded_qkv = jnp.pad(self_qkv, extra)
    own_qkv = lax.dynamic_slice_in_dim(padded_qkv, slot_of * own, own, 2).swapaxes(1, 2)
    padded_out = jnp.pad(self_out, [(0, padded - width), (0, 0)])
    index = jnp.arange(length)
    block = index // seg
    position = ((block % seqs) * groups + block // seqs) * seg + index % seg
    position = position.astype(jnp.int32)
    first_low, projected, sent_mix, self_prob, self_weight = self_forward(
        all_inputs,
        gain_rows[0],
        own_qkv,
        position[:, None],
        position[None, :],
        groups,
    )
    sent_mix, seconds = lax.optimization_barrier((sent_mix, [a[1] for a in arrived]))
    self_mix = traded(sent_mix).reshape(padded, length)
    slot = jnp.full((1,), slot_of, jnp.int32)
    cross_query, after_self, second_low = query_stage(
        all_inputs, self_mix, padded_out, gain_rows[1], cross_q.T, slot, groups
    )

    cross_query, thirds = lax.optimization_barrier((cross_query, [a[2] for a in arrived]))
    pairs = [first_pair]
    came = []
    for first, second, third in zip(firsts, seconds, thirds):
        pairs.append(project_rows([first], turned_kv))
        pairs.append(project_rows([second, third], turned_kv))
        came += [first, second, third]

    part_mix, cross_prob, local_top = cross_forward(cross_query, pairs, bias, width, groups)

    own_cotangent = gathered(cotangent)
    (
        own_output,
        cross_grad,
        cross_grad_low,
        third_low,
        hidden_low,
        pre_low,
        cross_mix,
        payload,
        gain_three,
    ) = token_stage(
        traded(part_mix),
        after_self,
        cross_out,
        gain_rows[2],
        ffn_in,
        ffn_out,
        own_cotangent,
        groups,
    )
    packed = traded(payload)

    def by_rows(grad):
        return grad.astype(BF16).reshape(blocks, columns, -1, grad.shape[-1]).swapaxes(0, 1)

    def placed(rows, counts):
        count, full = rows.shape
        split = rows.reshape(count, columns, full // columns).swapaxes(0, 1)
        moved = lax.all_to_all(split, "dp", 0, 0).astype(F32)
        ends = [sum(counts[: i + 1]) for i in range(len(counts) - 1)]
        return [p.reshape(-1, full // columns) for p in jnp.split(moved, ends, axis=1)]

    unit = width // blocks // columns
    staged = (
        padded == width
        and columns * own == width
        and columns * seqs == blocks
        and columns % 2 == 0
        and ffn_in.shape[1] == columns * width
        and ffn_in.shape[1] // blocks * columns == 2 * width
        and blocks == 8
    )
    if staged:
        chunks = early_weight_grads(
            third_low,
            pre_low,
            hidden_low,
            own_cotangent,
            cross_mix,
            cross_grad_low,
            columns,
            blocks,
        )
        packed, chunks, own_output = lax.optimization_barrier((packed, chunks, own_output))
        inner = chunks.shape[2:]
        hidden = lax.psum_scatter(
            chunks.reshape(-1, inner[1]), "dp", scatter_dimension=0, tiled=True
        )
    else:
        in_chunks = dot(third_low, pre_low, 0, 0).astype(BF16)
        in_chunks = in_chunks.reshape(blocks, width // blocks, columns, -1).transpose(2, 0, 1, 3)
        out_chunks = by_rows(dot(hidden_low, own_cotangent, 0, 0))
    together = lambda *values: lax.optimization_barrier(values)

    output_parts = leaving(own_output)

    def rows_backward(place, subset, earlier):
        return cross_backward(
            cross_query, subset, cross_prob, place, packed, local_top, earlier, width, groups
        )

    shares = [0, 11, 19, 23, 28]
    marks = [enc_rows * share // 28 for share in shares]
    part_grads, came_key, came_value = rows_backward(1, pairs[1:], None)
    pieces = row_grads(came_key, came_value, cross_kv, marks)

    def sent_back(piece):
        return lax.ppermute(piece, "blk", shifted(1))

    part_grads, pieces, output_parts = together(part_grads, pieces, output_parts)
    back_1 = sent_back(pieces[0])
    query_parts, own_key, own_value = rows_backward(0, pairs[:1], part_grads)
    key_low, value_low = [own_key, came_key], [own_value, came_value]
    query_parts, key_low, value_low, back_1, pieces = together(
        query_parts, key_low, value_low, back_1, pieces
    )
    joined = traded(query_parts)
    here = jnp.full((1,), mine, jnp.int32)

    def moved(array, axis, step):
        size = lax.axis_size(axis)
        return lax.ppermute(array, axis, [(i, i ^ step) for i in range(size)])

    def bit_of(axis, step):
        return jnp.full((1,), lax.rem(lax.axis_index(axis) // step, 2), jnp.int32)

    def chunks_of(kernel_dots, operands, specs):
        return weight_chunks(
            kernel_dots, operands, specs, bit_of("dp", 1), slot, columns, blocks, width
        )

    back_2 = sent_back(pieces[1])
    output = returned(output_parts)
    if staged:
        cuts = [0]
        for piece in came:
            cuts.append(cuts[-1] + piece.shape[0])

        def rows_dot(grad):
            def one(refs):
                total = dot(refs[0][...], refs[grad][...], 0, 0)
                for i, (start, stop) in enumerate(zip(cuts, cuts[1:])):
                    total += dot(refs[1 + i][...], refs[grad + 1][start:stop, :], 0, 0)
                return total

            return one

        count = 1 + len(came)
        operands = [own_rows_low, *came, *key_low, *value_low]
        kept_1, sent_1 = chunks_of(
            [
                rows_dot(count),
                rows_dot(count + 2),
            ],
            operands,
            [None] * len(operands),
        )
        joined, pieces, back_2, output, hidden, kept_1, sent_1 = together(
            joined, pieces, back_2, output, hidden, kept_1, sent_1
        )
        hidden = lax.psum_scatter(hidden, "blk", scatter_dimension=0, tiled=True)
        got_1 = moved(sent_1, "dp", 1)
    query_grad, self_grad, self_grad_low, mixed_grad, gain_two = mixed_stage(
        joined, cross_q, after_self, gain_rows[1], cross_grad, padded_out, groups, own
    )
    if staged:
        query_grad, self_grad, self_grad_low, mixed_grad, gain_two, kept_1, got_1, pieces = (
            together(
                query_grad, self_grad, self_grad_low, mixed_grad, gain_two, kept_1, got_1, pieces
            )
        )
    own_mixed = traded(mixed_grad)
    if staged:
        back_3 = sent_back(pieces[2])
        kept_1, sent_1 = fold([(kept_1, got_1)], bit_of("dp", 2), blocks)
        operands = [second_low, query_grad, self_mix, self_grad_low]
        specs = [None] * 2
        specs += [pl.BlockSpec((width, tokens), lambda i, c, n: (0, n[0])), None]
        kept_2, sent_2 = chunks_of(
            [
                lambda refs: dot(refs[0][...], refs[1][...], 0, 1),
                lambda refs: dot(refs[2][...], refs[3][...], 1, 0),
            ],
            operands,
            specs,
        )
        own_mixed, back_3, kept_1, sent_1, kept_2, sent_2, pieces = together(
            own_mixed, back_3, kept_1, sent_1, kept_2, sent_2, pieces
        )
        got_1 = moved(sent_1, "dp", 2)
        got_2 = moved(sent_2, "dp", 1)
    own_grads = self_backward(projected, sent_mix, own_mixed, self_prob, self_weight, groups)
    if staged:
        own_grads, kept_2, got_2, pieces = together(own_grads, kept_2, got_2, pieces)
    back = traded(own_grads)
    if staged:
        back_4 = sent_back(pieces[3])
        kept_2, sent_2 = fold([(kept_2, got_2)], bit_of("dp", 2), blocks)
        got_2 = moved(sent_2, "dp", 2)
        *parts_w, gain_one = own_weight_grads(
            first_low,
            gain_rows[0],
            own_grads,
            own_qkv,
            jnp.full((1,), lax.axis_index("dp"), jnp.int32),
            columns,
            blocks,
        )
        gains = jnp.concatenate([gain_one, gain_two, gain_three], axis=0)
        gains = gains + moved(gains, "dp", 1)
        gains = gains + moved(gains, "dp", 2)
        back, back_4, kept_1, got_1, kept_2, got_2, parts_w, gains, key_low = together(
            back, back_4, kept_1, got_1, kept_2, got_2, parts_w, gains, key_low
        )
    own_grad = input_stage(back, padded_qkv, all_inputs, gain_rows[0], self_grad, slot, groups)
    if staged:
        own_grad, key_low = together(own_grad, key_low)
    dec_parts = leaving(own_grad)
    if staged:
        late = traded(sums_for([(kept_1, got_1), (kept_2, got_2)], groups))
        parts_w = [parts_w[0]] + [moved(p, "dp", r) for r, p in enumerate(parts_w) if r]
        gains_got = moved(gains, "blk", 1)
        (enc_own,) = row_grads(key_low[0], value_low[0], cross_kv, [0, enc_rows])
        enc_grad = both_queries(enc_own, [back_1, back_2, back_3, back_4], here)
        dec_parts, late, parts_w, gains, gains_got, enc_grad = together(
            dec_parts, late, parts_w, gains, gains_got, enc_grad
        )
        gains = gains + gains_got
    if staged:
        (kept_j, sent_j), halves = sums_of(
            [[late[g] for g in range(groups)], [p.reshape(seqs, -1, own) for p in parts_w]], here
        )
        got_j = moved(sent_j, "blk", groups)
        got_w = []
        for step, piece in enumerate(halves):
            pairs = []
            for b in range(blocks):
                row = (b // groups + step) % seqs
                for d in range(columns):
                    pairs.append((b * columns + d, (d * seqs + row) * columns + b % groups))
            piece = piece.reshape(3, width // blocks, own)
            got_w.append(lax.ppermute(piece, ("blk", "dp"), pairs))
        gains = gains + moved(gains, "blk", 2)
        dec_grad = returned(dec_parts)
        dec_grad, kept_j, got_j, got_w, gains = together(dec_grad, kept_j, got_j, got_w, gains)
        gain_grads = gains + moved(gains, "blk", 4)
        qkv = sum(piece.astype(F32) for piece in got_w)
        ffn_in_own, ffn_out_own, kv_own, cross_out_own, cross_q_own, self_out_own = unpacked(
            hidden, (kept_j, got_j), width // blocks, width // columns
        )
    else:
        rest = sent_back(jnp.concatenate(pieces[2:], axis=0))
        (enc_own,) = row_grads(key_low[0], value_low[0], cross_kv, [0, enc_rows])
        enc_grad = both_queries(enc_own, [back_1, back_2, rest], here)
        own_rows = lambda array: lax.dynamic_slice_in_dim(array, slot_of * tokens, tokens, 0)
        full = back.transpose(1, 0, 2, 3).reshape(3, padded, tokens)[:, :width]
        first_back = sum(dot(full[c], self_qkv[c], 0, 1) for c in range(3))
        unused, gain_one = pulled_norm(
            own_rows(all_inputs).astype(F32), gain_rows[0], first_back
        )
        gains = jnp.concatenate([gain_one, gain_two, gain_three], axis=0)
        gain_grads = total_of(total_of(gains, "dp"), "blk")
        dec_grad = returned(dec_parts)
        reduced = lambda array: halved(halved(array, "dp", 0), "blk", 0)
        own_first = own_rows(first_low)
        own_self_mix = lax.dynamic_slice_in_dim(self_mix, slot_of * tokens, tokens, 1)
        encoded = [own_rows_low, jnp.concatenate(came, axis=0)]
        late = [
            sum(dot(e, g, 0, 0) for e, g in zip(encoded, key_low)),
            sum(dot(e, g, 0, 0) for e, g in zip(encoded, value_low)),
            dot(cross_mix, cross_grad_low, 1, 0),
            dot(second_low, query_grad, 0, 1),
            dot(own_self_mix[:width], self_grad_low, 1, 0),
        ] + [dot(own_first, full[c], 0, 1) for c in range(3)]
        chunks = [out_chunks] + [by_rows(grad) for grad in late]
        counts = [out_chunks.shape[2]] + [unit] * 8
        rows = placed(reduced(jnp.concatenate(chunks, axis=2)), counts)
        ffn_out_own, key_own, value_own, cross_out_own, cross_q_own, self_out_own = rows[:6]
        kv_own = jnp.stack([key_own, value_own])
        qkv = jnp.stack(rows[6:])
        ffn_in_own = reduced(in_chunks).astype(F32)

    return (
        output,
        dec_grad,
        enc_grad,
        gain_grads,
        qkv,
        self_out_own,
        cross_q_own,
        kv_own,
        cross_out_own,
        ffn_in_own,
        ffn_out_own,
    )


def solution(mesh):
    placed = (
        P("blk", "dp", None),
        P("dp", "blk", None),
        P("dp", None),
        P(),
        P(),
        P(),
        P(),
        P(),
        P(),
        P(),
        P(),
        P("blk", "dp", None),
    )
    return jax.shard_map(
        body,
        mesh=mesh,
        in_specs=placed,
        out_specs=(
            P("blk", "dp", None),
            P("blk", "dp", None),
            P("dp", "blk", None),
            P(),
            P(None, "blk", "dp"),
            P("blk", "dp"),
            P("blk", "dp"),
            P(None, "blk", "dp"),
            P("blk", "dp"),
            P("blk", "dp"),
            P("blk", "dp"),
        ),
        check_vma=False,
    )
```

```python
import functools

import jax
import jax.numpy as jnp
from jax import lax
from jax.experimental import pallas as pl
from jax.experimental.pallas import tpu as pltpu
from jax.sharding import PartitionSpec as P

HEAD_DIM = 64
SLOTS = 448
F32 = jnp.float32
BF16 = jnp.bfloat16
epsilon = 1e-06
negative_fill = -1e30
safe_score = 60.0
VMEM_LIMIT = 60 * 1024 * 1024


def dot(left, right, left_dim, right_dim):
    return lax.dot_general(
        left, right, (((left_dim,), (right_dim,)), ((), ())), preferred_element_type=F32
    )


def split_low(value):
    high = value.astype(BF16)
    return high, (value - high.astype(F32)).astype(BF16)


def normed(values, gain):
    return values * lax.rsqrt(jnp.mean(values * values, axis=-1, keepdims=True) + epsilon) * gain


def parted(array, axis, dim):
    size = lax.axis_size(axis)
    shape = array.shape
    above = size // shape[dim]
    split = array.reshape(shape[:dim] + (shape[dim] // 2, 2) + shape[dim + 1 :])
    bit = lax.rem(lax.axis_index(axis) // above, 2)
    kept = lax.dynamic_index_in_dim(split, bit, dim + 1, False)
    sent = lax.dynamic_index_in_dim(split, 1 - bit, dim + 1, False)
    return kept, sent, [(i, i ^ above) for i in range(size)]


def added(kept, got):
    return (kept.astype(F32) + got.astype(F32)).astype(BF16)


def fold(pairs, bit, low):
    count, _, width = pairs[0][0].shape
    rows = [k.shape[1] for k, _ in pairs]
    high, total = count // 2 // low, sum(rows)

    def kernel(s_ref, *refs):
        start = 0
        for i, size in enumerate(rows):
            for side in range(2):
                kept, got = refs[4 * i + 2 * side], refs[4 * i + 2 * side + 1]
                both = kept[...].astype(F32) + got[...].astype(F32)
                refs[4 * len(rows) + side][:, start : start + size, :] = both.reshape(
                    high * low, size, width
                ).astype(BF16)
            start += size

    def spec(size, side):
        return pl.BlockSpec(
            (high, 1, low, size, width), lambda j, s: (0, (s[0] + side) % 2, 0, 0, 0)
        )

    split = lambda array: array.reshape(high, 2, low, array.shape[1], width)
    out = pl.BlockSpec((high * low, total, width), lambda j, s: (0, 0, 0))
    return pl.pallas_call(
        kernel,
        grid_spec=pltpu.PrefetchScalarGridSpec(
            num_scalar_prefetch=1,
            grid=(1,),
            in_specs=[spec(size, side) for size in rows for side in range(2) for _ in range(2)],
            out_specs=[out] * 2,
        ),
        out_shape=[jax.ShapeDtypeStruct((high * low, total, width), BF16)] * 2,
        compiler_params=params(),
        cost_estimate=estimate(flops=0, bytes_accessed=0, transcendentals=0),
        name="fold",
    )(bit, *[split(array) for k, g in pairs for array in (k, g, k, g)])


def weight_chunks(kernel_dots, operands, specs, core, slot, columns, blocks, width):
    number = len(kernel_dots)
    size, piece = width // blocks, width // columns
    rows = number // 2 * size + number % 2 * size // 2
    shape = (columns // 2 * blocks, rows, 2 * piece)

    def kernel(c_ref, n_ref, *refs):
        kept_ref, sent_ref = refs[-2:]
        grads = [one(refs[:-2]).astype(BF16) for one in kernel_dots]

        def chunk(b, d):
            cut = lambda g, start, stop: g[
                b * size + start : b * size + stop, d * piece : (d + 1) * piece
            ]
            sides = [
                jnp.concatenate([cut(g, 0, size), cut(h, 0, size)], axis=1)
                for g, h in zip(grads[::2], grads[1::2])
            ]
            if number % 2:
                g = grads[-1]
                sides.append(
                    jnp.concatenate([cut(g, 0, size // 2), cut(g, size // 2, size)], axis=1)
                )
            return sides[0] if len(sides) == 1 else jnp.concatenate(sides, axis=0)

        for bit in range(2):

            @pl.when(c_ref[0] == bit)
            def put():
                for b in range(blocks):
                    for d in range(columns):
                        ref = kept_ref if d % 2 == bit else sent_ref
                        ref[d // 2 * blocks + b] = chunk(b, d)

    whole = lambda *shape: pl.BlockSpec(shape, lambda i, c, n: (0,) * len(shape))
    in_specs = [spec or whole(*array.shape) for array, spec in zip(operands, specs)]
    return pl.pallas_call(
        kernel,
        grid_spec=pltpu.PrefetchScalarGridSpec(
            num_scalar_prefetch=2,
            grid=(1,),
            in_specs=in_specs,
            out_specs=[whole(*shape)] * 2,
        ),
        out_shape=[jax.ShapeDtypeStruct(shape, BF16)] * 2,
        compiler_params=params(),
        cost_estimate=estimate(flops=0, bytes_accessed=0, transcendentals=0),
        name="weight_chunks",
    )(core, slot, *operands)


def row_grads(keys, values, weights, marks):
    rows, width = keys.shape
    sizes = [b - a for a, b in zip(marks, marks[1:])]

    def kernel(k_ref, v_ref, w_ref, *out_refs):
        total = dot(k_ref[...], w_ref[0], 1, 1) + dot(v_ref[...], w_ref[1], 1, 1)
        for ref, start, size in zip(out_refs, marks, sizes):
            ref[...] = total[start : start + size].astype(BF16)

    return pl.pallas_call(
        kernel,
        out_shape=[jax.ShapeDtypeStruct((size, width), BF16) for size in sizes],
        compiler_params=params(),
        cost_estimate=estimate(flops=0, bytes_accessed=0, transcendentals=0),
        name="row_grads",
    )(keys, values, weights)


def unpacked(early, late, size, piece):
    half = size // 2

    def kernel(e_ref, lk_ref, lg_ref, in_ref, out_ref, kv_ref, co_ref, cq_ref, so_ref):
        first = e_ref[...].astype(F32)
        in_ref[...] = jnp.concatenate([first[:size], first[size : 2 * size]], axis=1)
        turned = first[2 * size : 4 * size].T
        out_ref[...] = jnp.concatenate([turned[:piece], turned[piece:]], axis=1)
        co_ref[:half, :] = first[4 * size :, :piece]
        co_ref[half:, :] = first[4 * size :, piece:]
        second = lk_ref[...].astype(F32) + lg_ref[...].astype(F32)
        kv_ref[0] = second[:size, :piece]
        kv_ref[1] = second[:size, piece:]
        cq_ref[...] = second[size:, :piece]
        so_ref[...] = second[size:, piece:]

    flat = lambda *shape: jax.ShapeDtypeStruct(shape, F32)
    outs = pl.pallas_call(
        kernel,
        out_shape=[
            flat(size, 4 * piece),
            flat(piece, 4 * size),
            flat(2, size, piece),
            flat(size, piece),
            flat(size, piece),
            flat(size, piece),
        ],
        compiler_params=params(),
        cost_estimate=estimate(flops=0, bytes_accessed=0, transcendentals=0),
        name="unpacked",
    )(early, *late)
    return (outs[0], outs[1].T) + tuple(outs[2:])


def halved(array, axis, dim):
    while array.shape[dim] > 1:
        kept, sent, pairs = parted(array, axis, dim)
        array = added(kept, lax.ppermute(sent, axis, pairs))
    return jnp.squeeze(array, dim)


def total_of(array, axis):
    size = lax.axis_size(axis)
    copies = jnp.broadcast_to(array[None], (size,) + array.shape)
    return jnp.sum(lax.all_to_all(copies, axis, 0, 0), axis=0)


def estimate(flops, bytes_accessed, transcendentals):
    scale = 10**9
    return pl.CostEstimate(
        flops=max(flops // scale, 1),
        bytes_accessed=max(bytes_accessed // scale, 1),
        transcendentals=transcendentals // scale,
    )


def params():
    return pltpu.CompilerParams(vmem_limit_bytes=VMEM_LIMIT)


def cross_forward(query, pairs, bias, width, groups):
    heads = width // HEAD_DIM
    length = query.shape[1]
    tokens = length // groups
    parts = len(pairs)
    rows = [p.shape[2] for p in pairs]
    starts = [sum(rows[:i]) for i in range(parts)]
    total = sum(rows)
    stat_rows = 16 * ((heads + 15) // 16)

    def kernel(*refs):
        q_ref = refs[0]
        k_refs = refs[1 : 1 + parts]
        v_refs = refs[1 + parts : 1 + 2 * parts]
        b_refs = refs[1 + 2 * parts : 1 + 3 * parts]
        o_ref, p_ref, m_ref, lse_ref = refs[1 + 3 * parts :]
        head = pl.program_id(0)

        @pl.when(head == 0)
        def clear():
            lse_ref[...] = jnp.zeros_like(lse_ref)

        query = q_ref[...]
        aug_query = jnp.concatenate([query, jnp.ones((16, length), BF16)], axis=0)
        q_norm = jnp.max(jnp.sum(jnp.square(query.astype(F32)), axis=0, keepdims=True))
        k_norm = jnp.float32(0)
        for k_ref in k_refs:
            k_norm = jnp.maximum(
                k_norm, jnp.max(jnp.sum(jnp.square(k_ref[0].astype(F32)), axis=0, keepdims=True))
            )
        small = q_norm * k_norm < safe_score * safe_score

        def score(i):
            return dot(jnp.concatenate([k_refs[i][0], b_refs[i][...]], axis=0), aug_query, 0, 0)

        def finish(probs, top):
            mixed = None
            for i in range(parts):
                aug_value = jnp.concatenate([v_refs[i][0], jnp.ones((16, rows[i]), BF16)], axis=0)
                term = dot(aug_value, probs[i], 1, 0)
                mixed = term if mixed is None else mixed + term
            norm = mixed[HEAD_DIM : HEAD_DIM + 1]
            out = (mixed[:HEAD_DIM] / norm).astype(BF16)
            where = pl.ds(pl.multiple_of(head * HEAD_DIM, HEAD_DIM), HEAD_DIM)
            for g in range(groups):
                o_ref[g, where, :] = out[:, g * tokens : (g + 1) * tokens]
            lse_ref[pl.ds(head, 1), :] = top + jnp.log(norm)
            m_ref[0] = top

        @pl.when(small)
        def plain():
            probs = []
            for i in range(parts):
                prob = jnp.exp(score(i)).astype(BF16)
                p_ref[0, starts[i] : starts[i] + rows[i], :] = prob
                probs.append(prob)
            finish(probs, jnp.zeros((1, length), F32))

        @pl.when(jnp.logical_not(small))
        def shifted():
            raw = [score(i) for i in range(parts)]
            top = jnp.max(raw[0], axis=0, keepdims=True)
            for i in range(1, parts):
                top = jnp.maximum(top, jnp.max(raw[i], axis=0, keepdims=True))
            probs = []
            for i in range(parts):
                prob = jnp.exp(raw[i] - top).astype(BF16)
                p_ref[0, starts[i] : starts[i] + rows[i], :] = prob
                probs.append(prob)
            finish(probs, top)

        @pl.when(head == heads - 1)
        def stats():
            high, low = split_low(lse_ref[...])
            for g in range(groups):
                o_ref[g, width : width + stat_rows, :] = high[:, g * tokens : (g + 1) * tokens]
                o_ref[g, width + stat_rows :, :] = low[:, g * tokens : (g + 1) * tokens]

    payload = width + 2 * stat_rows
    key_specs = [pl.BlockSpec((1, HEAD_DIM, r), lambda h: (0, h, 0)) for r in rows]
    value_specs = [pl.BlockSpec((1, HEAD_DIM, r), lambda h: (1, h, 0)) for r in rows]
    return pl.pallas_call(
        kernel,
        grid=(heads,),
        in_specs=[pl.BlockSpec((HEAD_DIM, length), lambda h: (h, 0))]
        + key_specs
        + value_specs
        + [pl.BlockSpec((16, r), lambda h: (0, 0)) for r in rows],
        out_specs=[
            pl.BlockSpec((groups, payload, tokens), lambda h: (0, 0, 0)),
            pl.BlockSpec((1, total, length), lambda h: (h, 0, 0)),
            pl.BlockSpec((1, 1, length), lambda h: (h, 0, 0)),
        ],
        out_shape=[
            jax.ShapeDtypeStruct((groups, payload, tokens), BF16),
            jax.ShapeDtypeStruct((heads, total, length), BF16),
            jax.ShapeDtypeStruct((heads, 1, length), F32),
        ],
        scratch_shapes=[pltpu.VMEM((stat_rows, length), F32)],
        compiler_params=params(),
        cost_estimate=estimate(
            flops=16 * heads * total * length * HEAD_DIM,
            bytes_accessed=2 * heads * total * length,
            transcendentals=heads * total * length,
        ),
        name="cross_forward",
    )(query, *pairs, *pairs, *bias)


def cross_backward(query, pairs, prob, place, grads, tops, earlier, width, groups):
    heads = width // HEAD_DIM
    length = query.shape[1]
    tokens = length // groups
    parts = len(pairs)
    rows = [p.shape[2] for p in pairs]
    starts = [sum(rows[:i]) for i in range(parts)]
    total = sum(rows)
    pair = 2
    stat_rows = grads.shape[1] - width
    each = stat_rows // 4

    def kernel(*refs):
        q_ref = refs[0]
        k_refs = refs[1 : 1 + parts]
        v_refs = refs[1 + parts : 1 + 2 * parts]
        p_ref, g_ref, s_ref, t_ref = refs[1 + 2 * parts : 5 + 2 * parts]
        dq_ref, dk_ref, dv_ref = refs[-3:]
        step = pl.program_id(0)
        stats = jnp.concatenate([s_ref[g] for g in range(groups)], axis=1).astype(F32)
        lse = stats[:each] + stats[each : 2 * each]
        delta = stats[2 * each : 3 * each] + stats[3 * each :]
        row = lax.broadcasted_iota(jnp.int32, (each, length), 0)
        key_out = [[] for _ in range(parts)]
        value_out = [[] for _ in range(parts)]
        for j in range(pair):
            at = slice(j * HEAD_DIM, (j + 1) * HEAD_DIM)
            grad = jnp.concatenate([g_ref[g, at, :] for g in range(groups)], axis=1).astype(F32)
            pick = lambda x: jnp.sum(
                jnp.where(row == step * pair + j, x, 0.0), axis=0, keepdims=True
            )
            scale = jnp.exp(t_ref[j] - pick(lse))
            scaled = grad * scale
            high, low = split_low(-pick(delta) * scale)
            scaled_low = scaled.astype(BF16)
            pad = jnp.zeros((14, length), BF16)
            aug = jnp.concatenate([scaled_low, high, low, pad], axis=0)
            scaled_rows = scaled.T.astype(BF16)
            query_rows = q_ref[at, :].astype(F32).T.astype(BF16)
            query_grad = None
            for i in range(parts):
                aug_value = jnp.concatenate(
                    [v_refs[i][0, at, :], jnp.ones((16, rows[i]), BF16)], axis=0
                )
                prob = p_ref[j, starts[i] : starts[i] + rows[i], :]
                score = (prob.astype(F32) * dot(aug_value, aug, 0, 0)).astype(BF16)
                value_out[i].append(dot(prob, scaled_rows, 1, 0).astype(BF16))
                key_out[i].append(dot(score, query_rows, 1, 0).astype(BF16))
                term = dot(k_refs[i][0, at, :], score, 1, 0)
                query_grad = term if query_grad is None else query_grad + term
            query_grad = query_grad * 0.125
            if earlier is not None:
                before = refs[5 + 2 * parts]
                query_grad += jnp.concatenate(
                    [before[g, at, :] for g in range(groups)], axis=1
                ).astype(F32)
            query_low = query_grad.astype(BF16)
            for g in range(groups):
                dq_ref[g, at, :] = query_low[:, g * tokens : (g + 1) * tokens]
        for i in range(parts):
            at = slice(starts[i], starts[i] + rows[i])
            dk_ref[at, :] = jnp.concatenate(key_out[i], axis=1)
            dv_ref[at, :] = jnp.concatenate(value_out[i], axis=1)

    size = pair * HEAD_DIM
    key_specs = [pl.BlockSpec((1, size, r), lambda h: (0, h, 0)) for r in rows]
    value_specs = [pl.BlockSpec((1, size, r), lambda h: (1, h, 0)) for r in rows]
    token_spec = pl.BlockSpec((groups, size, tokens), lambda h: (0, h, 0))
    row_spec = pl.BlockSpec((total, size), lambda h: (0, h))
    more = [] if earlier is None else [earlier]
    return pl.pallas_call(
        kernel,
        grid=(heads // pair,),
        in_specs=[pl.BlockSpec((size, length), lambda h: (h, 0))]
        + key_specs
        + value_specs
        + [
            pl.BlockSpec((pair, total, length), lambda h: (h, place, 0)),
            token_spec,
            pl.BlockSpec((groups, stat_rows, tokens), lambda h: (0, width // stat_rows, 0)),
            pl.BlockSpec((pair, 1, length), lambda h: (h, 0, 0)),
        ]
        + [token_spec for _ in more],
        out_specs=[token_spec, row_spec, row_spec],
        out_shape=[jax.ShapeDtypeStruct((groups, width, tokens), BF16)]
        + [jax.ShapeDtypeStruct((total, width), BF16)] * 2,
        compiler_params=params(),
        cost_estimate=estimate(
            flops=32 * heads * total * length * HEAD_DIM,
            bytes_accessed=2 * heads * total * length,
            transcendentals=0,
        ),
        name="cross_backward",
    )(query, *pairs, *pairs, prob, grads, grads, tops, *more)


def self_forward(inputs, gain, weights, key_pos, query_pos, groups):
    length, width = inputs.shape
    own = weights.shape[1]
    heads = own // HEAD_DIM

    def kernel(x_ref, g_ref, w_ref, kp_ref, qp_ref, a_ref, pr_ref, o_ref, p_ref, n_ref):
        head = pl.program_id(0)

        @pl.when(head == 0)
        def project():
            low = normed(x_ref[...].astype(F32), g_ref[...]).astype(BF16)
            a_ref[...] = low
            for c in range(3):
                pr_ref[c] = dot(w_ref[c], low, 1, 1).astype(BF16)

        at = pl.ds(pl.multiple_of(head * HEAD_DIM, HEAD_DIM), HEAD_DIM)
        raw = dot(pr_ref[1, at, :], pr_ref[0, at, :], 0, 0) * 0.125
        raw = jnp.where(kp_ref[...] <= qp_ref[...], raw, negative_fill)
        top = jnp.max(raw, axis=0, keepdims=True)
        prob = jnp.exp(raw - top).astype(BF16)
        p_ref[0] = prob
        aug_value = jnp.concatenate([pr_ref[2, at, :], jnp.ones((16, length), BF16)], axis=0)
        mixed = dot(aug_value, prob, 1, 0)
        inverse = 1.0 / mixed[HEAD_DIM : HEAD_DIM + 1]
        out = (mixed[:HEAD_DIM] * inverse).astype(BF16)
        for g in range(groups):
            o_ref[g] = out
        n_ref[0] = inverse

    whole = lambda *shape: pl.BlockSpec(shape, lambda h: (0,) * len(shape))
    return pl.pallas_call(
        kernel,
        grid=(heads,),
        in_specs=[
            whole(length, width),
            whole(1, width),
            whole(3, own, width),
            whole(length, 1),
            whole(1, length),
        ],
        out_specs=[
            whole(length, width),
            whole(3, own, length),
            pl.BlockSpec((groups, HEAD_DIM, length), lambda h: (0, h, 0)),
            pl.BlockSpec((1, length, length), lambda h: (h, 0, 0)),
            pl.BlockSpec((1, 1, length), lambda h: (h, 0, 0)),
        ],
        out_shape=[
            jax.ShapeDtypeStruct((length, width), BF16),
            jax.ShapeDtypeStruct((3, own, length), BF16),
            jax.ShapeDtypeStruct((groups, own, length), BF16),
            jax.ShapeDtypeStruct((heads, length, length), BF16),
            jax.ShapeDtypeStruct((heads, 1, length), F32),
        ],
        compiler_params=params(),
        cost_estimate=estimate(
            flops=16 * heads * length * length * HEAD_DIM,
            bytes_accessed=2 * heads * length * length,
            transcendentals=heads * length * length,
        ),
        name="self_forward",
    )(inputs, gain, weights, key_pos, query_pos)


def project_rows(pieces, weights):
    counts = [p.shape[0] for p in pieces]
    total, width = sum(counts), pieces[0].shape[1]

    def kernel(*refs):
        w_ref, out_ref = refs[len(counts) :]
        start = 0
        for e_ref, count in zip(refs, counts):
            out_ref[0, :, start : start + count] = dot(w_ref[0], e_ref[...], 1, 1).astype(BF16)
            start += count

    return pl.pallas_call(
        kernel,
        grid=(2,),
        in_specs=[pl.BlockSpec((count, width), lambda c: (0, 0)) for count in counts]
        + [pl.BlockSpec((1, width, width), lambda c: (c, 0, 0))],
        out_specs=pl.BlockSpec((1, width, total), lambda c: (c, 0, 0)),
        out_shape=jax.ShapeDtypeStruct((2, width, total), BF16),
        compiler_params=params(),
        cost_estimate=estimate(
            flops=4 * total * width * width, bytes_accessed=8 * total * width, transcendentals=0
        ),
        name="project_rows",
    )(*pieces, weights)


def query_stage(inputs, mixed, out_weight, gain, query_weight, slot, groups):
    length, width = inputs.shape
    tokens = length // groups
    rows = mixed.shape[0]
    wide = 2 if groups % 2 == 0 else 1
    chunk = wide * tokens

    def kernel(s_ref, x_ref, o_ref, w_ref, g_ref, q_ref, qc_ref, h_ref, a_ref):
        after = x_ref[...].astype(F32) + dot(o_ref[...], w_ref[...], 0, 0)
        low = normed(after, g_ref[...]).astype(BF16)
        scaled = dot(q_ref[...], low, 1, 1).astype(BF16)
        qc_ref[...] = (scaled.astype(F32) * 0.125).astype(BF16)

        for part in range(wide):

            @pl.when(pl.program_id(0) * wide + part == s_ref[0])
            def keep():
                h_ref[...] = after[part * tokens : (part + 1) * tokens]
                a_ref[...] = low[part * tokens : (part + 1) * tokens]

    whole = lambda *shape: pl.BlockSpec(shape, lambda i, s: (0,) * len(shape))
    return pl.pallas_call(
        kernel,
        grid_spec=pltpu.PrefetchScalarGridSpec(
            num_scalar_prefetch=1,
            grid=(groups // wide,),
            in_specs=[
                pl.BlockSpec((chunk, width), lambda i, s: (i, 0)),
                pl.BlockSpec((rows, chunk), lambda i, s: (0, i)),
                whole(rows, width),
                whole(1, width),
                whole(width, width),
            ],
            out_specs=[
                pl.BlockSpec((width, chunk), lambda i, s: (0, i)),
                whole(tokens, width),
                whole(tokens, width),
            ],
        ),
        out_shape=[
            jax.ShapeDtypeStruct((width, length), BF16),
            jax.ShapeDtypeStruct((tokens, width), F32),
            jax.ShapeDtypeStruct((tokens, width), BF16),
        ],
        compiler_params=params(),
        cost_estimate=estimate(
            flops=8 * length * width * width, bytes_accessed=8 * width * width, transcendentals=0
        ),
        name="query_stage",
    )(slot, inputs, mixed, out_weight, gain, query_weight)


def gelu_parts(value):
    root = 0.7978845608028654
    cubic = 0.044715
    square = value * value
    bent = jnp.tanh(root * value * (1.0 + cubic * square))
    half = 0.5 * (1.0 + bent)
    slope = half + 0.5 * value * (1.0 - bent * bent) * root * (1.0 + 3.0 * cubic * square)
    return value * half, slope


def pulled_norm(values, gain, grad):
    inverse = lax.rsqrt(jnp.mean(values * values, axis=-1, keepdims=True) + epsilon)
    scaled = values * inverse
    gain_grad = jnp.sum(grad * scaled, axis=0, keepdims=True)
    weighted = grad * gain
    back = inverse * (weighted - scaled * jnp.mean(weighted * scaled, axis=-1, keepdims=True))
    return back, gain_grad


def token_stage(parts, after_self, cross_out, gain, ffn_in, ffn_out, cotangent, groups):
    tokens, width = after_self.shape
    heads = width // HEAD_DIM
    stat_rows = (parts.shape[1] - width) // 2
    hidden = ffn_in.shape[1]
    piece = 1536
    steps = hidden // piece
    payload = width + 4 * stat_rows

    def kernel(
        r_ref, h_ref, co_ref, g_ref, w1_ref, w2_ref, c_ref,
        out_ref, dh_ref, g2_ref, a_ref, z_ref, du_ref, o_ref, pay_ref, gain_ref,
        after_ref, acc_ref, back_ref, lse_ref,
    ):
        step = pl.program_id(0)

        @pl.when(step == 0)
        def join():
            lse = [
                r_ref[g, width : width + stat_rows, :].astype(F32)
                + r_ref[g, width + stat_rows :, :].astype(F32)
                for g in range(groups)
            ]
            top = functools.reduce(jnp.maximum, lse)
            share = [jnp.exp(l - top) for l in lse]
            total = functools.reduce(jnp.add, share)
            lse_ref[...] = top + jnp.log(total)
            share = [s / total for s in share]
            for h in range(heads):
                at = slice(h * HEAD_DIM, (h + 1) * HEAD_DIM)
                mixed = None
                for g in range(groups):
                    term = r_ref[g, at, :].astype(F32) * share[g][h : h + 1]
                    mixed = term if mixed is None else mixed + term
                o_ref[at, :] = mixed.astype(BF16)
            after = h_ref[...] + dot(o_ref[...], co_ref[...], 0, 0)
            after_ref[...] = after
            a_ref[...] = normed(after, g_ref[...]).astype(BF16)
            acc_ref[...] = jnp.zeros_like(acc_ref)
            back_ref[...] = jnp.zeros_like(back_ref)

        pre = dot(a_ref[...], w1_ref[...], 1, 0)
        act, slope = gelu_parts(pre)
        act = act.astype(BF16)
        z_ref[...] = act
        acc_ref[...] += dot(act, w2_ref[...], 1, 0)
        pre_grad = (dot(c_ref[...], w2_ref[...], 1, 1) * slope).astype(BF16)
        du_ref[...] = pre_grad
        back_ref[...] += dot(pre_grad, w1_ref[...], 1, 1)

        @pl.when(step == steps - 1)
        def finish():
            after = after_ref[...]
            out_ref[...] = (after + acc_ref[...]).astype(BF16)
            back, gain_grad = pulled_norm(after, g_ref[...], back_ref[...])
            gain_ref[...] = gain_grad
            grad = c_ref[...].astype(F32) + back
            dh_ref[...] = grad
            low = grad.astype(BF16)
            g2_ref[...] = low
            mix_grad = dot(co_ref[...], low, 1, 1).astype(BF16)
            both = mix_grad.astype(F32) * o_ref[...].astype(F32)
            rows = [
                jnp.sum(both[h * HEAD_DIM : (h + 1) * HEAD_DIM], axis=0, keepdims=True)
                for h in range(heads)
            ]
            rows.append(jnp.zeros((stat_rows - heads, tokens), F32))
            stats = [*split_low(lse_ref[...]), *split_low(jnp.concatenate(rows, axis=0))]
            for g in range(groups):
                pay_ref[g, :width, :] = mix_grad
                for i in range(4):
                    start = width + i * stat_rows
                    pay_ref[g, start : start + stat_rows, :] = stats[i]

    whole = lambda *shape: pl.BlockSpec(shape, lambda i: (0,) * len(shape))
    flat = lambda rows, kind: jax.ShapeDtypeStruct((rows, width), kind)
    return pl.pallas_call(
        kernel,
        grid=(steps,),
        in_specs=[
            whole(*parts.shape),
            whole(tokens, width),
            whole(width, width),
            whole(1, width),
            pl.BlockSpec((width, piece), lambda i: (0, i)),
            pl.BlockSpec((piece, width), lambda i: (i, 0)),
            whole(tokens, width),
        ],
        out_specs=[
            whole(tokens, width),
            whole(tokens, width),
            whole(tokens, width),
            whole(tokens, width),
            pl.BlockSpec((tokens, piece), lambda i: (0, i)),
            pl.BlockSpec((tokens, piece), lambda i: (0, i)),
            whole(width, tokens),
            whole(groups, payload, tokens),
            whole(1, width),
        ],
        out_shape=[
            flat(tokens, BF16),
            flat(tokens, F32),
            flat(tokens, BF16),
            flat(tokens, BF16),
            jax.ShapeDtypeStruct((tokens, hidden), BF16),
            jax.ShapeDtypeStruct((tokens, hidden), BF16),
            jax.ShapeDtypeStruct((width, tokens), BF16),
            jax.ShapeDtypeStruct((groups, payload, tokens), BF16),
            flat(1, F32),
        ],
        scratch_shapes=[pltpu.VMEM((tokens, width), F32)] * 3
        + [pltpu.VMEM((stat_rows, tokens), F32)],
        compiler_params=params(),
        cost_estimate=estimate(
            flops=8 * tokens * width * hidden,
            bytes_accessed=4 * width * hidden,
            transcendentals=tokens * hidden,
        ),
        name="token_stage",
    )(parts, after_self, cross_out, gain, ffn_in, ffn_out, cotangent)


def early_weight_grads(low, pre_grad, act, cotangent, mixed, mixed_grad, columns, blocks):
    tokens, width = low.shape
    hidden = act.shape[1]
    step_size = hidden // blocks
    size, piece = width // blocks, width // columns
    half = step_size // 2

    def kernel(a_ref, du_ref, z_ref, c_ref, m_ref, g_ref, out_ref):
        step = pl.program_id(0)
        first = dot(a_ref[...], du_ref[...], 0, 0).astype(BF16)
        for p in range(2):

            @pl.when(lax.rem(step, 2) == p)
            def put():
                for b in range(blocks):
                    out_ref[step // 2, b, p * size : (p + 1) * size, :] = first[
                        b * size : (b + 1) * size
                    ]

        second = dot(z_ref[...], c_ref[...], 0, 0).astype(BF16)
        for d in range(columns):
            at = slice(d * piece, (d + 1) * piece)
            out_ref[d, step, 2 * size : 2 * size + half, :] = jnp.concatenate(
                [second[:half, at], second[half:, at]], axis=1
            )
        third = dot(m_ref[...], g_ref[...], 1, 0).astype(BF16)
        for d in range(columns):
            at = slice(d * piece, (d + 1) * piece)
            out_ref[d, step, 2 * size + half :, :] = jnp.concatenate(
                [third[: size // 2, at], third[size // 2 :, at]], axis=1
            )

    shape = (columns, blocks, 2 * size + half + size // 2, 2 * piece)
    whole = lambda *shape: pl.BlockSpec(shape, lambda i: (0,) * len(shape))
    return pl.pallas_call(
        kernel,
        grid=(blocks,),
        in_specs=[
            whole(tokens, width),
            pl.BlockSpec((tokens, step_size), lambda i: (0, i)),
            pl.BlockSpec((tokens, step_size), lambda i: (0, i)),
            whole(tokens, width),
            pl.BlockSpec((size, tokens), lambda i: (i, 0)),
            whole(tokens, width),
        ],
        out_specs=whole(*shape),
        out_shape=jax.ShapeDtypeStruct(shape, BF16),
        compiler_params=params(),
        cost_estimate=estimate(
            flops=4 * tokens * width * hidden,
            bytes_accessed=4 * width * hidden,
            transcendentals=0,
        ),
        name="early_weight_grads",
    )(low, pre_grad, act, cotangent, mixed, mixed_grad)


def mixed_stage(parts, cross_q, after_self, gain, cross_grad, self_out, groups, own):
    tokens, width = after_self.shape
    rows = self_out.shape[0]

    def kernel(r_ref, q_ref, h_ref, g_ref, dh_ref, w_ref, dq_ref, out_ref, g1_ref, do_ref, gain_ref):
        total = r_ref[0].astype(F32)
        for g in range(1, groups):
            total = total + r_ref[g].astype(F32)
        query_grad = total.astype(BF16)
        dq_ref[...] = query_grad
        back, gain_grad = pulled_norm(h_ref[...], g_ref[...], dot(query_grad, q_ref[...], 0, 1))
        gain_ref[...] = gain_grad
        grad = dh_ref[...] + back
        out_ref[...] = grad
        low = grad.astype(BF16)
        g1_ref[...] = low
        mixed = dot(w_ref[...], low, 1, 1).astype(BF16)
        for g in range(groups):
            do_ref[g] = mixed[g * own : (g + 1) * own]

    return pl.pallas_call(
        kernel,
        out_shape=[
            jax.ShapeDtypeStruct((width, tokens), BF16),
            jax.ShapeDtypeStruct((tokens, width), F32),
            jax.ShapeDtypeStruct((tokens, width), BF16),
            jax.ShapeDtypeStruct((groups, own, tokens), BF16),
            jax.ShapeDtypeStruct((1, width), F32),
        ],
        compiler_params=params(),
        cost_estimate=estimate(
            flops=4 * tokens * width * width, bytes_accessed=8 * width * width, transcendentals=0
        ),
        name="mixed_stage",
    )(parts, cross_q, after_self, gain, cross_grad, self_out)


def input_stage(back, weights, inputs, gain, self_grad, slot, groups):
    own, tokens = back.shape[2:]
    width = inputs.shape[1]
    padded = groups * own

    def kernel(s_ref, b_ref, w_ref, x_ref, g_ref, h_ref, out_ref, acc_ref):
        step = pl.program_id(0)
        grads = jnp.concatenate([b_ref[g, 0] for g in range(groups)], axis=0)
        term = dot(grads, w_ref[0], 0, 1)

        @pl.when(step == 0)
        def first():
            acc_ref[...] = term

        @pl.when(step > 0)
        def more():
            acc_ref[...] += term

        @pl.when(step == 2)
        def last():
            back, unused = pulled_norm(x_ref[...].astype(F32), g_ref[...], acc_ref[...])
            out_ref[...] = (h_ref[...] + back).astype(BF16)

    whole = lambda *shape: pl.BlockSpec(shape, lambda i, s: (0,) * len(shape))
    return pl.pallas_call(
        kernel,
        grid_spec=pltpu.PrefetchScalarGridSpec(
            num_scalar_prefetch=1,
            grid=(3,),
            in_specs=[
                pl.BlockSpec((groups, 1, own, tokens), lambda i, s: (0, i, 0, 0)),
                pl.BlockSpec((1, width, padded), lambda i, s: (i, 0, 0)),
                pl.BlockSpec((tokens, width), lambda i, s: (s[0], 0)),
                whole(1, width),
                whole(tokens, width),
            ],
            out_specs=whole(tokens, width),
            scratch_shapes=[pltpu.VMEM((tokens, width), F32)],
        ),
        out_shape=jax.ShapeDtypeStruct((tokens, width), BF16),
        compiler_params=params(),
        cost_estimate=estimate(
            flops=6 * tokens * width * width, bytes_accessed=6 * width * width, transcendentals=0
        ),
        name="input_stage",
    )(slot, back, weights, inputs, gain, self_grad)


def both_queries(own, pieces, mine):
    rows, width = own.shape

    def kernel(s_ref, own_ref, *refs):
        out_ref = refs[-1]

        @pl.when(pl.program_id(0) == s_ref[0])
        def here():
            out_ref[0] = own_ref[...]

        @pl.when(pl.program_id(0) != s_ref[0])
        def there():
            start = 0
            for ref in refs[:-1]:
                out_ref[0, start : start + ref.shape[0], :] = ref[...]
                start += ref.shape[0]

    whole = lambda *shape: pl.BlockSpec(shape, lambda i, s: (0,) * len(shape))
    return pl.pallas_call(
        kernel,
        grid_spec=pltpu.PrefetchScalarGridSpec(
            num_scalar_prefetch=1,
            grid=(2,),
            in_specs=[whole(*own.shape)] + [whole(*p.shape) for p in pieces],
            out_specs=pl.BlockSpec((1, rows, width), lambda i, s: (i, 0, 0)),
        ),
        out_shape=jax.ShapeDtypeStruct((2, rows, width), own.dtype),
        compiler_params=params(),
        cost_estimate=estimate(flops=0, bytes_accessed=8 * rows * width, transcendentals=0),
        name="both_queries",
    )(mine, own, *pieces)


def own_weight_grads(low, gain, grads, weights, column, columns, blocks):
    length, width = low.shape
    groups, _, own, tokens = grads.shape
    rows = width // blocks
    per = blocks // columns

    def kernel(c_ref, a_ref, g_ref, d_ref, w_ref, *refs):
        gain_ref = refs[-1]
        step = pl.program_id(0)
        grads = jnp.concatenate([d_ref[g, 0] for g in range(groups)], axis=1)
        turned = dot(grads, a_ref[...], 1, 0)
        weight = turned.T.astype(BF16)
        for d in range(columns):

            @pl.when(c_ref[0] == d)
            def put():
                for b in range(blocks):
                    refs[b // per ^ d][b % per, 0] = weight[b * rows : (b + 1) * rows]

        term = jnp.sum(turned * w_ref[0].astype(F32), axis=0, keepdims=True) / g_ref[...]

        @pl.when(step == 0)
        def first():
            gain_ref[...] = term

        @pl.when(step > 0)
        def more():
            gain_ref[...] += term

    shape = (per, 3, rows, own)
    whole = lambda *shape: pl.BlockSpec(shape, lambda i, c: (0,) * len(shape))
    part = pl.BlockSpec((per, 1, rows, own), lambda i, c: (0, i, 0, 0))
    return pl.pallas_call(
        kernel,
        grid_spec=pltpu.PrefetchScalarGridSpec(
            num_scalar_prefetch=1,
            grid=(3,),
            in_specs=[
                whole(length, width),
                whole(1, width),
                pl.BlockSpec((groups, 1, own, tokens), lambda i, c: (0, i, 0, 0)),
                pl.BlockSpec((1, own, width), lambda i, c: (i, 0, 0)),
            ],
            out_specs=[part] * columns + [whole(1, width)],
        ),
        out_shape=[jax.ShapeDtypeStruct(shape, BF16)] * columns
        + [jax.ShapeDtypeStruct((1, width), F32)],
        compiler_params=params(),
        cost_estimate=estimate(
            flops=12 * length * width * own, bytes_accessed=4 * length * width, transcendentals=0
        ),
        name="own_weight_grads",
    )(column, low, gain, grads, weights)


def sums_for(pairs, groups):
    blocks, _, width = pairs[0][0].shape
    rows = [k.shape[1] for k, _ in pairs]
    high = blocks // groups

    def kernel(*refs):
        out_ref = refs[-1]
        start = 0
        for i, size in enumerate(rows):
            both = refs[2 * i][...].astype(F32) + refs[2 * i + 1][...].astype(F32)
            both = both.astype(BF16)
            for b in range(blocks):
                out_ref[b % groups, b // groups, start : start + size, :] = both[b]
            start += size

    return pl.pallas_call(
        kernel,
        out_shape=jax.ShapeDtypeStruct((groups, high, sum(rows), width), BF16),
        compiler_params=params(),
        cost_estimate=estimate(flops=0, bytes_accessed=0, transcendentals=0),
        name="sums_for",
    )(*[array for pair in pairs for array in pair])


def sums_of(lists, bit):
    arrays = [array for one in lists for array in one]

    def kernel(s_ref, *refs):
        start = 0
        for i, one in enumerate(lists):
            for side in range(2):
                terms = [refs[2 * (start + n) + side][0].astype(F32) for n in range(len(one))]
                total = functools.reduce(jnp.add, terms)
                refs[2 * (len(arrays) + i) + side][...] = total.astype(BF16)
            start += len(one)

    def spec(array, side):
        return pl.BlockSpec((1,) + array.shape[1:], lambda j, s: ((s[0] + side) % 2, 0, 0))

    outs = pl.pallas_call(
        kernel,
        grid_spec=pltpu.PrefetchScalarGridSpec(
            num_scalar_prefetch=1,
            grid=(1,),
            in_specs=[spec(array, side) for array in arrays for side in range(2)],
            out_specs=[
                pl.BlockSpec(one[0].shape[1:], lambda j, s: (0, 0)) for one in lists for _ in range(2)
            ],
        ),
        out_shape=[
            jax.ShapeDtypeStruct(one[0].shape[1:], BF16) for one in lists for _ in range(2)
        ],
        compiler_params=params(),
        cost_estimate=estimate(flops=0, bytes_accessed=0, transcendentals=0),
        name="sums_of",
    )(bit, *[array for array in arrays for _ in range(2)])
    return list(zip(outs[::2], outs[1::2]))


def self_backward(projected, mixed, grads, prob, weight, groups):
    own, length = projected.shape[1:]
    heads = own // HEAD_DIM
    tokens = length // groups

    def kernel(q_ref, k_ref, v_ref, o_ref, g_ref, p_ref, w_ref, out_ref):
        grad = jnp.concatenate([g_ref[g] for g in range(groups)], axis=1).astype(F32)
        scaled = grad * w_ref[0]
        high, low = split_low(-jnp.sum(scaled * o_ref[0].astype(F32), axis=0, keepdims=True))
        scaled_low = scaled.astype(BF16)
        aug = jnp.concatenate([scaled_low, high, low, jnp.zeros((14, length), BF16)], axis=0)
        aug_value = jnp.concatenate([v_ref[0], jnp.ones((16, length), BF16)], axis=0)
        prob = p_ref[0]
        score = (prob.astype(F32) * dot(aug_value, aug, 0, 0)).astype(BF16)
        results = (
            dot(k_ref[0], score, 1, 0) * 0.125,
            dot(q_ref[0], score, 1, 1) * 0.125,
            dot(scaled_low, prob, 1, 1),
        )
        for c in range(3):
            result = results[c].astype(BF16)
            for g in range(groups):
                out_ref[g, c] = result[:, g * tokens : (g + 1) * tokens]

    spec = lambda c: pl.BlockSpec((1, HEAD_DIM, length), lambda h: (c, h, 0))
    return pl.pallas_call(
        kernel,
        grid=(heads,),
        in_specs=[
            spec(0),
            spec(1),
            spec(2),
            pl.BlockSpec((1, HEAD_DIM, length), lambda h: (0, h, 0)),
            pl.BlockSpec((groups, HEAD_DIM, tokens), lambda h: (0, h, 0)),
            pl.BlockSpec((1, length, length), lambda h: (h, 0, 0)),
            pl.BlockSpec((1, 1, length), lambda h: (h, 0, 0)),
        ],
        out_specs=pl.BlockSpec((groups, 3, HEAD_DIM, tokens), lambda h: (0, 0, h, 0)),
        out_shape=jax.ShapeDtypeStruct((groups, 3, own, tokens), BF16),
        compiler_params=params(),
        cost_estimate=estimate(
            flops=32 * heads * length * length * HEAD_DIM,
            bytes_accessed=2 * heads * length * length,
            transcendentals=0,
        ),
        name="self_backward",
    )(projected, projected, projected, mixed, grads, prob, weight)


def body(
    dec_input,
    enc_output,
    lengths,
    gains,
    self_qkv,
    self_out,
    cross_q,
    cross_kv,
    cross_out,
    ffn_in,
    ffn_out,
    cotangent,
):
    seg, seqs, width = dec_input.shape
    heads = width // HEAD_DIM
    blocks = lax.axis_size("blk")
    place = lax.axis_index("blk")
    groups = blocks // seqs
    mine = place // groups
    slot_of = lax.rem(place, groups)
    members = [[s * groups + g for g in range(groups)] for s in range(seqs)]
    own_heads = -(-heads // groups)
    own = own_heads * HEAD_DIM
    padded = own * groups
    tokens = seqs * seg
    length = groups * tokens
    enc_rows = enc_output.shape[1]
    columns = lax.axis_size("dp")
    gain_rows = gains.astype(F32)[:, None, :]

    def shifted(step):
        return [(b, (b + step * groups) % blocks) for b in range(blocks)]

    def exchange(pieces):
        parts = [pieces(mine)]
        for step in range(1, seqs):
            parts.append(lax.ppermute(pieces(lax.rem(mine + step, seqs)), "blk", shifted(step)))
        return parts

    def in_order(parts):
        ordered = []
        for s in range(seqs):
            choice = parts[0]
            for step in range(1, seqs):
                from_there = lax.rem(mine - step + seqs, seqs) == s
                choice = jnp.where(from_there, parts[step], choice)
            ordered.append(choice)
        return ordered

    def spread(array):
        return lax.all_to_all(
            jnp.broadcast_to(array[None], (groups,) + array.shape),
            "blk",
            0,
            0,
            axis_index_groups=members,
        )

    def traded(array):
        return lax.all_to_all(array, "blk", 0, 0, axis_index_groups=members)

    def gathered(array):
        by_query = lax.optimization_barrier(array.swapaxes(0, 1))
        take = lambda s: lax.dynamic_index_in_dim(by_query, s, 0, False)
        return jnp.concatenate(in_order(exchange(take)), axis=0)

    def leaving(array):
        split = array.reshape(seqs, seg, width)
        return exchange(lambda s: lax.dynamic_index_in_dim(split, s, 0, False))

    def returned(parts):
        return jnp.stack(in_order(parts), axis=1)

    own_inputs = gathered(dec_input)
    all_inputs = spread(own_inputs).reshape(length, width)

    pick = lambda s: lax.dynamic_index_in_dim(enc_output, s, 0, False)
    cuts = [max(enc_rows * 3 // 7 // 128 * 128, 128)]
    cuts.append(cuts[0] + 128)
    spans = [(0, 0, enc_rows)]
    arrived = []
    for step in range(1, seqs):
        sent = pick(lax.rem(mine + step, seqs))
        arrived.append([lax.ppermute(sent[: cuts[0]], "blk", shifted(step))])
        spans += [(step, 0, cuts[0]), (step, cuts[0], enc_rows)]
        for start, stop in ((cuts[0], cuts[1]), (cuts[1], enc_rows)):
            piece, unused = lax.optimization_barrier((sent[start:stop], arrived[-1][-1]))
            arrived[-1].append(lax.ppermute(piece, "blk", shifted(step)))
    own_rows_low = pick(mine)
    turned_kv = cross_kv.swapaxes(1, 2)
    first_pair = project_rows([own_rows_low], turned_kv)
    all_inputs, first_pair, firsts = lax.optimization_barrier(
        (all_inputs, first_pair, [a[0] for a in arrived])
    )

    row_lengths = lax.dynamic_index_in_dim(lengths, mine, 0, False)
    bias = []
    for step, start, stop in spans:
        source = lax.rem(place - step * groups + blocks, blocks)
        slot = source * enc_rows + jnp.arange(start, stop)
        match = (slot // SLOTS)[:, None] == jnp.arange(lengths.shape[1])[None, :]
        filled = jnp.sum(jnp.where(match, row_lengths[None, :], 0), axis=-1)
        row = jnp.where((slot % SLOTS) < filled, 0.0, negative_fill).astype(BF16)
        bias.append(jnp.concatenate([row[None], jnp.zeros((15, stop - start), BF16)], axis=0))

    extra = [(0, 0), (0, 0), (0, padded - width)]
    padded_qkv = jnp.pad(self_qkv, extra)
    own_qkv = lax.dynamic_slice_in_dim(padded_qkv, slot_of * own, own, 2).swapaxes(1, 2)
    padded_out = jnp.pad(self_out, [(0, padded - width), (0, 0)])
    index = jnp.arange(length)
    block = index // seg
    position = ((block % seqs) * groups + block // seqs) * seg + index % seg
    position = position.astype(jnp.int32)
    first_low, projected, sent_mix, self_prob, self_weight = self_forward(
        all_inputs,
        gain_rows[0],
        own_qkv,
        position[:, None],
        position[None, :],
        groups,
    )
    sent_mix, seconds = lax.optimization_barrier((sent_mix, [a[1] for a in arrived]))
    self_mix = traded(sent_mix).reshape(padded, length)
    slot = jnp.full((1,), slot_of, jnp.int32)
    cross_query, after_self, second_low = query_stage(
        all_inputs, self_mix, padded_out, gain_rows[1], cross_q.T, slot, groups
    )

    cross_query, thirds = lax.optimization_barrier((cross_query, [a[2] for a in arrived]))
    pairs = [first_pair]
    came = []
    for first, second, third in zip(firsts, seconds, thirds):
        pairs.append(project_rows([first], turned_kv))
        pairs.append(project_rows([second, third], turned_kv))
        came += [first, second, third]

    part_mix, cross_prob, local_top = cross_forward(cross_query, pairs, bias, width, groups)

    own_cotangent = gathered(cotangent)
    (
        own_output,
        cross_grad,
        cross_grad_low,
        third_low,
        hidden_low,
        pre_low,
        cross_mix,
        payload,
        gain_three,
    ) = token_stage(
        traded(part_mix),
        after_self,
        cross_out,
        gain_rows[2],
        ffn_in,
        ffn_out,
        own_cotangent,
        groups,
    )
    packed = traded(payload)

    def by_rows(grad):
        return grad.astype(BF16).reshape(blocks, columns, -1, grad.shape[-1]).swapaxes(0, 1)

    def placed(rows, counts):
        count, full = rows.shape
        split = rows.reshape(count, columns, full // columns).swapaxes(0, 1)
        moved = lax.all_to_all(split, "dp", 0, 0).astype(F32)
        ends = [sum(counts[: i + 1]) for i in range(len(counts) - 1)]
        return [p.reshape(-1, full // columns) for p in jnp.split(moved, ends, axis=1)]

    unit = width // blocks // columns
    staged = (
        padded == width
        and columns * own == width
        and columns * seqs == blocks
        and columns % 2 == 0
        and ffn_in.shape[1] == columns * width
        and ffn_in.shape[1] // blocks * columns == 2 * width
        and blocks == 8
    )
    if staged:
        chunks = early_weight_grads(
            third_low,
            pre_low,
            hidden_low,
            own_cotangent,
            cross_mix,
            cross_grad_low,
            columns,
            blocks,
        )
        packed, chunks, own_output = lax.optimization_barrier((packed, chunks, own_output))
        inner = chunks.shape[2:]
        hidden = lax.psum_scatter(
            chunks.reshape(-1, inner[1]), "dp", scatter_dimension=0, tiled=True
        )
    else:
        in_chunks = dot(third_low, pre_low, 0, 0).astype(BF16)
        in_chunks = in_chunks.reshape(blocks, width // blocks, columns, -1).transpose(2, 0, 1, 3)
        out_chunks = by_rows(dot(hidden_low, own_cotangent, 0, 0))
    together = lambda *values: lax.optimization_barrier(values)

    output_parts = leaving(own_output)

    def rows_backward(place, subset, earlier):
        return cross_backward(
            cross_query, subset, cross_prob, place, packed, local_top, earlier, width, groups
        )

    shares = [0, 12, 19, 23, 28]
    marks = [enc_rows * share // 28 for share in shares]
    part_grads, came_key, came_value = rows_backward(1, pairs[1:], None)
    pieces = row_grads(came_key, came_value, cross_kv, marks)

    def sent_back(piece):
        return lax.ppermute(piece, "blk", shifted(1))

    part_grads, pieces, output_parts = together(part_grads, pieces, output_parts)
    back_1 = sent_back(pieces[0])
    query_parts, own_key, own_value = rows_backward(0, pairs[:1], part_grads)
    key_low, value_low = [own_key, came_key], [own_value, came_value]
    query_parts, key_low, value_low, back_1, pieces = together(
        query_parts, key_low, value_low, back_1, pieces
    )
    joined = traded(query_parts)
    here = jnp.full((1,), mine, jnp.int32)

    def moved(array, axis, step):
        size = lax.axis_size(axis)
        return lax.ppermute(array, axis, [(i, i ^ step) for i in range(size)])

    def bit_of(axis, step):
        return jnp.full((1,), lax.rem(lax.axis_index(axis) // step, 2), jnp.int32)

    def chunks_of(kernel_dots, operands, specs):
        return weight_chunks(
            kernel_dots, operands, specs, bit_of("dp", 1), slot, columns, blocks, width
        )

    back_2 = sent_back(pieces[1])
    output = returned(output_parts)
    if staged:
        cuts = [0]
        for piece in came:
            cuts.append(cuts[-1] + piece.shape[0])

        def rows_dot(grad):
            def one(refs):
                total = dot(refs[0][...], refs[grad][...], 0, 0)
                for i, (start, stop) in enumerate(zip(cuts, cuts[1:])):
                    total += dot(refs[1 + i][...], refs[grad + 1][start:stop, :], 0, 0)
                return total

            return one

        count = 1 + len(came)
        operands = [own_rows_low, *came, *key_low, *value_low]
        kept_1, sent_1 = chunks_of(
            [
                rows_dot(count),
                rows_dot(count + 2),
            ],
            operands,
            [None] * len(operands),
        )
        joined, pieces, back_2, output, hidden, kept_1, sent_1 = together(
            joined, pieces, back_2, output, hidden, kept_1, sent_1
        )
        hidden = lax.psum_scatter(hidden, "blk", scatter_dimension=0, tiled=True)
        got_1 = moved(sent_1, "dp", 1)
    query_grad, self_grad, self_grad_low, mixed_grad, gain_two = mixed_stage(
        joined, cross_q, after_self, gain_rows[1], cross_grad, padded_out, groups, own
    )
    if staged:
        query_grad, self_grad, self_grad_low, mixed_grad, gain_two, kept_1, got_1, pieces = (
            together(
                query_grad, self_grad, self_grad_low, mixed_grad, gain_two, kept_1, got_1, pieces
            )
        )
    own_mixed = traded(mixed_grad)
    if staged:
        back_3 = sent_back(pieces[2])
        kept_1, sent_1 = fold([(kept_1, got_1)], bit_of("dp", 2), blocks)
        operands = [second_low, query_grad, self_mix, self_grad_low]
        specs = [None] * 2
        specs += [pl.BlockSpec((width, tokens), lambda i, c, n: (0, n[0])), None]
        kept_2, sent_2 = chunks_of(
            [
                lambda refs: dot(refs[0][...], refs[1][...], 0, 1),
                lambda refs: dot(refs[2][...], refs[3][...], 1, 0),
            ],
            operands,
            specs,
        )
        own_mixed, back_3, kept_1, sent_1, kept_2, sent_2, pieces = together(
            own_mixed, back_3, kept_1, sent_1, kept_2, sent_2, pieces
        )
        got_1 = moved(sent_1, "dp", 2)
        got_2 = moved(sent_2, "dp", 1)
    own_grads = self_backward(projected, sent_mix, own_mixed, self_prob, self_weight, groups)
    if staged:
        own_grads, kept_2, got_2, pieces = together(own_grads, kept_2, got_2, pieces)
    back = traded(own_grads)
    if staged:
        back_4 = sent_back(pieces[3])
        kept_2, sent_2 = fold([(kept_2, got_2)], bit_of("dp", 2), blocks)
        got_2 = moved(sent_2, "dp", 2)
        *parts_w, gain_one = own_weight_grads(
            first_low,
            gain_rows[0],
            own_grads,
            own_qkv,
            jnp.full((1,), lax.axis_index("dp"), jnp.int32),
            columns,
            blocks,
        )
        gains = jnp.concatenate([gain_one, gain_two, gain_three], axis=0)
        gains = gains + moved(gains, "dp", 1)
        gains = gains + moved(gains, "dp", 2)
        back, back_4, kept_1, got_1, kept_2, got_2, parts_w, gains, key_low = together(
            back, back_4, kept_1, got_1, kept_2, got_2, parts_w, gains, key_low
        )
    own_grad = input_stage(back, padded_qkv, all_inputs, gain_rows[0], self_grad, slot, groups)
    if staged:
        own_grad, key_low = together(own_grad, key_low)
    dec_parts = leaving(own_grad)
    if staged:
        late = traded(sums_for([(kept_1, got_1), (kept_2, got_2)], groups))
        parts_w = [parts_w[0]] + [moved(p, "dp", r) for r, p in enumerate(parts_w) if r]
        gains_got = moved(gains, "blk", 1)
        (enc_own,) = row_grads(key_low[0], value_low[0], cross_kv, [0, enc_rows])
        enc_grad = both_queries(enc_own, [back_1, back_2, back_3, back_4], here)
        dec_parts, late, parts_w, gains, gains_got, enc_grad = together(
            dec_parts, late, parts_w, gains, gains_got, enc_grad
        )
        gains = gains + gains_got
    if staged:
        (kept_j, sent_j), halves = sums_of(
            [[late[g] for g in range(groups)], [p.reshape(seqs, -1, own) for p in parts_w]], here
        )
        got_j = moved(sent_j, "blk", groups)
        got_w = []
        for step, piece in enumerate(halves):
            pairs = []
            for b in range(blocks):
                row = (b // groups + step) % seqs
                for d in range(columns):
                    pairs.append((b * columns + d, (d * seqs + row) * columns + b % groups))
            piece = piece.reshape(3, width // blocks, own)
            got_w.append(lax.ppermute(piece, ("blk", "dp"), pairs))
        gains = gains + moved(gains, "blk", 2)
        dec_grad = returned(dec_parts)
        dec_grad, kept_j, got_j, got_w, gains = together(dec_grad, kept_j, got_j, got_w, gains)
        gain_grads = gains + moved(gains, "blk", 4)
        qkv = sum(piece.astype(F32) for piece in got_w)
        ffn_in_own, ffn_out_own, kv_own, cross_out_own, cross_q_own, self_out_own = unpacked(
            hidden, (kept_j, got_j), width // blocks, width // columns
        )
    else:
        rest = sent_back(jnp.concatenate(pieces[2:], axis=0))
        (enc_own,) = row_grads(key_low[0], value_low[0], cross_kv, [0, enc_rows])
        enc_grad = both_queries(enc_own, [back_1, back_2, rest], here)
        own_rows = lambda array: lax.dynamic_slice_in_dim(array, slot_of * tokens, tokens, 0)
        full = back.transpose(1, 0, 2, 3).reshape(3, padded, tokens)[:, :width]
        first_back = sum(dot(full[c], self_qkv[c], 0, 1) for c in range(3))
        unused, gain_one = pulled_norm(
            own_rows(all_inputs).astype(F32), gain_rows[0], first_back
        )
        gains = jnp.concatenate([gain_one, gain_two, gain_three], axis=0)
        gain_grads = total_of(total_of(gains, "dp"), "blk")
        dec_grad = returned(dec_parts)
        reduced = lambda array: halved(halved(array, "dp", 0), "blk", 0)
        own_first = own_rows(first_low)
        own_self_mix = lax.dynamic_slice_in_dim(self_mix, slot_of * tokens, tokens, 1)
        encoded = [own_rows_low, jnp.concatenate(came, axis=0)]
        late = [
            sum(dot(e, g, 0, 0) for e, g in zip(encoded, key_low)),
            sum(dot(e, g, 0, 0) for e, g in zip(encoded, value_low)),
            dot(cross_mix, cross_grad_low, 1, 0),
            dot(second_low, query_grad, 0, 1),
            dot(own_self_mix[:width], self_grad_low, 1, 0),
        ] + [dot(own_first, full[c], 0, 1) for c in range(3)]
        chunks = [out_chunks] + [by_rows(grad) for grad in late]
        counts = [out_chunks.shape[2]] + [unit] * 8
        rows = placed(reduced(jnp.concatenate(chunks, axis=2)), counts)
        ffn_out_own, key_own, value_own, cross_out_own, cross_q_own, self_out_own = rows[:6]
        kv_own = jnp.stack([key_own, value_own])
        qkv = jnp.stack(rows[6:])
        ffn_in_own = reduced(in_chunks).astype(F32)

    return (
        output,
        dec_grad,
        enc_grad,
        gain_grads,
        qkv,
        self_out_own,
        cross_q_own,
        kv_own,
        cross_out_own,
        ffn_in_own,
        ffn_out_own,
    )


def solution(mesh):
    placed = (
        P("blk", "dp", None),
        P("dp", "blk", None),
        P("dp", None),
        P(),
        P(),
        P(),
        P(),
        P(),
        P(),
        P(),
        P(),
        P("blk", "dp", None),
    )
    return jax.shard_map(
        body,
        mesh=mesh,
        in_specs=placed,
        out_specs=(
            P("blk", "dp", None),
            P("blk", "dp", None),
            P("dp", "blk", None),
            P(),
            P(None, "blk", "dp"),
            P("blk", "dp"),
            P("blk", "dp"),
            P(None, "blk", "dp"),
            P("blk", "dp"),
            P("blk", "dp"),
            P("blk", "dp"),
        ),
        check_vma=False,
    )
```
